256 devices in a mesh: section: 2 (over core), head: 8 (over z), seq: 16 (over y, x).
Axes of the slice: x: 4, y: 4, z: 8, core: 2. Of those that a mesh axis runs over, the one named last changes fastest.
Arguments:
- patches: bfloat16 [4, 384, 3072], P(None, 'seq', 'head'), may hold values from -6 to 6
- cache_k: bfloat16 [2, 1536, 3072], P('section', 'seq', 'head'), may hold values from -7 to 7
- cache_v: bfloat16 [2, 1536, 3072], P('section', 'seq', 'head'), may hold values from -4 to 4
- w_qkv: bfloat16 [2, 3072, 3, 3072], P('section', 'seq', None, 'head'), may hold values from -0.109375 to 0.109375
- w_out: bfloat16 [2, 3072, 3072], P('section', None, 'head'), may hold values from -0.109375 to 0.109375
- modulation: float32 [2, 3, 3072], P('section'), may hold values from -4 to 4
- qk_gain: float32 [2, 2, 128], P('section'), may hold values from 1 to 2.2
- patch_order: int32 [4], replicated, may hold values from 0 to 3, each once
- patch_start: int32 [4], replicated, may hold values from 0 to 1152, as said below
Outputs:
- block_out: bfloat16 [2, 4, 384, 3072], P('section', None, 'seq', 'head')
- new_k: bfloat16 [2, 1536, 3072], P('section', 'seq', 'head')
- new_v: bfloat16 [2, 1536, 3072], P('section', 'seq', 'head')
The draws below stay inside these ranges and needn't reach their ends.
Inputs may be any that keep to these rules, and one draw needn't show every extreme that they name: `patch_order`: each patch appears once. Every entry is a multiple of 96; patch p covers positions patch_start[p] to patch_start[p] + 383; patches may intersect.
All inputs are finite; a program needn't handle non-finite values.
Results may differ from the reference program's by a relative error of at most 0.015.
Values may be sent and summed in bfloat16 or wider, within the bound.
A program may use at most 64 MiB of HBM per device.

```python
import math
import jax
import jax.numpy as jnp
from jax import lax

HEADS = 24
HEAD_DIM = 128
D = 3072
CT_DEV = 96
PATCHES = 4
BLOCKS = 2
CACHE = 1536
PATCH_TOK = 384


def draw_patch_start(key, part):
    key = jax.random.fold_in(key, 7)
    key_vals, key_ends = jax.random.split(key)
    span_count = (CACHE - PATCH_TOK) // CT_DEV
    values = jax.random.randint(key_vals, (PATCHES,), 0, span_count + 1)
    chosen = jax.random.permutation(key_ends, PATCHES)
    values = values.at[chosen[0]].set(0)
    values = values.at[chosen[1]].set(span_count)
    return (values * CT_DEV).astype(jnp.int32)


def steps_of(stream_key, shape, cuts, low, high):
    factor_of = 1.0
    for dim, blocks in cuts:
        draws = jax.random.uniform(jax.random.fold_in(jax.random.fold_in(stream_key, 6), dim), (blocks,), jnp.float32, low / len(cuts), high / len(cuts))
        factor_of = factor_of * jnp.repeat(jnp.exp(draws), shape[dim] // blocks).reshape((-1,) + (1,) * (len(shape) - 1 - dim))
    return factor_of


def gaussian(rng, extent, deviation, reach, cuts=(), dtype=jnp.bfloat16):
    values = deviation * jax.random.normal(rng, extent, jnp.float32)
    if cuts:
        values = values * steps_of(rng, extent, cuts, -0.22, 0.18)
    return jnp.clip(values, -reach, reach).astype(dtype)


def setup_inputs(seed: int = 0) -> dict:
    keys = jax.random.split(jax.random.key(seed), 10)
    patches = gaussian(keys[0], (PATCHES, PATCH_TOK, D), 1.0, 6.0, ((1, 16), (2, 8)))
    cache_k = gaussian(keys[1], (BLOCKS, CACHE, D), 1.2, 7.0, ((0, 2), (1, 16), (2, 8)))
    cache_v = gaussian(keys[2], (BLOCKS, CACHE, D), 1.0, 4.0, ((0, 2), (1, 16), (2, 8)))
    w_qkv = gaussian(keys[3], (BLOCKS, D, 3, D), D ** -0.5, 0.109375, ((0, 2), (1, 16), (3, 8)))
    w_out = gaussian(keys[4], (BLOCKS, D, D), D ** -0.5, 0.109375, ((0, 2), (2, 8)))
    modulation = gaussian(keys[5], (BLOCKS, 3, D), 1.0, 4.0, ((0, 2),), jnp.float32)
    qk_gain = jnp.clip(jnp.exp(math.log(2.2) - 0.7884574 * jax.random.uniform(keys[6], (BLOCKS, 2, HEAD_DIM), jnp.float32) ** steps_of(keys[6], (BLOCKS, 2, HEAD_DIM), ((0, 2),), -0.2, 0.2)), 1.0, 2.2)
    patch_order = jax.random.permutation(keys[7], PATCHES).astype(jnp.int32)
    patch_start = draw_patch_start(jax.random.fold_in(keys[9], 71), 0)
    return {"patches": patches, "cache_k": cache_k, "cache_v": cache_v, "w_qkv": w_qkv, "w_out": w_out, "modulation": modulation, "qk_gain": qk_gain, "patch_order": patch_order, "patch_start": patch_start}


def layer_norm(stream):
    average = lax.optimization_barrier(jnp.mean(stream, axis=-1, keepdims=True))
    spread = lax.optimization_barrier(jnp.mean((stream - average) ** 2, axis=-1, keepdims=True))
    return (stream - average) * lax.rsqrt(spread + 1e-06)

def rms_heads(heads_in, norm_gain):
    power = lax.optimization_barrier(jnp.mean(heads_in * heads_in, axis=-1, keepdims=True))
    return heads_in * lax.rsqrt(power + 1e-06) * norm_gain

def reference(patches, cache_k, cache_v, w_qkv, w_out, modulation, qk_gain, patch_order, patch_start):
    score_scale = 1.0 / math.sqrt(HEAD_DIM)
    hidden = patches
    block_list = []
    key_list = []
    value_list = []
    for block_idx in range(BLOCKS):
        key_cache = cache_k[block_idx]
        value_cache = cache_v[block_idx]
        modulate = modulation[block_idx]
        result = jnp.zeros_like(patches)
        for step_idx in range(PATCHES):
            patch_id = patch_order[step_idx].astype(jnp.int32)
            begin = patch_start[patch_id].astype(jnp.int32)
            stream = hidden[patch_id].astype(jnp.float32)
            normed = (layer_norm(stream) * (1.0 + modulate[1]) + modulate[0]).astype(jnp.bfloat16)
            projected = jnp.dot(normed, w_qkv[block_idx].reshape(D, 3 * D), preferred_element_type=jnp.float32)
            projected = projected.reshape(PATCH_TOK, 3, HEADS, HEAD_DIM)
            queries = rms_heads(projected[:, 0], qk_gain[block_idx, 0]).astype(jnp.bfloat16)
            fresh_key = rms_heads(projected[:, 1], qk_gain[block_idx, 1]).astype(jnp.bfloat16)
            fresh_value = projected[:, 2].astype(jnp.bfloat16)
            zero_index = jnp.zeros((), jnp.int32)
            key_cache = lax.dynamic_update_slice(key_cache, fresh_key.reshape(PATCH_TOK, D), (begin, zero_index))
            value_cache = lax.dynamic_update_slice(value_cache, fresh_value.reshape(PATCH_TOK, D), (begin, zero_index))
            key_heads = key_cache.reshape(CACHE, HEADS, HEAD_DIM).astype(jnp.float32)
            val_heads = value_cache.reshape(CACHE, HEADS, HEAD_DIM).astype(jnp.float32)
            scores = jnp.einsum('qhd,khd->hqk', queries.astype(jnp.float32), key_heads) * score_scale
            weights_exp = jnp.exp(scores)
            denom_sum = lax.optimization_barrier(jnp.sum(weights_exp, axis=-1))
            rounded = lax.optimization_barrier(weights_exp.astype(jnp.bfloat16))
            numer_sum = jnp.einsum('hqk,khd->qhd', rounded.astype(jnp.float32), val_heads)
            attended = (numer_sum / jnp.transpose(denom_sum)[:, :, None]).astype(jnp.bfloat16).reshape(PATCH_TOK, D)
            projected_out = jnp.dot(attended, w_out[block_idx], preferred_element_type=jnp.float32)
            updated = (stream + modulate[2] * projected_out).astype(jnp.bfloat16)
            result = result.at[patch_id].set(updated)
        hidden = result
        block_list.append(result)
        key_list.append(key_cache)
        value_list.append(value_cache)
    return (jnp.stack(block_list), jnp.stack(key_list), jnp.stack(value_list))
```

```python
import functools
import math

import jax
import jax.numpy as jnp
from jax import lax
from jax.experimental import pallas as pl
from jax.experimental.pallas import tpu as pltpu
from jax.sharding import PartitionSpec as P

MESH = pl.DeviceIdType.MESH
F32 = jnp.float32
BF16 = jnp.bfloat16
FAR = -1e30


def square_side(count):
    side = math.isqrt(count)
    assert side * side == count
    return side


def block_kernel(
    nz,
    ny,
    nx,
    patches,
    tok,
    head_dim,
    order,
    start,
    x_in,
    ck,
    cv,
    w,
    wo,
    mod,
    gain,
    bo,
    nk,
    nv,
    xg,
    ns,
    xe,
    wbuf,
    wo_v,
    psend,
    precv,
    qg,
    kall,
    vall,
    bias,
    tag,
    nsend,
    nrecv,
    ag,
    rsend,
    rrecv,
    loc,
    xg_s,
    xg_r,
    ns_s,
    xe_r,
    w_s,
    w_r,
    c_s,
    c_r,
    p_s,
    p_r,
    q_s,
    q_r,
    kv_s,
    kv_r,
    n_s,
    n_r,
    ag_s,
    ag_r,
    r_s,
    r_r,
    hand_s,
    hand_r,
    go,
):
    sec = lax.axis_index("section")
    z = lax.axis_index("head")
    seq = lax.axis_index("seq")
    y = seq // nx
    x = lax.rem(seq, nx)
    rows, feat = x_in.shape
    chunk = ck.shape[0]
    heads = feat // head_dim
    width = nz * feat
    w_rows = w.shape[1]
    hz = nz // ny
    fresh = ny * rows
    span = ny * chunk
    pad = rrecv.shape[2]

    def on_z(d):
        return (sec, lax.rem(z + d, nz), seq)

    def on_y(d):
        return (sec, z, lax.rem(y + d, ny) * nx + x)

    def on_x(d):
        return (sec, z, y * nx + lax.rem(x + d, nx))

    other = (1 - sec, z, seq)

    def z_at(d):
        return lax.rem(z + d, nz)

    def y_at(d):
        return lax.rem(y + d, ny)

    def x_at(d):
        return lax.rem(x + d, nx)

    def copy(src, dst, ss, rs, dev):
        return pltpu.make_async_remote_copy(
            src_ref=src, dst_ref=dst, send_sem=ss, recv_sem=rs, device_id=dev, device_id_type=MESH
        )

    def arrived(dst, rs):
        copy(dst, dst, rs, rs, other).wait_recv()

    barrier = pltpu.get_barrier_semaphore()
    partners = (
        [on_z(d) for d in range(1, nz)]
        + [on_y(d) for d in range(1, ny)]
        + [on_x(d) for d in range(1, nx)]
        + [other]
    )
    for dev in partners:
        pl.semaphore_signal(barrier, inc=1, device_id=dev, device_id_type=MESH)
    pl.semaphore_wait(barrier, len(partners))

    my_w_rows = pl.ds(pl.multiple_of(x * w_rows, w_rows), w_rows)
    my_cache = pl.ds(pl.multiple_of(fresh + y * chunk, chunk), chunk)
    local = [
        pltpu.make_async_copy(w, wbuf.at[:, my_w_rows, :], loc.at[0]),
        pltpu.make_async_copy(ck, kall.at[my_cache, :], loc.at[1]),
        pltpu.make_async_copy(cv, vall.at[my_cache, :], loc.at[2]),
        pltpu.make_async_copy(wo, wo_v, loc.at[3]),
    ]

    hand = copy(bo, xg.at[z], hand_s, hand_r, other)
    z_copies = [copy(xg.at[z], xg.at[z], xg_s.at[d], xg_r.at[z], on_z(d)) for d in range(1, nz)]
    w_copies = [
        copy(w, wbuf.at[:, my_w_rows, :], w_s.at[d], w_r.at[x], on_x(d)) for d in range(1, nx)
    ]
    cache_copies = [
        copy(src, dst.at[my_cache, :], c_s.at[i, d], c_r.at[i, y], on_y(d))
        for d in range(1, ny)
        for i, (src, dst) in enumerate(((ck, kall), (cv, vall)))
    ]
    n_copies = [copy(ns.at[d], xe.at[y], ns_s.at[d], xe_r.at[y], on_y(d)) for d in range(1, ny)]
    p_copies = [
        [
            copy(psend.at[i, y_at(d)], precv.at[i, y], p_s.at[i, d], p_r.at[i, y], on_y(d))
            for d in range(1, ny)
        ]
        for i in range(3)
    ]
    q_copies = [copy(qg.at[x], qg.at[x], q_s.at[d], q_r.at[x], on_x(d)) for d in range(1, nx)]
    my_fresh = pl.ds(pl.multiple_of(y * rows, rows), rows)
    kv_copies = [
        [
            copy(
                ref.at[my_fresh, :], ref.at[my_fresh, :], kv_s.at[i, d], kv_r.at[i, y], on_y(d)
            )
            for d in range(1, ny)
        ]
        for i, ref in enumerate((kall, vall))
    ]
    num_copies = [
        copy(nsend.at[x_at(d)], nrecv.at[x], n_s.at[d], n_r.at[x], on_x(d)) for d in range(1, nx)
    ]
    a_copies = [copy(ag.at[z], ag.at[z], ag_s.at[d], ag_r.at[z], on_z(d)) for d in range(1, nz)]
    r_copies = [
        copy(rsend.at[i, x_at(d)], rrecv.at[i, x], r_s.at[i, d], r_r.at[i, x], on_x(d))
        for d in range(1, nx)
        for i in range(2)
    ]

    @pl.when(sec == 0)
    def _():
        xg[z] = x_in[...]
        for c in z_copies + w_copies:
            c.start()

    for c in local:
        c.start()

    @pl.when(sec == 1)
    def _():
        pl.semaphore_wait(go.at[0], 1)
        for c in w_copies:
            c.start()
        pl.semaphore_wait(go.at[1], 1)
        for c in cache_copies:
            c.start()

    places = [order[i] for i in range(patches)]
    begins = [start[i] for i in range(patches)]
    steps = [
        sum(jnp.where(places[s] == p, s, 0) for s in range(patches)) for p in range(patches)
    ]

    def first_after(step, pos):
        found = patches
        for p in range(patches):
            hit = (steps[p] > step) & (begins[p] <= pos) & (pos < begins[p] + span)
            found = jnp.where(hit, jnp.minimum(found, steps[p]), found)
        return found

    lane = lax.broadcasted_iota(jnp.int32, (tok, head_dim), 1)
    lane_chunk = lax.broadcasted_iota(jnp.int32, (chunk, head_dim), 1)
    for j in range(ny):
        parts = []
        for p in range(patches):
            upto = first_after(steps[p], begins[p] + j * chunk)
            parts.append(jnp.where((lane >= steps[p]) & (lane < upto), 0.0, FAR))
        bias[j * rows : (j + 1) * rows, :] = jnp.concatenate(parts, axis=0).astype(BF16)
        upto = first_after(-1, (j * nx + x) * chunk)
        bias[fresh + j * chunk : fresh + (j + 1) * chunk, :] = jnp.where(
            lane_chunk < upto, 0.0, FAR
        ).astype(BF16)
    tag[...] = jnp.concatenate(
        [jnp.where(lane == steps[p], 1.0, 0.0) for p in range(patches)], axis=0
    ).astype(BF16)

    @pl.when(sec == 1)
    def _():
        arrived(xg.at[z], hand_r)
        for c in z_copies:
            c.start()

    for d in range(1, nz):
        arrived(xg.at[z_at(d)], xg_r.at[z_at(d)])
    total = jnp.zeros((rows, feat), F32)
    for i in range(nz):
        total += xg[i].astype(F32)
    mean = jnp.sum(total, axis=-1, keepdims=True) * (1.0 / width)
    total = jnp.zeros((rows, feat), F32)
    for i in range(nz):
        diff = xg[i].astype(F32) - mean
        total += diff * diff
    spread = jnp.sum(total, axis=-1, keepdims=True) * (1.0 / width)
    scale = lax.rsqrt(spread + 1e-06)

    def normed(i):
        at = pl.ds(pl.multiple_of(i * feat, feat), feat)
        value = (xg[i].astype(F32) - mean) * scale * (1.0 + mod[1, :, at]) + mod[0, :, at]
        return value.astype(BF16)

    for d in list(range(1, ny)) + [0]:
        for i in range(hz):
            value = normed(y_at(d) * hz + i)
            if d:
                ns[d, :, i * feat : (i + 1) * feat] = value
            else:
                xe[y, :, i * feat : (i + 1) * feat] = value
        if d:
            n_copies[d - 1].start()

    @pl.when(sec == 0)
    def _():
        for c in cache_copies:
            c.start()

    local[0].wait()
    for d in range(1, nx):
        at = pl.ds(pl.multiple_of(x_at(d) * w_rows, w_rows), w_rows)
        arrived(wbuf.at[:, at, :], w_r.at[x_at(d)])

    @pl.when(sec == 0)
    def _():
        pl.semaphore_signal(go.at[0], inc=1, device_id=other, device_id_type=MESH)

    for d in range(1, ny):
        arrived(xe.at[y_at(d)], xe_r.at[y_at(d)])
    tokens = xe[...].reshape(ny * rows, hz * feat)
    for i in (1, 0, 2):
        value = jnp.dot(tokens, wbuf[i], preferred_element_type=F32)
        psend[i] = value.astype(BF16).reshape(ny, rows, feat)
        for c in p_copies[i]:
            c.start()

    def projected(i):
        value = psend[i, y].astype(F32)
        for d in range(1, ny):
            arrived(precv.at[i, y_at(d)], p_r.at[i, y_at(d)])
            value += precv[i, y_at(d)].astype(F32)
        return value

    def rms_heads(value, which):
        out = []
        for h in range(heads):
            part = value[:, h * head_dim : (h + 1) * head_dim]
            power = jnp.sum(part * part, axis=-1, keepdims=True) * (1.0 / head_dim)
            out.append(part * lax.rsqrt(power + 1e-06) * gain[which : which + 1, :])
        return jnp.concatenate(out, axis=-1).astype(BF16)

    kall[my_fresh, :] = rms_heads(projected(1), 1)
    for c in kv_copies[0]:
        c.start()
    qg[x] = rms_heads(projected(0), 0)
    for c in q_copies:
        c.start()
    vall[my_fresh, :] = projected(2).astype(BF16)
    for c in kv_copies[1]:
        c.start()

    for i, ref in enumerate((kall, vall)):
        local[1 + i].wait()
        for d in range(1, ny):
            at = pl.ds(pl.multiple_of(fresh + y_at(d) * chunk, chunk), chunk)
            arrived(ref.at[at, :], c_r.at[i, y_at(d)])
    for i, ref in enumerate((kall, vall)):
        for d in range(1, ny):
            at = pl.ds(pl.multiple_of(y_at(d) * rows, rows), rows)
            arrived(ref.at[at, :], kv_r.at[i, y_at(d)])
    for d in range(1, nx):
        arrived(qg.at[x_at(d)], q_r.at[x_at(d)])

    @pl.when(sec == 0)
    def _():
        pl.semaphore_signal(go.at[1], inc=1, device_id=other, device_id_type=MESH)

    tags = jnp.concatenate([tag[...]] * nx, axis=0)
    lane_all = lax.broadcasted_iota(jnp.int32, (nx * rows, head_dim), 1)
    sums = jnp.zeros((nx * rows, head_dim), F32)
    exponent = math.log2(math.e) / math.sqrt(head_dim)
    for h in range(heads):
        at = slice(h * head_dim, (h + 1) * head_dim)
        queries = jnp.concatenate([qg[:, :, at].reshape(nx * rows, head_dim), tags], axis=1)
        keys = jnp.concatenate([kall[:, at], bias[...]], axis=1)
        scores = lax.dot_general(
            queries, keys, (((1,), (1,)), ((), ())), preferred_element_type=F32
        )
        weight = jnp.exp2(scores * exponent)
        denom = jnp.sum(weight, axis=-1, keepdims=True)
        numer = jnp.dot(weight.astype(BF16), vall[:, at], preferred_element_type=F32)
        nsend[:, :, at] = numer.astype(BF16).reshape(nx, rows, head_dim)
        high = denom.astype(BF16).astype(F32)
        sums = jnp.where(lane_all == 2 * h, high, sums)
        sums = jnp.where(lane_all == 2 * h + 1, denom - high, sums)
    nsend[:, :, feat:] = sums.astype(BF16).reshape(nx, rows, head_dim)
    for c in num_copies:
        c.start()

    def source(c):
        pos = c * chunk
        last = -1
        first_row = -fresh - pad
        for p in range(patches):
            hit = (begins[p] <= pos) & (pos < begins[p] + span) & (steps[p] > last)
            last = jnp.where(hit, steps[p], last)
            row = (pos - begins[p]) // chunk * rows + p * tok
            first_row = jnp.where(hit, row, first_row)
        return first_row, last

    in_row = lax.broadcasted_iota(jnp.int32, (pad, fresh), 0)
    in_col = lax.broadcasted_iota(jnp.int32, (pad, fresh), 1)
    picks = []
    for c in range(nx):
        first_row, _ = source(y * nx + c)
        hit = (in_col - in_row == first_row) & (in_row < tok)
        picks.append(jnp.where(hit, 1.0, 0.0).astype(BF16))
    pick = jnp.concatenate(picks, axis=0)
    for i, ref in enumerate((kall, vall)):
        value = jnp.dot(pick, ref[0:fresh, :], preferred_element_type=F32)
        rsend[i] = value.astype(BF16).reshape(nx, pad, feat)
    for c in r_copies:
        c.start()

    numer = nsend[x, :, 0:feat].astype(F32)
    denom = nsend[x, :, feat:].astype(F32)
    for d in range(1, nx):
        arrived(nrecv.at[x_at(d)], n_r.at[x_at(d)])
        numer += nrecv[x_at(d), :, 0:feat].astype(F32)
        denom += nrecv[x_at(d), :, feat:].astype(F32)
    attended = []
    for h in range(heads):
        part = numer[:, h * head_dim : (h + 1) * head_dim]
        attended.append(part / (denom[:, 2 * h : 2 * h + 1] + denom[:, 2 * h + 1 : 2 * h + 2]))
    ag[z] = jnp.concatenate(attended, axis=-1).astype(BF16)
    for c in a_copies:
        c.start()

    local[3].wait()
    result = jnp.zeros((rows, feat), F32)
    for d in range(nz):
        i = z_at(d)
        if d:
            arrived(ag.at[i], ag_r.at[i])
        at = pl.ds(pl.multiple_of(i * feat, feat), feat)
        result += jnp.dot(ag[i], wo_v[at, :], preferred_element_type=F32)
    gate = mod[2, :, pl.ds(pl.multiple_of(z * feat, feat), feat)]
    bo[...] = (xg[z].astype(F32) + gate * result).astype(BF16)

    @pl.when(sec == 0)
    def _():
        hand.start()

    for i in range(2):
        for d in range(1, nx):
            arrived(rrecv.at[i, x_at(d)], r_r.at[i, x_at(d)])
        rrecv[i, x] = rsend[i, x]
    out_row = lax.broadcasted_iota(jnp.int32, (chunk, nx * pad), 0)
    out_col = lax.broadcasted_iota(jnp.int32, (chunk, nx * pad), 1)
    block = out_col // pad
    within = out_col - block * pad
    hit = (out_row == block * tok + within) & (within < tok)
    place = jnp.where(hit, 1.0, 0.0).astype(BF16)
    _, last = source(seq)
    for i, (old, new) in enumerate(((kall, nk), (vall, nv))):
        value = jnp.dot(place, rrecv[i].reshape(nx * pad, feat), preferred_element_type=F32)
        new[...] = jnp.where(last >= 0, value, old[my_cache, :].astype(F32)).astype(BF16)

    @pl.when(sec == 0)
    def _():
        hand.wait_send()

    for c in z_copies + w_copies + cache_copies + n_copies + q_copies + num_copies:
        c.wait_send()
    for c in sum(p_copies, []) + sum(kv_copies, []) + a_copies + r_copies:
        c.wait_send()


def per_device(
    patches, cache_k, cache_v, w_qkv, w_out, modulation, qk_gain, patch_order, patch_start
):
    nz = lax.axis_size("head")
    ny = nx = square_side(lax.axis_size("seq"))
    count, tok, feat = patches.shape
    chunk = cache_k.shape[1]
    head_dim = qk_gain.shape[-1]
    rows = count * tok
    hz = nz // ny
    width = nz * feat
    w_rows = w_qkv.shape[1]
    pad = -(-tok // 16) * 16
    keys = ny * (rows + chunk)
    dma = pltpu.SemaphoreType.DMA
    vmem = pl.BlockSpec(memory_space=pltpu.VMEM)
    smem = pl.BlockSpec(memory_space=pltpu.SMEM)
    hbm = pl.BlockSpec(memory_space=pl.ANY)
    out, new_k, new_v = pl.pallas_call(
        functools.partial(block_kernel, nz, ny, nx, count, tok, head_dim),
        name="blocks",
        out_shape=(
            jax.ShapeDtypeStruct((rows, feat), BF16),
            jax.ShapeDtypeStruct((chunk, feat), BF16),
            jax.ShapeDtypeStruct((chunk, feat), BF16),
        ),
        in_specs=[smem, smem, vmem, vmem, vmem, hbm, hbm, vmem, vmem],
        out_specs=(vmem, vmem, vmem),
        scratch_shapes=[
            pltpu.VMEM((nz, rows, feat), BF16),
            pltpu.VMEM((ny, rows, hz * feat), BF16),
            pltpu.VMEM((ny, rows, hz * feat), BF16),
            pltpu.VMEM((3, nx * w_rows, feat), BF16),
            pltpu.VMEM((width, feat), BF16),
            pltpu.VMEM((3, ny, rows, feat), BF16),
            pltpu.VMEM((3, ny, rows, feat), BF16),
            pltpu.VMEM((nx, rows, feat), BF16),
            pltpu.VMEM((keys, feat), BF16),
            pltpu.VMEM((keys, feat), BF16),
            pltpu.VMEM((keys, head_dim), BF16),
            pltpu.VMEM((rows, head_dim), BF16),
            pltpu.VMEM((nx, rows, feat + head_dim), BF16),
            pltpu.VMEM((nx, rows, feat + head_dim), BF16),
            pltpu.VMEM((nz, rows, feat), BF16),
            pltpu.VMEM((2, nx, pad, feat), BF16),
            pltpu.VMEM((2, nx, pad, feat), BF16),
            dma((4,)),
            dma((nz,)),
            dma((nz,)),
            dma((ny,)),
            dma((ny,)),
            dma((nx,)),
            dma((nx,)),
            dma((2, ny)),
            dma((2, ny)),
            dma((3, ny)),
            dma((3, ny)),
            dma((nx,)),
            dma((nx,)),
            dma((2, ny)),
            dma((2, ny)),
            dma((nx,)),
            dma((nx,)),
            dma((nz,)),
            dma((nz,)),
            dma((2, nx)),
            dma((2, nx)),
            dma,
            dma,
            pltpu.SemaphoreType.REGULAR((2,)),
        ],
        compiler_params=pltpu.CompilerParams(
            collective_id=0, has_side_effects=True, vmem_limit_bytes=48 << 20
        ),
    )(
        patch_order,
        patch_start,
        patches.reshape(rows, feat),
        cache_k[0],
        cache_v[0],
        jnp.transpose(w_qkv[0], (1, 0, 2)),
        w_out[0],
        jnp.transpose(modulation, (1, 0, 2)),
        qk_gain[0],
    )
    return (out.reshape(1, count, tok, feat), new_k[None], new_v[None])


def solution(mesh):
    return jax.shard_map(
        per_device,
        mesh=mesh,
        in_specs=(
            P(None, "seq", "head"),
            P("section", "seq", "head"),
            P("section", "seq", "head"),
            P("section", "seq", None, "head"),
            P("section", None, "head"),
            P("section", None, None),
            P("section", None, None),
            P(),
            P(),
        ),
        out_specs=(
            P("section", None, "seq", "head"),
            P("section", "seq", "head"),
            P("section", "seq", "head"),
        ),
        check_vma=False,
    )
```

```python
import functools
import math

import jax
import jax.numpy as jnp
from jax import lax
from jax.experimental import pallas as pl
from jax.experimental.pallas import tpu as pltpu
from jax.sharding import PartitionSpec as P

MESH = pl.DeviceIdType.MESH
F32 = jnp.float32
BF16 = jnp.bfloat16
FAR = -1e30


def square_side(count):
    side = math.isqrt(count)
    assert side * side == count
    return side


def block_kernel(
    nz,
    ny,
    nx,
    patches,
    tok,
    head_dim,
    order_h,
    start_h,
    x_in,
    ck,
    cv,
    w,
    wo,
    mod_h,
    gain_h,
    bo,
    nk,
    nv,
    order,
    start,
    mod,
    gain,
    xg,
    ns,
    xe,
    wbuf,
    wo_v,
    psend,
    precv,
    qg,
    kall,
    vall,
    bias,
    tag,
    nsend,
    nrecv,
    ag,
    rsend,
    rrecv,
    loc,
    xg_s,
    xg_r,
    ns_s,
    xe_r,
    w_s,
    w_r,
    c_s,
    c_r,
    p_s,
    p_r,
    q_s,
    q_r,
    kv_s,
    kv_r,
    n_s,
    n_r,
    ag_s,
    ag_r,
    r_s,
    r_r,
    hand_s,
    go,
):
    sec = lax.axis_index("section")
    z = lax.axis_index("head")
    seq = lax.axis_index("seq")
    y = seq // nx
    x = lax.rem(seq, nx)
    _, rows, feat = xg.shape
    chunk = ck.shape[0]
    heads = feat // head_dim
    width = nz * feat
    w_rows = w.shape[1]
    hz = nz // ny
    fresh = ny * rows
    span = ny * chunk
    pad = rrecv.shape[2]

    def on_z(d):
        return (sec, lax.rem(z + d, nz), seq)

    def on_y(d):
        return (sec, z, lax.rem(y + d, ny) * nx + x)

    def on_x(d):
        return (sec, z, y * nx + lax.rem(x + d, nx))

    other = (1 - sec, z, seq)

    def next_block(d):
        return (1, lax.rem(z + d, nz), seq)

    def last_block(d):
        return (0, lax.rem(z + d, nz), seq)

    def z_at(d):
        return lax.rem(z + d, nz)

    def y_at(d):
        return lax.rem(y + d, ny)

    def x_at(d):
        return lax.rem(x + d, nx)

    def copy(src, dst, ss, rs, dev):
        return pltpu.make_async_remote_copy(
            src_ref=src, dst_ref=dst, send_sem=ss, recv_sem=rs, device_id=dev, device_id_type=MESH
        )

    def arrived(dst, rs):
        copy(dst, dst, rs, rs, other).wait_recv()

    barrier = pltpu.get_barrier_semaphore()
    partners = (
        [on_z(d) for d in range(1, nz)]
        + [on_y(d) for d in range(1, ny)]
        + [on_x(d) for d in range(1, nx)]
        + [other]
    )
    for dev in partners:
        pl.semaphore_signal(barrier, inc=1, device_id=dev, device_id_type=MESH)

    @pl.when(sec == 1)
    def _():
        for d in range(1, nz):
            pl.semaphore_signal(barrier, inc=1, device_id=last_block(d), device_id_type=MESH)
        pl.semaphore_wait(barrier, len(partners))

    @pl.when(sec == 0)
    def _():
        pl.semaphore_wait(barrier, len(partners) + nz - 1)

    my_w_rows = pl.ds(pl.multiple_of(x * w_rows, w_rows), w_rows)
    my_cache = pl.ds(pl.multiple_of(fresh + y * chunk, chunk), chunk)
    local = [
        pltpu.make_async_copy(w, wbuf.at[:, my_w_rows, :], loc.at[0]),
        pltpu.make_async_copy(ck, kall.at[my_cache, :], loc.at[1]),
        pltpu.make_async_copy(cv, vall.at[my_cache, :], loc.at[2]),
        pltpu.make_async_copy(wo, wo_v, loc.at[3]),
        pltpu.make_async_copy(order_h, order, loc.at[4]),
        pltpu.make_async_copy(start_h, start, loc.at[5]),
        pltpu.make_async_copy(mod_h, mod, loc.at[6]),
        pltpu.make_async_copy(gain_h, gain, loc.at[7]),
    ]
    own_x = pltpu.make_async_copy(x_in, xg.at[z], loc.at[8])

    z_copies = [copy(x_in, xg.at[z], xg_s.at[d], xg_r.at[z], on_z(d)) for d in range(1, nz)]
    hand_copies = [
        copy(bo, xg.at[z], hand_s.at[d], xg_r.at[z], next_block(d)) for d in range(nz)
    ]
    w_copies = [
        copy(w, wbuf.at[:, my_w_rows, :], w_s.at[d], w_r.at[x], on_x(d)) for d in range(1, nx)
    ]
    cache_copies = [
        copy(src, dst.at[my_cache, :], c_s.at[i, d], c_r.at[i, y], on_y(d))
        for d in range(1, ny)
        for i, (src, dst) in enumerate(((ck, kall), (cv, vall)))
    ]
    n_copies = [copy(ns.at[d], xe.at[y], ns_s.at[d], xe_r.at[y], on_y(d)) for d in range(1, ny)]
    p_copies = [
        [
            copy(psend.at[i, y_at(d)], precv.at[i, y], p_s.at[i, d], p_r.at[i, y], on_y(d))
            for d in range(1, ny)
        ]
        for i in range(3)
    ]
    q_copies = [copy(qg.at[x], qg.at[x], q_s.at[d], q_r.at[x], on_x(d)) for d in range(1, nx)]
    my_fresh = pl.ds(pl.multiple_of(y * rows, rows), rows)
    kv_copies = [
        [
            copy(
                ref.at[my_fresh, :], ref.at[my_fresh, :], kv_s.at[i, d], kv_r.at[i, y], on_y(d)
            )
            for d in range(1, ny)
        ]
        for i, ref in enumerate((kall, vall))
    ]
    num_copies = [
        copy(nsend.at[x_at(d)], nrecv.at[x], n_s.at[d], n_r.at[x], on_x(d)) for d in range(1, nx)
    ]
    a_copies = [copy(ag.at[z], ag.at[z], ag_s.at[d], ag_r.at[z], on_z(d)) for d in range(1, nz)]
    r_copies = [
        copy(rsend.at[i, x_at(d)], rrecv.at[i, x], r_s.at[i, d], r_r.at[i, x], on_x(d))
        for d in range(1, nx)
        for i in range(2)
    ]

    @pl.when(sec == 0)
    def _():
        for c in z_copies + [own_x] + w_copies:
            c.start()

    for i in (4, 5, 6, 7, 0, 1, 2, 3):
        local[i].start()

    @pl.when(sec == 1)
    def _():
        pl.semaphore_wait(go.at[0], 1)
        for c in w_copies:
            c.start()
        pl.semaphore_wait(go.at[1], 1)
        for c in cache_copies:
            c.start()

    local[4].wait()
    local[5].wait()
    places = [order[i] for i in range(patches)]
    begins = [start[i] for i in range(patches)]
    steps = [
        sum(jnp.where(places[s] == p, s, 0) for s in range(patches)) for p in range(patches)
    ]

    def first_after(step, pos):
        found = patches
        for p in range(patches):
            hit = (steps[p] > step) & (begins[p] <= pos) & (pos < begins[p] + span)
            found = jnp.where(hit, jnp.minimum(found, steps[p]), found)
        return found

    lane = lax.broadcasted_iota(jnp.int32, (tok, head_dim), 1)
    lane_chunk = lax.broadcasted_iota(jnp.int32, (chunk, head_dim), 1)
    for j in range(ny):
        parts = []
        for p in range(patches):
            upto = first_after(steps[p], begins[p] + j * chunk)
            parts.append(jnp.where((lane >= steps[p]) & (lane < upto), 0.0, FAR))
        bias[j * rows : (j + 1) * rows, :] = jnp.concatenate(parts, axis=0).astype(BF16)
        upto = first_after(-1, (j * nx + x) * chunk)
        bias[fresh + j * chunk : fresh + (j + 1) * chunk, :] = jnp.where(
            lane_chunk < upto, 0.0, FAR
        ).astype(BF16)
    tag[...] = jnp.concatenate(
        [jnp.where(lane == steps[p], 1.0, 0.0) for p in range(patches)], axis=0
    ).astype(BF16)

    @pl.when(sec == 0)
    def _():
        own_x.wait()

    @pl.when(sec == 1)
    def _():
        arrived(xg.at[z], xg_r.at[z])

    for d in range(1, nz):
        arrived(xg.at[z_at(d)], xg_r.at[z_at(d)])
    total = jnp.zeros((rows, feat), F32)
    for i in range(nz):
        total += xg[i].astype(F32)
    mean = jnp.sum(total, axis=-1, keepdims=True) * (1.0 / width)
    total = jnp.zeros((rows, feat), F32)
    for i in range(nz):
        diff = xg[i].astype(F32) - mean
        total += diff * diff
    spread = jnp.sum(total, axis=-1, keepdims=True) * (1.0 / width)
    scale = lax.rsqrt(spread + 1e-06)
    local[6].wait()
    local[7].wait()

    def normed(i):
        at = pl.ds(pl.multiple_of(i * feat, feat), feat)
        value = (xg[i].astype(F32) - mean) * scale * (1.0 + mod[1, :, at]) + mod[0, :, at]
        return value.astype(BF16)

    for d in list(range(1, ny)) + [0]:
        for i in range(hz):
            value = normed(y_at(d) * hz + i)
            if d:
                ns[d, :, i * feat : (i + 1) * feat] = value
            else:
                xe[y, :, i * feat : (i + 1) * feat] = value
        if d:
            n_copies[d - 1].start()

    @pl.when(sec == 0)
    def _():
        for c in cache_copies:
            c.start()

    local[0].wait()
    for d in range(1, nx):
        at = pl.ds(pl.multiple_of(x_at(d) * w_rows, w_rows), w_rows)
        arrived(wbuf.at[:, at, :], w_r.at[x_at(d)])

    @pl.when(sec == 0)
    def _():
        pl.semaphore_signal(go.at[0], inc=1, device_id=other, device_id_type=MESH)

    for d in range(1, ny):
        arrived(xe.at[y_at(d)], xe_r.at[y_at(d)])
    tokens = xe[...].reshape(ny * rows, hz * feat)
    for i in (1, 0, 2):
        value = jnp.dot(tokens, wbuf[i], preferred_element_type=F32)
        psend[i] = value.astype(BF16).reshape(ny, rows, feat)
        for c in p_copies[i]:
            c.start()

    def projected(i):
        value = psend[i, y].astype(F32)
        for d in range(1, ny):
            arrived(precv.at[i, y_at(d)], p_r.at[i, y_at(d)])
            value += precv[i, y_at(d)].astype(F32)
        return value

    def rms_heads(value, which):
        out = []
        for h in range(heads):
            part = value[:, h * head_dim : (h + 1) * head_dim]
            power = jnp.sum(part * part, axis=-1, keepdims=True) * (1.0 / head_dim)
            out.append(part * lax.rsqrt(power + 1e-06) * gain[which : which + 1, :])
        return jnp.concatenate(out, axis=-1).astype(BF16)

    kall[my_fresh, :] = rms_heads(projected(1), 1)
    for c in kv_copies[0]:
        c.start()
    qg[x] = rms_heads(projected(0), 0)
    for c in q_copies:
        c.start()
    vall[my_fresh, :] = projected(2).astype(BF16)
    for c in kv_copies[1]:
        c.start()

    for i, ref in enumerate((kall, vall)):
        local[1 + i].wait()
        for d in range(1, ny):
            at = pl.ds(pl.multiple_of(fresh + y_at(d) * chunk, chunk), chunk)
            arrived(ref.at[at, :], c_r.at[i, y_at(d)])
    for i, ref in enumerate((kall, vall)):
        for d in range(1, ny):
            at = pl.ds(pl.multiple_of(y_at(d) * rows, rows), rows)
            arrived(ref.at[at, :], kv_r.at[i, y_at(d)])
    for d in range(1, nx):
        arrived(qg.at[x_at(d)], q_r.at[x_at(d)])

    @pl.when(sec == 0)
    def _():
        pl.semaphore_signal(go.at[1], inc=1, device_id=other, device_id_type=MESH)

    tags = jnp.concatenate([tag[...]] * nx, axis=0)
    lane_all = lax.broadcasted_iota(jnp.int32, (nx * rows, head_dim), 1)
    sums = jnp.zeros((nx * rows, head_dim), F32)
    exponent = math.log2(math.e) / math.sqrt(head_dim)
    for h in range(heads):
        at = slice(h * head_dim, (h + 1) * head_dim)
        queries = jnp.concatenate([qg[:, :, at].reshape(nx * rows, head_dim), tags], axis=1)
        keys = jnp.concatenate([kall[:, at], bias[...]], axis=1)
        scores = lax.dot_general(
            queries, keys, (((1,), (1,)), ((), ())), preferred_element_type=F32
        )
        weight = jnp.exp2(scores * exponent)
        denom = jnp.sum(weight, axis=-1, keepdims=True)
        numer = jnp.dot(weight.astype(BF16), vall[:, at], preferred_element_type=F32)
        nsend[:, :, at] = numer.astype(BF16).reshape(nx, rows, head_dim)
        high = denom.astype(BF16).astype(F32)
        sums = jnp.where(lane_all == 2 * h, high, sums)
        sums = jnp.where(lane_all == 2 * h + 1, denom - high, sums)
    nsend[:, :, feat:] = sums.astype(BF16).reshape(nx, rows, head_dim)
    for c in num_copies:
        c.start()

    def source(c):
        pos = c * chunk
        last = -1
        first_row = -fresh - pad
        for p in range(patches):
            hit = (begins[p] <= pos) & (pos < begins[p] + span) & (steps[p] > last)
            last = jnp.where(hit, steps[p], last)
            row = (pos - begins[p]) // chunk * rows + p * tok
            first_row = jnp.where(hit, row, first_row)
        return first_row, last

    in_row = lax.broadcasted_iota(jnp.int32, (pad, fresh), 0)
    in_col = lax.broadcasted_iota(jnp.int32, (pad, fresh), 1)
    picks = []
    for c in range(nx):
        first_row, _ = source(y * nx + c)
        hit = (in_col - in_row == first_row) & (in_row < tok)
        picks.append(jnp.where(hit, 1.0, 0.0).astype(BF16))
    pick = jnp.concatenate(picks, axis=0)
    for i, ref in enumerate((kall, vall)):
        value = jnp.dot(pick, ref[0:fresh, :], preferred_element_type=F32)
        rsend[i] = value.astype(BF16).reshape(nx, pad, feat)
    for c in r_copies:
        c.start()

    numer = nsend[x, :, 0:feat].astype(F32)
    denom = nsend[x, :, feat:].astype(F32)
    for d in range(1, nx):
        arrived(nrecv.at[x_at(d)], n_r.at[x_at(d)])
        numer += nrecv[x_at(d), :, 0:feat].astype(F32)
        denom += nrecv[x_at(d), :, feat:].astype(F32)
    attended = []
    for h in range(heads):
        part = numer[:, h * head_dim : (h + 1) * head_dim]
        attended.append(part / (denom[:, 2 * h : 2 * h + 1] + denom[:, 2 * h + 1 : 2 * h + 2]))
    ag[z] = jnp.concatenate(attended, axis=-1).astype(BF16)
    for c in a_copies:
        c.start()

    local[3].wait()
    result = jnp.zeros((rows, feat), F32)
    for d in range(nz):
        i = z_at(d)
        if d:
            arrived(ag.at[i], ag_r.at[i])
        at = pl.ds(pl.multiple_of(i * feat, feat), feat)
        result += jnp.dot(ag[i], wo_v[at, :], preferred_element_type=F32)
    gate = mod[2, :, pl.ds(pl.multiple_of(z * feat, feat), feat)]
    bo[...] = (xg[z].astype(F32) + gate * result).astype(BF16)

    @pl.when(sec == 0)
    def _():
        for c in hand_copies:
            c.start()

    for i in range(2):
        for d in range(1, nx):
            arrived(rrecv.at[i, x_at(d)], r_r.at[i, x_at(d)])
        rrecv[i, x] = rsend[i, x]
    out_row = lax.broadcasted_iota(jnp.int32, (chunk, nx * pad), 0)
    out_col = lax.broadcasted_iota(jnp.int32, (chunk, nx * pad), 1)
    block = out_col // pad
    within = out_col - block * pad
    hit = (out_row == block * tok + within) & (within < tok)
    place = jnp.where(hit, 1.0, 0.0).astype(BF16)
    _, last = source(seq)
    for i, (old, new) in enumerate(((kall, nk), (vall, nv))):
        value = jnp.dot(place, rrecv[i].reshape(nx * pad, feat), preferred_element_type=F32)
        new[...] = jnp.where(last >= 0, value, old[my_cache, :].astype(F32)).astype(BF16)

    @pl.when(sec == 0)
    def _():
        for c in z_copies + hand_copies:
            c.wait_send()

    for c in w_copies + cache_copies + n_copies + q_copies + num_copies:
        c.wait_send()
    for c in sum(p_copies, []) + sum(kv_copies, []) + a_copies + r_copies:
        c.wait_send()


def write_kernel(*refs):
    count = (len(refs) - 1) // 2
    sem = refs[-1]
    copies = [
        pltpu.make_async_copy(refs[i], refs[count + i], sem.at[i]) for i in range(count)
    ]
    for c in copies:
        c.start()
    for c in copies:
        c.wait()


def written(*arrays):
    return pl.pallas_call(
        write_kernel,
        name="write",
        out_shape=tuple(jax.ShapeDtypeStruct(a.shape, a.dtype) for a in arrays),
        in_specs=[pl.BlockSpec(memory_space=pl.ANY)] * len(arrays),
        out_specs=(pl.BlockSpec(memory_space=pl.ANY),) * len(arrays),
        scratch_shapes=[pltpu.SemaphoreType.DMA((len(arrays),))],
        compiler_params=pltpu.CompilerParams(vmem_limit_bytes=60 << 20),
    )(*arrays)


def per_device(
    patches, cache_k, cache_v, w_qkv, w_out, modulation, qk_gain, patch_order, patch_start
):
    nz = lax.axis_size("head")
    ny = nx = square_side(lax.axis_size("seq"))
    count, tok, feat = patches.shape
    chunk = cache_k.shape[1]
    head_dim = qk_gain.shape[-1]
    rows = count * tok
    hz = nz // ny
    width = nz * feat
    w_rows = w_qkv.shape[1]
    pad = -(-tok // 16) * 16
    keys = ny * (rows + chunk)
    dma = pltpu.SemaphoreType.DMA
    vmem = pl.BlockSpec(memory_space=pltpu.VMEM)
    hbm = pl.BlockSpec(memory_space=pl.ANY)
    out, new_k, new_v = pl.pallas_call(
        functools.partial(block_kernel, nz, ny, nx, count, tok, head_dim),
        name="blocks",
        out_shape=(
            jax.ShapeDtypeStruct((rows, feat), BF16),
            jax.ShapeDtypeStruct((chunk, feat), BF16),
            jax.ShapeDtypeStruct((chunk, feat), BF16),
        ),
        in_specs=[hbm] * 9,
        out_specs=(vmem, vmem, vmem),
        scratch_shapes=[
            pltpu.SMEM((count,), jnp.int32),
            pltpu.SMEM((count,), jnp.int32),
            pltpu.VMEM((3, 1, width), F32),
            pltpu.VMEM((2, head_dim), F32),
            pltpu.VMEM((nz, rows, feat), BF16),
            pltpu.VMEM((ny, rows, hz * feat), BF16),
            pltpu.VMEM((ny, rows, hz * feat), BF16),
            pltpu.VMEM((3, nx * w_rows, feat), BF16),
            pltpu.VMEM((width, feat), BF16),
            pltpu.VMEM((3, ny, rows, feat), BF16),
            pltpu.VMEM((3, ny, rows, feat), BF16),
            pltpu.VMEM((nx, rows, feat), BF16),
            pltpu.VMEM((keys, feat), BF16),
            pltpu.VMEM((keys, feat), BF16),
            pltpu.VMEM((keys, head_dim), BF16),
            pltpu.VMEM((rows, head_dim), BF16),
            pltpu.VMEM((nx, rows, feat + head_dim), BF16),
            pltpu.VMEM((nx, rows, feat + head_dim), BF16),
            pltpu.VMEM((nz, rows, feat), BF16),
            pltpu.VMEM((2, nx, pad, feat), BF16),
            pltpu.VMEM((2, nx, pad, feat), BF16),
            dma((9,)),
            dma((nz,)),
            dma((nz,)),
            dma((ny,)),
            dma((ny,)),
            dma((nx,)),
            dma((nx,)),
            dma((2, ny)),
            dma((2, ny)),
            dma((3, ny)),
            dma((3, ny)),
            dma((nx,)),
            dma((nx,)),
            dma((2, ny)),
            dma((2, ny)),
            dma((nx,)),
            dma((nx,)),
            dma((nz,)),
            dma((nz,)),
            dma((2, nx)),
            dma((2, nx)),
            dma((nz,)),
            pltpu.SemaphoreType.REGULAR((2,)),
        ],
        compiler_params=pltpu.CompilerParams(
            collective_id=0, has_side_effects=True, vmem_limit_bytes=60 << 20
        ),
    )(
        patch_order,
        patch_start,
        patches.reshape(rows, feat),
        cache_k[0],
        cache_v[0],
        jnp.transpose(w_qkv[0], (1, 0, 2)),
        w_out[0],
        jnp.transpose(modulation, (1, 0, 2)),
        qk_gain[0],
    )
    out, new_k, new_v = written(out, new_k, new_v)
    return (out.reshape(1, count, tok, feat), new_k[None], new_v[None])


def solution(mesh):
    return jax.shard_map(
        per_device,
        mesh=mesh,
        in_specs=(
            P(None, "seq", "head"),
            P("section", "seq", "head"),
            P("section", "seq", "head"),
            P("section", "seq", None, "head"),
            P("section", None, "head"),
            P("section", None, None),
            P("section", None, None),
            P(),
            P(),
        ),
        out_specs=(
            P("section", None, "seq", "head"),
            P("section", "seq", "head"),
            P("section", "seq", "head"),
        ),
        check_vma=False,
    )
```

```python
import functools
import math

import jax
import jax.numpy as jnp
from jax import lax
from jax.experimental import pallas as pl
from jax.experimental.pallas import tpu as pltpu
from jax.sharding import PartitionSpec as P

MESH = pl.DeviceIdType.MESH
F32 = jnp.float32
BF16 = jnp.bfloat16
FAR = -1e30


def square_side(count):
    side = math.isqrt(count)
    assert side * side == count
    return side


def block_kernel(
    nz,
    ny,
    nx,
    patches,
    tok,
    head_dim,
    order_h,
    start_h,
    x_in,
    ck,
    cv,
    w,
    wo,
    mod_h,
    gain_h,
    bo,
    nk,
    nv,
    order,
    start,
    mod,
    gain,
    own,
    xr,
    xe,
    xg,
    xn,
    st_send,
    st_recv,
    st_norm,
    st_all,
    wbuf,
    wo_v,
    psend,
    precv,
    qg,
    kall,
    vall,
    bias,
    tag,
    nsend,
    nrecv,
    ag,
    rsend,
    rrecv,
    loc,
    x_s,
    x_r,
    st_s,
    st_r,
    sn_s,
    sn_r,
    h_s,
    h_r,
    w_s,
    w_r,
    wa_s,
    wa_r,
    wb_s,
    wb_r,
    wc_s,
    wc_r,
    wd_s,
    wd_r,
    c_s,
    c_r,
    p_s,
    p_r,
    q_s,
    q_r,
    kv_s,
    kv_r,
    n_s,
    n_r,
    ag_s,
    ag_r,
    r_s,
    r_r,
    go,
):
    sec = lax.axis_index("section")
    z = lax.axis_index("head")
    seq = lax.axis_index("seq")
    y = seq // nx
    x = lax.rem(seq, nx)
    rows, feat = own.shape
    chunk = ck.shape[0]
    heads = feat // head_dim
    width = nz * feat
    w_rows = w.shape[1]
    hz = nz // ny
    hy = z // hz
    fresh = ny * rows
    span = ny * chunk
    pad = rrecv.shape[2]

    def on_z(d):
        return (sec, lax.rem(z + d, nz), seq)

    def on_y(d):
        return (sec, z, lax.rem(y + d, ny) * nx + x)

    def on_x(d):
        return (sec, z, y * nx + lax.rem(x + d, nx))

    other = (1 - sec, z, seq)

    def z_at(d):
        return lax.rem(z + d, nz)

    def y_at(d):
        return lax.rem(y + d, ny)

    def x_at(d):
        return lax.rem(x + d, nx)

    def copy(src, dst, ss, rs, dev):
        return pltpu.make_async_remote_copy(
            src_ref=src, dst_ref=dst, send_sem=ss, recv_sem=rs, device_id=dev, device_id_type=MESH
        )

    def arrived(dst, rs):
        copy(dst, dst, rs, rs, other).wait_recv()

    w_slot = wbuf.at[:, y, x]
    my_cache = pl.ds(pl.multiple_of(fresh + y * chunk, chunk), chunk)
    own_x = pltpu.make_async_copy(x_in, own, loc.at[0])
    own_w = pltpu.make_async_copy(w, w_slot, loc.at[1])
    own_cache = [
        pltpu.make_async_copy(ck, kall.at[my_cache, :], loc.at[2]),
        pltpu.make_async_copy(cv, vall.at[my_cache, :], loc.at[3]),
    ]
    own_places = [
        pltpu.make_async_copy(order_h, order, loc.at[4]),
        pltpu.make_async_copy(start_h, start, loc.at[5]),
    ]
    own_scales = [
        pltpu.make_async_copy(mod_h, mod, loc.at[6]),
        pltpu.make_async_copy(gain_h, gain, loc.at[7]),
    ]
    own_wo = pltpu.make_async_copy(wo, wo_v, loc.at[8])

    slot = xr.at[y, lax.rem(z, hz)]
    slot_r = x_r.at[y, lax.rem(z, hz)]

    first_x = [
        copy(own, slot, x_s.at[d], slot_r, (0, z_at(d), hy * nx + x)) for d in range(nz)
    ]
    first_st = [
        copy(st_send, st_recv.at[z], st_s.at[d], st_r.at[z], on_z(d)) for d in range(1, nz)
    ]
    next_x = [
        copy(bo, xg.at[z], h_s.at[d], h_r.at[z], (1, z_at(d), seq)) for d in range(nz)
    ]
    sn_copies = [
        copy(st_norm, st_all.at[y], sn_s.at[d], sn_r.at[y], on_y(d)) for d in range(1, ny)
    ]
    w_copies = [copy(w_slot, w_slot, w_s.at[d], w_r.at[x], on_x(d)) for d in range(1, nx)]
    half = w_rows // 2
    upper, lower = pl.ds(0, half), pl.ds(half, half)

    def w_gather(view, ss, rs, at, to, count):
        return [copy(view, view, ss.at[d], rs.at[at], to(d)) for d in range(1, count)]

    wa_copies = w_gather(wbuf.at[:, y, x, upper], wa_s, wa_r, x, on_x, nx)
    wb_copies = w_gather(wbuf.at[:, y, x, lower], wb_s, wb_r, y, on_y, ny)
    wc_copies = [
        w_gather(wbuf.at[i, y, :, upper], wc_s.at[i], wc_r.at[i], y, on_y, ny) for i in range(3)
    ]
    wd_copies = [
        w_gather(wbuf.at[i, :, x, lower], wd_s.at[i], wd_r.at[i], x, on_x, nx) for i in range(3)
    ]
    cache_copies = [
        copy(ref.at[my_cache, :], ref.at[my_cache, :], c_s.at[i, d], c_r.at[i, y], on_y(d))
        for d in range(1, ny)
        for i, ref in enumerate((kall, vall))
    ]
    p_copies = [
        [
            copy(psend.at[i, y_at(d)], precv.at[i, y], p_s.at[i, d], p_r.at[i, y], on_y(d))
            for d in range(1, ny)
        ]
        for i in range(3)
    ]
    q_copies = [copy(qg.at[x], qg.at[x], q_s.at[d], q_r.at[x], on_x(d)) for d in range(1, nx)]
    my_fresh = pl.ds(pl.multiple_of(y * rows, rows), rows)
    kv_copies = [
        [
            copy(
                ref.at[my_fresh, :], ref.at[my_fresh, :], kv_s.at[i, d], kv_r.at[i, y], on_y(d)
            )
            for d in range(1, ny)
        ]
        for i, ref in enumerate((kall, vall))
    ]
    num_copies = [
        [
            copy(nsend.at[h, x_at(d)], nrecv.at[h, x], n_s.at[h, d], n_r.at[h, x], on_x(d))
            for d in range(1, nx)
        ]
        for h in range(heads)
    ]
    a_copies = [
        [
            copy(ag.at[h, z], ag.at[h, z], ag_s.at[h, d], ag_r.at[h, z], on_z(d))
            for d in range(1, nz)
        ]
        for h in range(heads)
    ]
    r_copies = [
        copy(rsend.at[i, x_at(d)], rrecv.at[i, x], r_s.at[i, d], r_r.at[i, x], on_x(d))
        for d in range(1, nx)
        for i in range(2)
    ]

    @pl.when(sec == 0)
    def _():
        own_x.start()

    for c in [own_w] + own_places + own_scales + own_cache + [own_wo]:
        c.start()

    barrier = pltpu.get_barrier_semaphore()

    def greet(dev):
        pl.semaphore_signal(barrier, inc=1, device_id=dev, device_id_type=MESH)

    partners = (
        [on_z(d) for d in range(1, nz)]
        + [on_y(d) for d in range(1, ny)]
        + [on_x(d) for d in range(1, nx)]
    )
    for dev in partners:
        greet(dev)

    def is_own(i, b):
        return (y == i) & (z == y * hz + b)

    @pl.when(sec == 0)
    def _():
        for i in range(ny):
            for b in range(hz):

                @pl.when(jnp.logical_not(is_own(i, b)))
                def _():
                    greet((0, y * hz + b, i * nx + x))

    @pl.when(sec == 1)
    def _():
        for d in range(nz):
            greet((0, z_at(d), seq))

    lane_rows = lax.broadcasted_iota(jnp.int32, (rows, head_dim), 1)

    def shard_stats(value):
        value = value.astype(F32)
        middle = jnp.sum(value, axis=-1, keepdims=True) * (1.0 / feat)
        value = value - middle
        square = jnp.sum(value * value, axis=-1, keepdims=True)
        both = jnp.where(lane_rows == 0, middle, jnp.where(lane_rows == 1, square, 0.0))
        both = jnp.concatenate([both, jnp.zeros((head_dim - rows, head_dim), F32)], axis=0)
        st_send[...] = jnp.transpose(both)[0:8, :]

    @pl.when(sec == 0)
    def _():
        own_x.wait()
        shard_stats(own[...])
        st_recv[z] = st_send[...]
        pl.semaphore_wait(barrier, len(partners) + 2 * nz - jnp.where(hy == y, 1, 0))
        for c in first_st + first_x[1:]:
            c.start()

        @pl.when(hy == y)
        def _():
            slot[...] = own[...]

        @pl.when(hy != y)
        def _():
            first_x[0].start()

    own_w.wait()
    for c in own_cache:
        c.wait()

    @pl.when(sec == 0)
    def _():
        for c in w_copies + cache_copies:
            c.start()

    @pl.when(sec == 1)
    def _():
        pl.semaphore_wait(barrier, len(partners))
        for c in wb_copies:
            c.start()
        pl.semaphore_wait(go.at[0], 1)
        for c in wa_copies:
            c.start()
        for d in range(1, ny):
            arrived(wbuf.at[:, y_at(d), x, lower], wb_r.at[y_at(d)])
        for d in range(1, nx):
            arrived(wbuf.at[:, y, x_at(d), upper], wa_r.at[x_at(d)])
        for c in wd_copies[1] + wd_copies[0]:
            c.start()
        pl.semaphore_wait(go.at[1], 1)
        for c in wc_copies[1] + wc_copies[0] + cache_copies + wc_copies[2]:
            c.start()
        pl.semaphore_wait(go.at[2], 1)
        for c in wd_copies[2]:
            c.start()

    for c in own_places:
        c.wait()
    places = [order[i] for i in range(patches)]
    begins = [start[i] for i in range(patches)]
    steps = [
        sum(jnp.where(places[s] == p, s, 0) for s in range(patches)) for p in range(patches)
    ]

    def first_after(step, pos):
        found = patches
        for p in range(patches):
            hit = (steps[p] > step) & (begins[p] <= pos) & (pos < begins[p] + span)
            found = jnp.where(hit, jnp.minimum(found, steps[p]), found)
        return found

    lane = lax.broadcasted_iota(jnp.int32, (tok, head_dim), 1)
    lane_chunk = lax.broadcasted_iota(jnp.int32, (chunk, head_dim), 1)
    for j in range(ny):
        parts = []
        for p in range(patches):
            upto = first_after(steps[p], begins[p] + j * chunk)
            parts.append(jnp.where((lane >= steps[p]) & (lane < upto), 0.0, FAR))
        bias[j * rows : (j + 1) * rows, :] = jnp.concatenate(parts, axis=0).astype(BF16)
        upto = first_after(-1, (j * nx + x) * chunk)
        bias[fresh + j * chunk : fresh + (j + 1) * chunk, :] = jnp.where(
            lane_chunk < upto, 0.0, FAR
        ).astype(BF16)
    tag[...] = jnp.concatenate(
        [jnp.where(lane == steps[p], 1.0, 0.0) for p in range(patches)], axis=0
    ).astype(BF16)

    for c in own_scales:
        c.wait()

    def rms_heads(value, which):
        out = []
        for h in range(heads):
            part = value[:, h * head_dim : (h + 1) * head_dim]
            power = jnp.sum(part * part, axis=-1, keepdims=True) * (1.0 / head_dim)
            out.append(part * lax.rsqrt(power + 1e-06) * gain[which : which + 1, :])
        return jnp.concatenate(out, axis=-1).astype(BF16)

    def spread_part(i, value):
        if i == 0:
            qg[x] = rms_heads(value, 0)
            copies = q_copies
        elif i == 1:
            kall[my_fresh, :] = rms_heads(value, 1)
            copies = kv_copies[0]
        else:
            vall[my_fresh, :] = value.astype(BF16)
            copies = kv_copies[1]
        for c in copies:
            c.start()

    @pl.when(sec == 0)
    def _():
        for d in range(1, nz):
            arrived(st_recv.at[z_at(d)], st_r.at[z_at(d)])
        middles = [st_recv[i, 0:1, :] for i in range(nz)]
        mean = sum(middles) * (1.0 / nz)
        square = sum(st_recv[i, 1:2, :] for i in range(nz))
        square += sum((m - mean) * (m - mean) for m in middles) * feat
        scale = lax.rsqrt(square * (1.0 / width) + 1e-06)
        line = lax.broadcasted_iota(jnp.int32, (8, head_dim), 0)
        value = jnp.where(line == 0, mean, jnp.where(line == 1, scale, 0.0))
        st_norm[...] = value
        st_all[y] = value
        for c in sn_copies:
            c.start()
        for d in range(1, ny):
            arrived(st_all.at[y_at(d)], sn_r.at[y_at(d)])
        value = st_all[...].reshape(8 * ny, head_dim)
        value = jnp.concatenate([value, jnp.zeros((head_dim - 8 * ny, head_dim), F32)], axis=0)
        stats = jnp.transpose(value)[0:rows, :]
        for d in range(1, nx):
            arrived(wbuf.at[:, y, x_at(d)], w_r.at[x_at(d)])
        pl.semaphore_signal(go.at[0], inc=1, device_id=other, device_id_type=MESH)
        for i in range(ny):
            for b in range(hz):

                @pl.when(jnp.logical_not(is_own(i, b)))
                def _():
                    arrived(xr.at[i, b], x_r.at[i, b])

                at = pl.ds(pl.multiple_of((y * hz + b) * feat, feat), feat)
                value = xr[i, b].astype(F32) - stats[:, 8 * i : 8 * i + 1]
                value = value * stats[:, 8 * i + 1 : 8 * i + 2]
                value = value * (1.0 + mod[1, :, at]) + mod[0, :, at]
                xe[i, :, b * feat : (b + 1) * feat] = value.astype(BF16)

        tokens = xe[...].reshape(ny * rows, hz * feat)
        for i in (1, 0, 2):
            weights = wbuf[i, y].reshape(nx * w_rows, feat)
            value = jnp.dot(tokens, weights, preferred_element_type=F32)
            psend[i] = value.astype(BF16).reshape(ny, rows, feat)
            for c in p_copies[i]:
                c.start()
        for i in (1, 0, 2):
            value = psend[i, y].astype(F32)
            for d in range(1, ny):
                arrived(precv.at[i, y_at(d)], p_r.at[i, y_at(d)])
                value += precv[i, y_at(d)].astype(F32)
            spread_part(i, value)

    @pl.when(sec == 1)
    def _():
        for i in range(nz):
            arrived(xg.at[i], h_r.at[i])
        own[...] = xg[z]
        total = jnp.zeros((rows, feat), F32)
        for i in range(nz):
            total += xg[i].astype(F32)
        mean = jnp.sum(total, axis=-1, keepdims=True) * (1.0 / width)
        total = jnp.zeros((rows, feat), F32)
        for i in range(nz):
            diff = xg[i].astype(F32) - mean
            total += diff * diff
        scale = lax.rsqrt(jnp.sum(total, axis=-1, keepdims=True) * (1.0 / width) + 1e-06)
        for i in range(nz):
            at = slice(i * feat, (i + 1) * feat)
            value = (xg[i].astype(F32) - mean) * scale * (1.0 + mod[1, :, at]) + mod[0, :, at]
            xn[:, at] = value.astype(BF16)
        for i in (1, 0, 2):
            for d in range(1, ny):
                arrived(wbuf.at[i, y_at(d), :, upper], wc_r.at[i, y_at(d)])
            for d in range(1, nx):
                arrived(wbuf.at[i, :, x_at(d), lower], wd_r.at[i, x_at(d)])
            weights = wbuf[i].reshape(width, feat)
            spread_part(i, jnp.dot(xn[...], weights, preferred_element_type=F32))

    for i, ref in enumerate((kall, vall)):
        for d in range(1, ny):
            at = pl.ds(pl.multiple_of(fresh + y_at(d) * chunk, chunk), chunk)
            arrived(ref.at[at, :], c_r.at[i, y_at(d)])
    for i, ref in enumerate((kall, vall)):
        for d in range(1, ny):
            at = pl.ds(pl.multiple_of(y_at(d) * rows, rows), rows)
            arrived(ref.at[at, :], kv_r.at[i, y_at(d)])
    for d in range(1, nx):
        arrived(qg.at[x_at(d)], q_r.at[x_at(d)])

    @pl.when(sec == 0)
    def _():
        pl.semaphore_signal(go.at[1], inc=1, device_id=other, device_id_type=MESH)

    tags = jnp.concatenate([tag[...]] * nx, axis=0)
    lane_all = lax.broadcasted_iota(jnp.int32, (nx * rows, head_dim), 1)
    exponent = math.log2(math.e) / math.sqrt(head_dim)
    for h in range(heads):
        at = slice(h * head_dim, (h + 1) * head_dim)
        queries = jnp.concatenate([qg[:, :, at].reshape(nx * rows, head_dim), tags], axis=1)
        keys = jnp.concatenate([kall[:, at], bias[...]], axis=1)
        scores = lax.dot_general(
            queries, keys, (((1,), (1,)), ((), ())), preferred_element_type=F32
        )
        weight = jnp.exp2(scores * exponent)
        denom = jnp.sum(weight, axis=-1, keepdims=True)
        numer = jnp.dot(weight.astype(BF16), vall[:, at], preferred_element_type=F32)
        nsend[h, :, :, 0:head_dim] = numer.astype(BF16).reshape(nx, rows, head_dim)
        high = denom.astype(BF16).astype(F32)
        sums = jnp.where(lane_all == 0, high, denom - high)
        nsend[h, :, :, head_dim:] = sums.astype(BF16).reshape(nx, rows, head_dim)
        for c in num_copies[h]:
            c.start()

    for h in range(heads):
        total = nsend[h, x].astype(F32)
        for d in range(1, nx):
            arrived(nrecv.at[h, x_at(d)], n_r.at[h, x_at(d)])
            total += nrecv[h, x_at(d)].astype(F32)
        denom = total[:, head_dim : head_dim + 1] + total[:, head_dim + 1 : head_dim + 2]
        ag[h, z] = (total[:, 0:head_dim] / denom).astype(BF16)
        for c in a_copies[h]:
            c.start()

    @pl.when(sec == 0)
    def _():
        pl.semaphore_signal(go.at[2], inc=1, device_id=other, device_id_type=MESH)

    def source(c):
        pos = c * chunk
        last = -1
        first_row = -fresh - pad
        for p in range(patches):
            hit = (begins[p] <= pos) & (pos < begins[p] + span) & (steps[p] > last)
            last = jnp.where(hit, steps[p], last)
            row = (pos - begins[p]) // chunk * rows + p * tok
            first_row = jnp.where(hit, row, first_row)
        return first_row, last

    in_row = lax.broadcasted_iota(jnp.int32, (pad, fresh), 0)
    in_col = lax.broadcasted_iota(jnp.int32, (pad, fresh), 1)
    picks = []
    for c in range(nx):
        first_row, _ = source(y * nx + c)
        hit = (in_col - in_row == first_row) & (in_row < tok)
        picks.append(jnp.where(hit, 1.0, 0.0).astype(BF16))
    pick = jnp.concatenate(picks, axis=0)
    for i, ref in enumerate((kall, vall)):
        value = jnp.dot(pick, ref[0:fresh, :], preferred_element_type=F32)
        rsend[i] = value.astype(BF16).reshape(nx, pad, feat)
    for c in r_copies:
        c.start()

    own_wo.wait()
    result = jnp.zeros((rows, feat), F32)
    for h in range(heads):
        for d in range(1, nz):
            arrived(ag.at[h, z_at(d)], ag_r.at[h, z_at(d)])
        attended = jnp.concatenate([ag[h, i] for i in range(nz)], axis=1)
        weights = wo_v[:, h].reshape(nz * head_dim, feat)
        result += jnp.dot(attended, weights, preferred_element_type=F32)
    gate = mod[2, :, pl.ds(pl.multiple_of(z * feat, feat), feat)]
    bo[...] = (own[...].astype(F32) + gate * result).astype(BF16)

    @pl.when(sec == 0)
    def _():
        for c in next_x:
            c.start()

    for i in range(2):
        for d in range(1, nx):
            arrived(rrecv.at[i, x_at(d)], r_r.at[i, x_at(d)])
        rrecv[i, x] = rsend[i, x]
    out_row = lax.broadcasted_iota(jnp.int32, (chunk, nx * pad), 0)
    out_col = lax.broadcasted_iota(jnp.int32, (chunk, nx * pad), 1)
    block = out_col // pad
    within = out_col - block * pad
    hit = (out_row == block * tok + within) & (within < tok)
    place = jnp.where(hit, 1.0, 0.0).astype(BF16)
    _, last = source(seq)
    for i, (old, new) in enumerate(((kall, nk), (vall, nv))):
        value = jnp.dot(place, rrecv[i].reshape(nx * pad, feat), preferred_element_type=F32)
        new[...] = jnp.where(last >= 0, value, old[my_cache, :].astype(F32)).astype(BF16)

    @pl.when(sec == 0)
    def _():
        for c in next_x + first_st + first_x[1:] + sn_copies + w_copies + sum(p_copies, []):
            c.wait_send()

        @pl.when(hy != y)
        def _():
            first_x[0].wait_send()

    @pl.when(sec == 1)
    def _():
        for c in wa_copies + wb_copies + sum(wc_copies + wd_copies, []):
            c.wait_send()

    for c in cache_copies + q_copies + r_copies + sum(kv_copies + num_copies + a_copies, []):
        c.wait_send()


def write_kernel(*refs):
    half = len(refs) // 2
    for src, dst in zip(refs[:half], refs[half:]):
        dst[...] = src[...]


def written(*arrays):
    vmem = pl.BlockSpec(memory_space=pltpu.VMEM)
    return pl.pallas_call(
        write_kernel,
        name="write",
        out_shape=tuple(jax.ShapeDtypeStruct(a.shape, a.dtype) for a in arrays),
        in_specs=[vmem] * len(arrays),
        out_specs=(vmem,) * len(arrays),
        compiler_params=pltpu.CompilerParams(vmem_limit_bytes=60 << 20),
    )(*arrays)


def per_device(
    patches, cache_k, cache_v, w_qkv, w_out, modulation, qk_gain, patch_order, patch_start
):
    nz = lax.axis_size("head")
    ny = nx = square_side(lax.axis_size("seq"))
    count, tok, feat = patches.shape
    chunk = cache_k.shape[1]
    head_dim = qk_gain.shape[-1]
    rows = count * tok
    hz = nz // ny
    heads = feat // head_dim
    w_rows = w_qkv.shape[1]
    pad = -(-tok // 16) * 16
    keys = ny * (rows + chunk)
    dma = pltpu.SemaphoreType.DMA
    vmem = pl.BlockSpec(memory_space=pltpu.VMEM)
    hbm = pl.BlockSpec(memory_space=pl.ANY)
    out, new_k, new_v = pl.pallas_call(
        functools.partial(block_kernel, nz, ny, nx, count, tok, head_dim),
        name="blocks",
        out_shape=(
            jax.ShapeDtypeStruct((rows, feat), BF16),
            jax.ShapeDtypeStruct((chunk, feat), BF16),
            jax.ShapeDtypeStruct((chunk, feat), BF16),
        ),
        in_specs=[hbm] * 9,
        out_specs=(vmem, vmem, vmem),
        scratch_shapes=[
            pltpu.SMEM((count,), jnp.int32),
            pltpu.SMEM((count,), jnp.int32),
            pltpu.VMEM((3, 1, nz * feat), F32),
            pltpu.VMEM((2, head_dim), F32),
            pltpu.VMEM((rows, feat), BF16),
            pltpu.VMEM((ny, hz, rows, feat), BF16),
            pltpu.VMEM((ny, rows, hz * feat), BF16),
            pltpu.VMEM((nz, rows, feat), BF16),
            pltpu.VMEM((rows, nz * feat), BF16),
            pltpu.VMEM((8, head_dim), F32),
            pltpu.VMEM((nz, 8, head_dim), F32),
            pltpu.VMEM((8, head_dim), F32),
            pltpu.VMEM((ny, 8, head_dim), F32),
            pltpu.VMEM((3, ny, nx, w_rows, feat), BF16),
            pltpu.VMEM((nz, heads, head_dim, feat), BF16),
            pltpu.VMEM((3, ny, rows, feat), BF16),
            pltpu.VMEM((3, ny, rows, feat), BF16),
            pltpu.VMEM((nx, rows, feat), BF16),
            pltpu.VMEM((keys, feat), BF16),
            pltpu.VMEM((keys, feat), BF16),
            pltpu.VMEM((keys, head_dim), BF16),
            pltpu.VMEM((rows, head_dim), BF16),
            pltpu.VMEM((heads, nx, rows, 2 * head_dim), BF16),
            pltpu.VMEM((heads, nx, rows, 2 * head_dim), BF16),
            pltpu.VMEM((heads, nz, rows, head_dim), BF16),
            pltpu.VMEM((2, nx, pad, feat), BF16),
            pltpu.VMEM((2, nx, pad, feat), BF16),
            dma((9,)),
            dma((nz,)),
            dma((ny, hz)),
            dma((nz,)),
            dma((nz,)),
            dma((ny,)),
            dma((ny,)),
            dma((nz,)),
            dma((nz,)),
            dma((nx,)),
            dma((nx,)),
            dma((nx,)),
            dma((nx,)),
            dma((ny,)),
            dma((ny,)),
            dma((3, ny)),
            dma((3, ny)),
            dma((3, nx)),
            dma((3, nx)),
            dma((2, ny)),
            dma((2, ny)),
            dma((3, ny)),
            dma((3, ny)),
            dma((nx,)),
            dma((nx,)),
            dma((2, ny)),
            dma((2, ny)),
            dma((heads, nx)),
            dma((heads, nx)),
            dma((heads, nz)),
            dma((heads, nz)),
            dma((2, nx)),
            dma((2, nx)),
            pltpu.SemaphoreType.REGULAR((3,)),
        ],
        compiler_params=pltpu.CompilerParams(
            collective_id=0, has_side_effects=True, vmem_limit_bytes=60 << 20
        ),
    )(
        patch_order,
        patch_start,
        patches.reshape(rows, feat),
        cache_k[0],
        cache_v[0],
        jnp.transpose(w_qkv[0], (1, 0, 2)),
        w_out[0].reshape(nz, feat // head_dim, head_dim, feat),
        jnp.transpose(modulation, (1, 0, 2)),
        qk_gain[0],
    )
    out, new_k, new_v = written(out, new_k, new_v)
    return (out.reshape(1, count, tok, feat), new_k[None], new_v[None])


def solution(mesh):
    return jax.shard_map(
        per_device,
        mesh=mesh,
        in_specs=(
            P(None, "seq", "head"),
            P("section", "seq", "head"),
            P("section", "seq", "head"),
            P("section", "seq", None, "head"),
            P("section", None, "head"),
            P("section", None, None),
            P("section", None, None),
            P(),
            P(),
        ),
        out_specs=(
            P("section", None, "seq", "head"),
            P("section", "seq", "head"),
            P("section", "seq", "head"),
        ),
        check_vma=False,
    )
```

```python
import functools
import math

import jax
import jax.numpy as jnp
from jax import lax
from jax.experimental import pallas as pl
from jax.experimental.pallas import tpu as pltpu
from jax.sharding import PartitionSpec as P

MESH = pl.DeviceIdType.MESH
F32 = jnp.float32
BF16 = jnp.bfloat16
FAR = -1e30


def square_side(count):
    side = math.isqrt(count)
    assert side * side == count
    return side


def block_kernel(
    nz,
    ny,
    nx,
    tok,
    waves,
    per_wave,
    head_dim,
    order_h,
    start_h,
    x_in,
    ck,
    cv,
    w,
    wo,
    mod_h,
    gain_h,
    bo,
    nk,
    nv,
    order,
    start,
    mod,
    gain,
    x_rows,
    own,
    done,
    xr,
    xe,
    xg,
    xn,
    st_send,
    st_recv,
    st_norm,
    st_all,
    wbuf,
    wo_v,
    psend,
    precv,
    qg,
    kv,
    bias,
    nsend,
    nrecv,
    ag,
    rsend,
    rrecv,
    loc,
    x_s,
    x_r,
    st_s,
    st_r,
    sn_s,
    sn_r,
    h_s,
    h_r,
    w_s,
    w_r,
    wa_s,
    wa_r,
    wb_s,
    wb_r,
    wc_s,
    wc_r,
    wd_s,
    wd_r,
    c_s,
    c_r,
    p_s,
    p_r,
    q_s,
    q_r,
    kv_s,
    kv_r,
    n_s,
    n_r,
    ag_s,
    ag_r,
    r_s,
    r_r,
    go,
):
    sec = lax.axis_index("section")
    z = lax.axis_index("head")
    seq = lax.axis_index("seq")
    y = seq // nx
    x = lax.rem(seq, nx)
    _, rows, feat = own.shape
    chunk = ck.shape[0]
    heads = feat // head_dim
    width = nz * feat
    w_rows = w.shape[1]
    hz = nz // ny
    hy = z // hz
    steps = waves * per_wave
    stale = ny * chunk
    fresh = ny * rows
    span = ny * chunk
    pad = rrecv.shape[1]

    def z_at(d):
        return lax.rem(z + d, nz)

    def y_at(d):
        return lax.rem(y + d, ny)

    def x_at(d):
        return lax.rem(x + d, nx)

    def on_z(d):
        return (sec, z_at(d), seq)

    def on_y(d):
        return (sec, z, y_at(d) * nx + x)

    def on_x(d):
        return (sec, z, y * nx + x_at(d))

    other = (1 - sec, z, seq)

    def copy(src, dst, ss, rs, dev):
        return pltpu.make_async_remote_copy(
            src_ref=src, dst_ref=dst, send_sem=ss, recv_sem=rs, device_id=dev, device_id_type=MESH
        )

    def arrived(dst, rs):
        copy(dst, dst, rs, rs, other).wait_recv()

    def cached(i):
        return pl.ds(pl.multiple_of(i * chunk, chunk), chunk)

    def freshly(v, i):
        return pl.ds(pl.multiple_of(stale + v * fresh + i * rows, rows), rows)

    w_slot = wbuf.at[:, y, x]
    own_x = pltpu.make_async_copy(x_in, x_rows, loc.at[0])
    own_w = pltpu.make_async_copy(w, w_slot, loc.at[1])
    own_cache = [
        pltpu.make_async_copy(ck, kv.at[cached(y), 0:feat], loc.at[2]),
        pltpu.make_async_copy(cv, kv.at[cached(y), feat : 2 * feat], loc.at[3]),
    ]
    own_places = [
        pltpu.make_async_copy(order_h, order, loc.at[4]),
        pltpu.make_async_copy(start_h, start, loc.at[5]),
    ]
    own_scales = [
        pltpu.make_async_copy(mod_h, mod, loc.at[6]),
        pltpu.make_async_copy(gain_h, gain, loc.at[7]),
    ]
    own_wo = pltpu.make_async_copy(wo, wo_v, loc.at[8])

    def by_wave(make):
        return [make(v) for v in range(waves)]

    first_x = by_wave(
        lambda v: [
            copy(
                own.at[v],
                xr.at[v, y, lax.rem(z, hz)],
                x_s.at[v, d],
                x_r.at[v, y, lax.rem(z, hz)],
                (0, z_at(d), hy * nx + x),
            )
            for d in range(nz)
        ]
    )
    first_st = [
        copy(st_send, st_recv.at[z], st_s.at[d], st_r.at[z], on_z(d)) for d in range(1, nz)
    ]
    next_x = by_wave(
        lambda v: [
            copy(done.at[v], xg.at[v, z], h_s.at[v, d], h_r.at[v, z], (1, z_at(d), seq))
            for d in range(nz)
        ]
    )
    sn_copies = [
        copy(st_norm, st_all.at[y], sn_s.at[d], sn_r.at[y], on_y(d)) for d in range(1, ny)
    ]
    w_copies = [copy(w_slot, w_slot, w_s.at[d], w_r.at[x], on_x(d)) for d in range(1, nx)]
    half = w_rows // 2
    upper, lower = pl.ds(0, half), pl.ds(half, half)

    def w_gather(view, ss, rs, at, to, count):
        return [copy(view, view, ss.at[d], rs.at[at], to(d)) for d in range(1, count)]

    wa_copies = w_gather(wbuf.at[:, y, x, upper], wa_s, wa_r, x, on_x, nx)
    wb_copies = w_gather(wbuf.at[:, y, x, lower], wb_s, wb_r, y, on_y, ny)
    wc_copies = [
        w_gather(wbuf.at[i, y, :, upper], wc_s.at[i], wc_r.at[i], y, on_y, ny) for i in range(3)
    ]
    wd_copies = [
        w_gather(wbuf.at[i, :, x, lower], wd_s.at[i], wd_r.at[i], x, on_x, nx) for i in range(3)
    ]
    cache_slot = kv.at[cached(y), :]
    cache_copies = [copy(cache_slot, cache_slot, c_s.at[d], c_r.at[y], on_y(d)) for d in range(1, ny)]
    p_copies = by_wave(
        lambda v: [
            copy(psend.at[v, y_at(d)], precv.at[v, y], p_s.at[v, d], p_r.at[v, y], on_y(d))
            for d in range(1, ny)
        ]
    )
    q_copies = by_wave(
        lambda v: [
            copy(qg.at[v, x], qg.at[v, x], q_s.at[v, d], q_r.at[v, x], on_x(d))
            for d in range(1, nx)
        ]
    )
    kv_copies = by_wave(
        lambda v: [
            copy(
                kv.at[freshly(v, y), :],
                kv.at[freshly(v, y), :],
                kv_s.at[v, d],
                kv_r.at[v, y],
                on_y(d),
            )
            for d in range(1, ny)
        ]
    )
    num_copies = by_wave(
        lambda v: [
            copy(nsend.at[v, x_at(d)], nrecv.at[v, x], n_s.at[v, d], n_r.at[v, x], on_x(d))
            for d in range(1, nx)
        ]
    )
    a_copies = by_wave(
        lambda v: [
            copy(ag.at[v, z], ag.at[v, z], ag_s.at[v, d], ag_r.at[v, z], on_z(d))
            for d in range(1, nz)
        ]
    )
    r_copies = [
        copy(rsend.at[x_at(d)], rrecv.at[x], r_s.at[d], r_r.at[x], on_x(d)) for d in range(1, nx)
    ]

    @pl.when(sec == 0)
    def _():
        own_x.start()

    for c in own_places + [own_w] + own_cache + own_scales + [own_wo]:
        c.start()

    barrier = pltpu.get_barrier_semaphore()

    def greet(dev):
        pl.semaphore_signal(barrier, inc=1, device_id=dev, device_id_type=MESH)

    partners = (
        [on_z(d) for d in range(1, nz)]
        + [on_y(d) for d in range(1, ny)]
        + [on_x(d) for d in range(1, nx)]
    )
    for dev in partners:
        greet(dev)

    def is_own(i, b):
        return (y == i) & (z == y * hz + b)

    @pl.when(sec == 0)
    def _():
        for i in range(ny):
            for b in range(hz):

                @pl.when(jnp.logical_not(is_own(i, b)))
                def _():
                    greet((0, y * hz + b, i * nx + x))

    @pl.when(sec == 1)
    def _():
        for d in range(nz):
            greet((0, z_at(d), seq))

    for c in own_places:
        c.wait()
    places = [order[s] for s in range(steps)]
    begins = [sum(jnp.where(places[s] == p, start[p], 0) for p in range(steps)) for s in range(steps)]

    lane_rows = lax.broadcasted_iota(jnp.int32, (steps * tok, head_dim), 1)

    def shard_stats(value):
        middle = jnp.sum(value, axis=-1, keepdims=True) * (1.0 / feat)
        value = value - middle
        square = jnp.sum(value * value, axis=-1, keepdims=True)
        both = jnp.where(lane_rows == 0, middle, jnp.where(lane_rows == 1, square, 0.0))
        both = jnp.concatenate([both, jnp.zeros((head_dim - steps * tok, head_dim), F32)], axis=0)
        st_send[...] = jnp.transpose(both)[0:8, :]

    @pl.when(sec == 0)
    def _():
        own_x.wait()
        value = x_rows[...].astype(F32)
        parts = [value[p * tok : (p + 1) * tok] for p in range(steps)]
        value = []
        for s in range(steps):
            chosen = parts[0]
            for p in range(1, steps):
                chosen = jnp.where(places[s] == p, parts[p], chosen)
            value.append(chosen)
        value = jnp.concatenate(value, axis=0)
        own[...] = value.astype(BF16).reshape(waves, rows, feat)
        shard_stats(value)
        st_recv[z] = st_send[...]
        pl.semaphore_wait(barrier, len(partners) + 2 * nz - jnp.where(hy == y, 1, 0))
        for c in first_st:
            c.start()
        for v in range(waves):
            for c in first_x[v][1:]:
                c.start()

            @pl.when(hy == y)
            def _():
                xr[v, y, lax.rem(z, hz)] = own[v]

            @pl.when(hy != y)
            def _():
                first_x[v][0].start()

    own_w.wait()
    for c in own_cache:
        c.wait()

    @pl.when(sec == 0)
    def _():
        for c in w_copies + cache_copies:
            c.start()

    @pl.when(sec == 1)
    def _():
        pl.semaphore_wait(barrier, len(partners))
        for c in wb_copies:
            c.start()
        pl.semaphore_wait(go.at[0], 1)
        for c in wa_copies:
            c.start()
        for d in range(1, ny):
            arrived(wbuf.at[:, y_at(d), x, lower], wb_r.at[y_at(d)])
        for c in wd_copies[1]:
            c.start()
        for d in range(1, nx):
            arrived(wbuf.at[:, y, x_at(d), upper], wa_r.at[x_at(d)])
        for c in wd_copies[0]:
            c.start()
        pl.semaphore_wait(go.at[1], 1)
        for c in wc_copies[1] + wc_copies[0] + wc_copies[2] + wd_copies[2] + cache_copies:
            c.start()
        pl.semaphore_wait(go.at[2], 1)

    def covers(s, pos):
        return (begins[s] <= pos) & (pos < begins[s] + span)

    def first_from(step, pos):
        found = steps
        for s in reversed(range(step, steps)):
            found = jnp.where(covers(s, pos), s, found)
        return found

    lane = lax.broadcasted_iota(jnp.int32, (tok, head_dim), 1)
    lane_chunk = lax.broadcasted_iota(jnp.int32, (chunk, head_dim), 1)
    for j in range(ny):
        upto = first_from(0, (j * nx + x) * chunk)
        value = jnp.where(lane_chunk < upto, 0.0, FAR)
        bias[j * chunk : (j + 1) * chunk, :] = value.astype(BF16)
        for v in range(waves):
            parts = []
            for s in range(v * per_wave, (v + 1) * per_wave):
                upto = first_from(s + 1, begins[s] + j * chunk)
                parts.append(jnp.where((lane >= s) & (lane < upto), 0.0, FAR))
            at = stale + v * fresh + j * rows
            bias[at : at + rows, :] = jnp.concatenate(parts, axis=0).astype(BF16)

    for c in own_scales:
        c.wait()

    def rms_heads(value, which):
        out = []
        for h in range(heads):
            part = value[:, h * head_dim : (h + 1) * head_dim]
            power = jnp.sum(part * part, axis=-1, keepdims=True) * (1.0 / head_dim)
            out.append(part * lax.rsqrt(power + 1e-06) * gain[which : which + 1, :])
        return jnp.concatenate(out, axis=-1).astype(BF16)

    def spread_out(v, query, key, value):
        kv[freshly(v, y), 0:feat] = rms_heads(key, 1)
        kv[freshly(v, y), feat : 2 * feat] = value.astype(BF16)
        for c in kv_copies[v]:
            c.start()
        qg[v, x] = rms_heads(query, 0)
        for c in q_copies[v]:
            c.start()

    @pl.when(sec == 0)
    def _():
        for d in range(1, nz):
            arrived(st_recv.at[z_at(d)], st_r.at[z_at(d)])
        middles = [st_recv[i, 0:1, :] for i in range(nz)]
        mean = sum(middles) * (1.0 / nz)
        square = sum(st_recv[i, 1:2, :] for i in range(nz))
        square += sum((m - mean) * (m - mean) for m in middles) * feat
        scale = lax.rsqrt(square * (1.0 / width) + 1e-06)
        line = lax.broadcasted_iota(jnp.int32, (8, head_dim), 0)
        value = jnp.where(line == 0, mean, jnp.where(line == 1, scale, 0.0))
        st_norm[...] = value
        st_all[y] = value
        for c in sn_copies:
            c.start()
        for d in range(1, ny):
            arrived(st_all.at[y_at(d)], sn_r.at[y_at(d)])
        value = st_all[...].reshape(8 * ny, head_dim)
        value = jnp.concatenate([value, jnp.zeros((head_dim - 8 * ny, head_dim), F32)], axis=0)
        stats = jnp.transpose(value)
        for v in range(waves):
            for i in range(ny):
                mean = stats[v * rows : (v + 1) * rows, 8 * i : 8 * i + 1]
                scale = stats[v * rows : (v + 1) * rows, 8 * i + 1 : 8 * i + 2]
                for b in range(hz):

                    @pl.when(jnp.logical_not(is_own(i, b)))
                    def _():
                        arrived(xr.at[v, i, b], x_r.at[v, i, b])

                    at = pl.ds(pl.multiple_of((y * hz + b) * feat, feat), feat)
                    value = (xr[v, i, b].astype(F32) - mean) * scale
                    value = value * (1.0 + mod[1, :, at]) + mod[0, :, at]
                    xe[v, i, :, b * feat : (b + 1) * feat] = value.astype(BF16)
            if v == 0:
                for d in range(1, nx):
                    arrived(wbuf.at[:, y, x_at(d)], w_r.at[x_at(d)])
                pl.semaphore_signal(go.at[0], inc=1, device_id=other, device_id_type=MESH)
            tokens = xe[v].reshape(ny * rows, hz * feat)
            for i in range(3):
                weights = wbuf[i, y].reshape(nx * w_rows, feat)
                value = jnp.dot(tokens, weights, preferred_element_type=F32)
                psend[v, :, :, i * feat : (i + 1) * feat] = value.astype(BF16).reshape(
                    ny, rows, feat
                )
            for c in p_copies[v]:
                c.start()
        for v in range(waves):
            value = psend[v, y].astype(F32)
            for d in range(1, ny):
                arrived(precv.at[v, y_at(d)], p_r.at[v, y_at(d)])
                value += precv[v, y_at(d)].astype(F32)
            spread_out(v, value[:, 0:feat], value[:, feat : 2 * feat], value[:, 2 * feat :])

    @pl.when(sec == 1)
    def _():
        for v in range(waves):
            for i in range(nz):
                arrived(xg.at[v, i], h_r.at[v, i])
            own[v] = xg[v, z]
            total = jnp.zeros((rows, feat), F32)
            for i in range(nz):
                total += xg[v, i].astype(F32)
            mean = jnp.sum(total, axis=-1, keepdims=True) * (1.0 / width)
            total = jnp.zeros((rows, feat), F32)
            for i in range(nz):
                diff = xg[v, i].astype(F32) - mean
                total += diff * diff
            scale = lax.rsqrt(jnp.sum(total, axis=-1, keepdims=True) * (1.0 / width) + 1e-06)
            for i in range(nz):
                at = slice(i * feat, (i + 1) * feat)
                value = (xg[v, i].astype(F32) - mean) * scale
                value = value * (1.0 + mod[1, :, at]) + mod[0, :, at]
                xn[v, :, at] = value.astype(BF16)
            parts = [None] * 3
            for i in (1, 0, 2):
                if v == 0:
                    for d in range(1, ny):
                        arrived(wbuf.at[i, y_at(d), :, upper], wc_r.at[i, y_at(d)])
                    for d in range(1, nx):
                        arrived(wbuf.at[i, :, x_at(d), lower], wd_r.at[i, x_at(d)])
                weights = wbuf[i].reshape(width, feat)
                parts[i] = jnp.dot(xn[v], weights, preferred_element_type=F32)
            spread_out(v, *parts)

    for d in range(1, ny):
        arrived(kv.at[cached(y_at(d)), :], c_r.at[y_at(d)])
    lane_all = lax.broadcasted_iota(jnp.int32, (nx * rows, head_dim), 1)
    lane_tok = lax.broadcasted_iota(jnp.int32, (tok, head_dim), 1)
    exponent = math.log2(math.e) / math.sqrt(head_dim)
    for v in range(waves):
        for d in range(1, ny):
            arrived(kv.at[freshly(v, y_at(d)), :], kv_r.at[v, y_at(d)])
        for d in range(1, nx):
            arrived(qg.at[v, x_at(d)], q_r.at[v, x_at(d)])

        if v == 0:

            @pl.when(sec == 0)
            def _():
                pl.semaphore_signal(go.at[1], inc=1, device_id=other, device_id_type=MESH)

        keys_now = stale + (v + 1) * fresh
        tags = [
            jnp.where(lane_tok == s, 1.0, 0.0) for s in range(v * per_wave, (v + 1) * per_wave)
        ]
        tags = jnp.concatenate(tags * nx, axis=0).astype(BF16)
        sums = jnp.zeros((nx * rows, head_dim), F32)
        for h in range(heads):
            at = slice(h * head_dim, (h + 1) * head_dim)
            queries = jnp.concatenate([qg[v, :, :, at].reshape(nx * rows, head_dim), tags], axis=1)
            keys = jnp.concatenate([kv[0:keys_now, at], bias[0:keys_now, :]], axis=1)
            scores = lax.dot_general(
                queries, keys, (((1,), (1,)), ((), ())), preferred_element_type=F32
            )
            weight = jnp.exp2(scores * exponent)
            denom = jnp.sum(weight, axis=-1, keepdims=True)
            values = kv[0:keys_now, feat + h * head_dim : feat + (h + 1) * head_dim]
            numer = jnp.dot(weight.astype(BF16), values, preferred_element_type=F32)
            nsend[v, :, :, at] = numer.astype(BF16).reshape(nx, rows, head_dim)
            high = denom.astype(BF16).astype(F32)
            sums = jnp.where(lane_all == 2 * h, high, sums)
            sums = jnp.where(lane_all == 2 * h + 1, denom - high, sums)
        nsend[v, :, :, feat:] = sums.astype(BF16).reshape(nx, rows, head_dim)
        for c in num_copies[v]:
            c.start()

    for v in range(waves):
        total = nsend[v, x].astype(F32)
        for d in range(1, nx):
            arrived(nrecv.at[v, x_at(d)], n_r.at[v, x_at(d)])
            total += nrecv[v, x_at(d)].astype(F32)
        parts = []
        for h in range(heads):
            at = feat + 2 * h
            denom = total[:, at : at + 1] + total[:, at + 1 : at + 2]
            parts.append(total[:, h * head_dim : (h + 1) * head_dim] / denom)
        ag[v, z] = jnp.concatenate(parts, axis=1).astype(BF16)
        for c in a_copies[v]:
            c.start()

    @pl.when(sec == 0)
    def _():
        pl.semaphore_signal(go.at[2], inc=1, device_id=other, device_id_type=MESH)

    def source(c):
        pos = c * chunk
        first_row = -waves * fresh - pad
        for s in range(steps):
            row = (s // per_wave) * fresh + (s % per_wave) * tok
            row += (pos - begins[s]) // chunk * rows
            first_row = jnp.where(covers(s, pos), row, first_row)
        return first_row

    in_row = lax.broadcasted_iota(jnp.int32, (pad, waves * fresh), 0)
    in_col = lax.broadcasted_iota(jnp.int32, (pad, waves * fresh), 1)
    picks = []
    for c in range(nx):
        hit = (in_col - in_row == source(y * nx + c)) & (in_row < tok)
        picks.append(jnp.where(hit, 1.0, 0.0).astype(BF16))
    pick = jnp.concatenate(picks, axis=0)
    value = jnp.dot(pick, kv[stale:, :], preferred_element_type=F32)
    rsend[...] = value.astype(BF16).reshape(nx, pad, 2 * feat)
    for c in r_copies:
        c.start()

    own_wo.wait()
    gate = mod[2, :, pl.ds(pl.multiple_of(z * feat, feat), feat)]
    results = []
    for v in range(waves):
        for d in range(1, nz):
            arrived(ag.at[v, z_at(d)], ag_r.at[v, z_at(d)])
        attended = jnp.concatenate([ag[v, i] for i in range(nz)], axis=1)
        result = jnp.dot(attended, wo_v[...], preferred_element_type=F32)
        result = (own[v].astype(F32) + gate * result).astype(BF16)
        done[v] = result
        results.append(result.astype(F32))

        @pl.when(sec == 0)
        def _():
            for c in next_x[v]:
                c.start()

    result = jnp.concatenate(results, axis=0)
    parts = [result[s * tok : (s + 1) * tok] for s in range(steps)]
    value = []
    for p in range(steps):
        chosen = parts[0]
        for s in range(1, steps):
            chosen = jnp.where(places[s] == p, parts[s], chosen)
        value.append(chosen)
    bo[...] = jnp.concatenate(value, axis=0).astype(BF16)

    for d in range(1, nx):
        arrived(rrecv.at[x_at(d)], r_r.at[x_at(d)])
    rrecv[x] = rsend[x]
    out_row = lax.broadcasted_iota(jnp.int32, (chunk, nx * pad), 0)
    out_col = lax.broadcasted_iota(jnp.int32, (chunk, nx * pad), 1)
    block = out_col // pad
    within = out_col - block * pad
    hit = (out_row == block * tok + within) & (within < tok)
    place = jnp.where(hit, 1.0, 0.0).astype(BF16)
    written_to = source(seq) >= 0
    value = jnp.dot(place, rrecv[...].reshape(nx * pad, 2 * feat), preferred_element_type=F32)
    value = jnp.where(written_to, value, kv[cached(y), :].astype(F32)).astype(BF16)
    nk[...] = value[:, 0:feat]
    nv[...] = value[:, feat:]

    @pl.when(sec == 0)
    def _():
        for c in first_st + sn_copies + w_copies + sum(next_x + p_copies, []):
            c.wait_send()
        for v in range(waves):
            for c in first_x[v][1:]:
                c.wait_send()

            @pl.when(hy != y)
            def _():
                first_x[v][0].wait_send()

    @pl.when(sec == 1)
    def _():
        for c in wa_copies + wb_copies + sum(wc_copies + wd_copies, []):
            c.wait_send()

    for c in cache_copies + r_copies + sum(q_copies + kv_copies + num_copies + a_copies, []):
        c.wait_send()


def write_kernel(*refs):
    half = len(refs) // 2
    for src, dst in zip(refs[:half], refs[half:]):
        dst[...] = src[...]


def written(*arrays):
    vmem = pl.BlockSpec(memory_space=pltpu.VMEM)
    return pl.pallas_call(
        write_kernel,
        name="write",
        out_shape=tuple(jax.ShapeDtypeStruct(a.shape, a.dtype) for a in arrays),
        in_specs=[vmem] * len(arrays),
        out_specs=(vmem,) * len(arrays),
        compiler_params=pltpu.CompilerParams(vmem_limit_bytes=60 << 20),
    )(*arrays)


def per_device(
    patches, cache_k, cache_v, w_qkv, w_out, modulation, qk_gain, patch_order, patch_start
):
    nz = lax.axis_size("head")
    ny = nx = square_side(lax.axis_size("seq"))
    count, tok, feat = patches.shape
    chunk = cache_k.shape[1]
    head_dim = qk_gain.shape[-1]
    waves = 2
    per_wave = count // waves
    rows = per_wave * tok
    hz = nz // ny
    w_rows = w_qkv.shape[1]
    pad = -(-tok // 16) * 16
    keys = ny * (waves * rows + chunk)
    dma = pltpu.SemaphoreType.DMA
    vmem = pl.BlockSpec(memory_space=pltpu.VMEM)
    hbm = pl.BlockSpec(memory_space=pl.ANY)
    out, new_k, new_v = pl.pallas_call(
        functools.partial(block_kernel, nz, ny, nx, tok, waves, per_wave, head_dim),
        name="blocks",
        out_shape=(
            jax.ShapeDtypeStruct((count * tok, feat), BF16),
            jax.ShapeDtypeStruct((chunk, feat), BF16),
            jax.ShapeDtypeStruct((chunk, feat), BF16),
        ),
        in_specs=[hbm] * 9,
        out_specs=(vmem, vmem, vmem),
        scratch_shapes=[
            pltpu.SMEM((count,), jnp.int32),
            pltpu.SMEM((count,), jnp.int32),
            pltpu.VMEM((3, 1, nz * feat), F32),
            pltpu.VMEM((2, head_dim), F32),
            pltpu.VMEM((count * tok, feat), BF16),
            pltpu.VMEM((waves, rows, feat), BF16),
            pltpu.VMEM((waves, rows, feat), BF16),
            pltpu.VMEM((waves, ny, hz, rows, feat), BF16),
            pltpu.VMEM((waves, ny, rows, hz * feat), BF16),
            pltpu.VMEM((waves, nz, rows, feat), BF16),
            pltpu.VMEM((waves, rows, nz * feat), BF16),
            pltpu.VMEM((8, head_dim), F32),
            pltpu.VMEM((nz, 8, head_dim), F32),
            pltpu.VMEM((8, head_dim), F32),
            pltpu.VMEM((ny, 8, head_dim), F32),
            pltpu.VMEM((3, ny, nx, w_rows, feat), BF16),
            pltpu.VMEM((nz * feat, feat), BF16),
            pltpu.VMEM((waves, ny, rows, 3 * feat), BF16),
            pltpu.VMEM((waves, ny, rows, 3 * feat), BF16),
            pltpu.VMEM((waves, nx, rows, feat), BF16),
            pltpu.VMEM((keys, 2 * feat), BF16),
            pltpu.VMEM((keys, head_dim), BF16),
            pltpu.VMEM((waves, nx, rows, feat + head_dim), BF16),
            pltpu.VMEM((waves, nx, rows, feat + head_dim), BF16),
            pltpu.VMEM((waves, nz, rows, feat), BF16),
            pltpu.VMEM((nx, pad, 2 * feat), BF16),
            pltpu.VMEM((nx, pad, 2 * feat), BF16),
            dma((9,)),
            dma((waves, nz)),
            dma((waves, ny, hz)),
            dma((nz,)),
            dma((nz,)),
            dma((ny,)),
            dma((ny,)),
            dma((waves, nz)),
            dma((waves, nz)),
            dma((nx,)),
            dma((nx,)),
            dma((nx,)),
            dma((nx,)),
            dma((ny,)),
            dma((ny,)),
            dma((3, ny)),
            dma((3, ny)),
            dma((3, nx)),
            dma((3, nx)),
            dma((ny,)),
            dma((ny,)),
            dma((waves, ny)),
            dma((waves, ny)),
            dma((waves, nx)),
            dma((waves, nx)),
            dma((waves, ny)),
            dma((waves, ny)),
            dma((waves, nx)),
            dma((waves, nx)),
            dma((waves, nz)),
            dma((waves, nz)),
            dma((nx,)),
            dma((nx,)),
            pltpu.SemaphoreType.REGULAR((3,)),
        ],
        compiler_params=pltpu.CompilerParams(
            collective_id=0, has_side_effects=True, vmem_limit_bytes=60 << 20
        ),
    )(
        patch_order,
        patch_start,
        patches.reshape(count * tok, feat),
        cache_k[0],
        cache_v[0],
        jnp.transpose(w_qkv[0], (1, 0, 2)),
        w_out[0],
        jnp.transpose(modulation, (1, 0, 2)),
        qk_gain[0],
    )
    out, new_k, new_v = written(out, new_k, new_v)
    return (out.reshape(1, count, tok, feat), new_k[None], new_v[None])


def solution(mesh):
    return jax.shard_map(
        per_device,
        mesh=mesh,
        in_specs=(
            P(None, "seq", "head"),
            P("section", "seq", "head"),
            P("section", "seq", "head"),
            P("section", "seq", None, "head"),
            P("section", None, "head"),
            P("section", None, None),
            P("section", None, None),
            P(),
            P(),
        ),
        out_specs=(
            P("section", None, "seq", "head"),
            P("section", "seq", "head"),
            P("section", "seq", "head"),
        ),
        check_vma=False,
    )
```

```python
import functools
import math

import jax
import jax.numpy as jnp
from jax import lax
from jax.experimental import pallas as pl
from jax.experimental.pallas import tpu as pltpu
from jax.sharding import PartitionSpec as P

MESH = pl.DeviceIdType.MESH
F32 = jnp.float32
BF16 = jnp.bfloat16
FAR = -1e30


def square_side(count):
    side = math.isqrt(count)
    assert side * side == count
    return side


def block_kernel(
    nz,
    ny,
    nx,
    tok,
    waves,
    per_wave,
    head_dim,
    order_h,
    start_h,
    x_in,
    ck,
    cv,
    w,
    wo,
    mod_h,
    gain_h,
    bo,
    nk,
    nv,
    order,
    start,
    mod,
    gain,
    x_rows,
    own,
    done,
    xr,
    xe,
    xg,
    xn,
    st_send,
    st_recv,
    st_norm,
    st_all,
    wbuf,
    wo_v,
    psend,
    precv,
    qg,
    kv,
    bias,
    nsend,
    nrecv,
    ag,
    rsend,
    rrecv,
    loc,
    x_s,
    x_r,
    st_s,
    st_r,
    sn_s,
    sn_r,
    h_s,
    h_r,
    w_s,
    w_r,
    wa_s,
    wa_r,
    wb_s,
    wb_r,
    wc_s,
    wc_r,
    wd_s,
    wd_r,
    c_s,
    c_r,
    p_s,
    p_r,
    q_s,
    q_r,
    kv_s,
    kv_r,
    n_s,
    n_r,
    ag_s,
    ag_r,
    r_s,
    r_r,
    go,
):
    sec = lax.axis_index("section")
    z = lax.axis_index("head")
    seq = lax.axis_index("seq")
    y = seq // nx
    x = lax.rem(seq, nx)
    _, rows, feat = own.shape
    chunk = ck.shape[0]
    heads = feat // head_dim
    width = nz * feat
    w_rows = w.shape[1]
    hz = nz // ny
    hy = z // hz
    steps = waves * per_wave
    stale = ny * chunk
    fresh = ny * rows
    span = ny * chunk
    pad = rrecv.shape[1]

    def z_at(d):
        return lax.rem(z + d, nz)

    def y_at(d):
        return lax.rem(y + d, ny)

    def x_at(d):
        return lax.rem(x + d, nx)

    def on_z(d):
        return (sec, z_at(d), seq)

    def on_y(d):
        return (sec, z, y_at(d) * nx + x)

    def on_x(d):
        return (sec, z, y * nx + x_at(d))

    other = (1 - sec, z, seq)
    z_order = sorted(range(1, nz), key=lambda d: -min(d, nz - d))
    y_order = sorted(range(1, ny), key=lambda d: -min(d, ny - d))
    x_order = sorted(range(1, nx), key=lambda d: -min(d, nx - d))

    def copy(src, dst, ss, rs, dev):
        return pltpu.make_async_remote_copy(
            src_ref=src, dst_ref=dst, send_sem=ss, recv_sem=rs, device_id=dev, device_id_type=MESH
        )

    def arrived(dst, rs):
        copy(dst, dst, rs, rs, other).wait_recv()

    def cached(i):
        return pl.ds(pl.multiple_of(i * chunk, chunk), chunk)

    def freshly(v, i):
        return pl.ds(pl.multiple_of(stale + v * fresh + i * rows, rows), rows)

    w_slot = wbuf.at[:, y, x]
    own_x = pltpu.make_async_copy(x_in, x_rows, loc.at[0])
    own_w = pltpu.make_async_copy(w, w_slot, loc.at[1])
    own_cache = [
        pltpu.make_async_copy(ck, kv.at[cached(y), 0:feat], loc.at[2]),
        pltpu.make_async_copy(cv, kv.at[cached(y), feat : 2 * feat], loc.at[3]),
    ]
    own_places = [
        pltpu.make_async_copy(order_h, order, loc.at[4]),
        pltpu.make_async_copy(start_h, start, loc.at[5]),
    ]
    own_scales = [
        pltpu.make_async_copy(mod_h, mod, loc.at[6]),
        pltpu.make_async_copy(gain_h, gain, loc.at[7]),
    ]
    own_wo = pltpu.make_async_copy(wo, wo_v, loc.at[8])

    def by_wave(make):
        return [make(v) for v in range(waves)]

    first_x = by_wave(
        lambda v: [
            copy(
                own.at[v],
                xr.at[v, y, lax.rem(z, hz)],
                x_s.at[v, d],
                x_r.at[v, y, lax.rem(z, hz)],
                (0, z_at(d), hy * nx + x),
            )
            for d in [0] + z_order
        ]
    )
    first_st = [
        copy(st_send, st_recv.at[z], st_s.at[d], st_r.at[z], on_z(d)) for d in z_order
    ]
    next_x = by_wave(
        lambda v: [
            copy(done.at[v], xg.at[v, z], h_s.at[v, d], h_r.at[v, z], (1, z_at(d), seq))
            for d in [0] + z_order
        ]
    )
    sn_copies = [
        copy(st_norm, st_all.at[y], sn_s.at[d], sn_r.at[y], on_y(d)) for d in y_order
    ]
    w_copies = [copy(w_slot, w_slot, w_s.at[d], w_r.at[x], on_x(d)) for d in x_order]
    half = w_rows // 2
    upper, lower = pl.ds(0, half), pl.ds(half, half)

    def w_gather(view, ss, rs, at, to, count):
        return [copy(view, view, ss.at[d], rs.at[at], to(d)) for d in range(1, count)]

    wa_copies = w_gather(wbuf.at[:, y, x, upper], wa_s, wa_r, x, on_x, nx)
    wb_copies = w_gather(wbuf.at[:, y, x, lower], wb_s, wb_r, y, on_y, ny)
    wc_copies = [
        w_gather(wbuf.at[i, y, :, upper], wc_s.at[i], wc_r.at[i], y, on_y, ny) for i in range(3)
    ]
    wd_copies = [
        w_gather(wbuf.at[i, :, x, lower], wd_s.at[i], wd_r.at[i], x, on_x, nx) for i in range(3)
    ]
    cache_slot = kv.at[cached(y), :]
    cache_copies = [copy(cache_slot, cache_slot, c_s.at[d], c_r.at[y], on_y(d)) for d in y_order]
    p_copies = by_wave(
        lambda v: [
            copy(psend.at[v, y_at(d)], precv.at[v, y], p_s.at[v, d], p_r.at[v, y], on_y(d))
            for d in y_order
        ]
    )
    q_copies = by_wave(
        lambda v: [
            copy(qg.at[v, x], qg.at[v, x], q_s.at[v, d], q_r.at[v, x], on_x(d))
            for d in x_order
        ]
    )
    kv_copies = by_wave(
        lambda v: [
            copy(
                kv.at[freshly(v, y), :],
                kv.at[freshly(v, y), :],
                kv_s.at[v, d],
                kv_r.at[v, y],
                on_y(d),
            )
            for d in y_order
        ]
    )
    num_copies = by_wave(
        lambda v: [
            copy(nsend.at[v, x_at(d)], nrecv.at[v, x], n_s.at[v, d], n_r.at[v, x], on_x(d))
            for d in x_order
        ]
    )
    a_copies = by_wave(
        lambda v: [
            copy(ag.at[v, z], ag.at[v, z], ag_s.at[v, d], ag_r.at[v, z], on_z(d))
            for d in z_order
        ]
    )
    r_copies = [
        copy(rsend.at[x_at(d)], rrecv.at[x], r_s.at[d], r_r.at[x], on_x(d)) for d in x_order
    ]

    @pl.when(sec == 0)
    def _():
        own_x.start()

    for c in own_places + [own_w] + own_cache + own_scales + [own_wo]:
        c.start()

    barrier = pltpu.get_barrier_semaphore()

    def greet(dev):
        pl.semaphore_signal(barrier, inc=1, device_id=dev, device_id_type=MESH)

    partners = (
        [on_z(d) for d in range(1, nz)]
        + [on_y(d) for d in range(1, ny)]
        + [on_x(d) for d in range(1, nx)]
    )
    for dev in partners:
        greet(dev)

    def is_own(i, b):
        return (y == i) & (z == y * hz + b)

    @pl.when(sec == 0)
    def _():
        for i in range(ny):
            for b in range(hz):

                @pl.when(jnp.logical_not(is_own(i, b)))
                def _():
                    greet((0, y * hz + b, i * nx + x))

    @pl.when(sec == 1)
    def _():
        for d in range(nz):
            greet((0, z_at(d), seq))

    for c in own_places:
        c.wait()
    places = [order[s] for s in range(steps)]
    begins = [sum(jnp.where(places[s] == p, start[p], 0) for p in range(steps)) for s in range(steps)]

    lane_rows = lax.broadcasted_iota(jnp.int32, (steps * tok, head_dim), 1)

    def shard_stats(value):
        middle = jnp.sum(value, axis=-1, keepdims=True) * (1.0 / feat)
        value = value - middle
        square = jnp.sum(value * value, axis=-1, keepdims=True)
        both = jnp.where(lane_rows == 0, middle, jnp.where(lane_rows == 1, square, 0.0))
        both = jnp.concatenate([both, jnp.zeros((head_dim - steps * tok, head_dim), F32)], axis=0)
        st_send[...] = jnp.transpose(both)[0:8, :]

    @pl.when(sec == 0)
    def _():
        own_x.wait()
        value = x_rows[...].astype(F32)
        parts = [value[p * tok : (p + 1) * tok] for p in range(steps)]
        value = []
        for s in range(steps):
            chosen = parts[0]
            for p in range(1, steps):
                chosen = jnp.where(places[s] == p, parts[p], chosen)
            value.append(chosen)
        value = jnp.concatenate(value, axis=0)
        own[...] = value.astype(BF16).reshape(waves, rows, feat)
        shard_stats(value)
        st_recv[z] = st_send[...]
        pl.semaphore_wait(barrier, len(partners) + 2 * nz - jnp.where(hy == y, 1, 0))
        own_w.wait()
        for c in w_copies + first_st:
            c.start()
        for v in range(waves):
            for c in first_x[v][1:]:
                c.start()

            @pl.when(hy == y)
            def _():
                xr[v, y, lax.rem(z, hz)] = own[v]

            @pl.when(hy != y)
            def _():
                first_x[v][0].start()

    @pl.when(sec == 1)
    def _():
        own_w.wait()

    for c in own_cache:
        c.wait()

    @pl.when(sec == 0)
    def _():
        for c in cache_copies:
            c.start()

    @pl.when(sec == 1)
    def _():
        pl.semaphore_wait(barrier, len(partners))
        for c in wb_copies:
            c.start()
        pl.semaphore_wait(go.at[0], 1)
        for c in wa_copies:
            c.start()
        for d in range(1, ny):
            arrived(wbuf.at[:, y_at(d), x, lower], wb_r.at[y_at(d)])
        for c in wd_copies[1]:
            c.start()
        for d in range(1, nx):
            arrived(wbuf.at[:, y, x_at(d), upper], wa_r.at[x_at(d)])
        for c in wd_copies[2]:
            c.start()
        pl.semaphore_wait(go.at[1], 1)
        for c in wc_copies[1] + wc_copies[2] + wc_copies[0] + wd_copies[0] + cache_copies:
            c.start()
        pl.semaphore_wait(go.at[2], 1)

    def covers(s, pos):
        return (begins[s] <= pos) & (pos < begins[s] + span)

    def first_from(step, pos):
        found = steps
        for s in reversed(range(step, steps)):
            found = jnp.where(covers(s, pos), s, found)
        return found

    lane = lax.broadcasted_iota(jnp.int32, (tok, head_dim), 1)
    lane_chunk = lax.broadcasted_iota(jnp.int32, (chunk, head_dim), 1)
    for j in range(ny):
        upto = first_from(0, (j * nx + x) * chunk)
        value = jnp.where(lane_chunk < upto, 0.0, FAR)
        bias[j * chunk : (j + 1) * chunk, :] = value.astype(BF16)
        for v in range(waves):
            parts = []
            for s in range(v * per_wave, (v + 1) * per_wave):
                upto = first_from(s + 1, begins[s] + j * chunk)
                parts.append(jnp.where((lane >= s) & (lane < upto), 0.0, FAR))
            at = stale + v * fresh + j * rows
            bias[at : at + rows, :] = jnp.concatenate(parts, axis=0).astype(BF16)

    for c in own_scales:
        c.wait()

    def rms_heads(value, which):
        out = []
        for h in range(heads):
            part = value[:, h * head_dim : (h + 1) * head_dim]
            power = jnp.sum(part * part, axis=-1, keepdims=True) * (1.0 / head_dim)
            out.append(part * lax.rsqrt(power + 1e-06) * gain[which : which + 1, :])
        return jnp.concatenate(out, axis=-1).astype(BF16)

    def spread_keys(v, key, value):
        kv[freshly(v, y), 0:feat] = rms_heads(key, 1)
        kv[freshly(v, y), feat : 2 * feat] = value.astype(BF16)
        for c in kv_copies[v]:
            c.start()

    def spread_queries(v, query):
        qg[v, x] = rms_heads(query, 0)
        for c in q_copies[v]:
            c.start()

    @pl.when(sec == 0)
    def _():
        for d in range(1, nz):
            arrived(st_recv.at[z_at(d)], st_r.at[z_at(d)])
        middles = [st_recv[i, 0:1, :] for i in range(nz)]
        mean = sum(middles) * (1.0 / nz)
        square = sum(st_recv[i, 1:2, :] for i in range(nz))
        square += sum((m - mean) * (m - mean) for m in middles) * feat
        scale = lax.rsqrt(square * (1.0 / width) + 1e-06)
        line = lax.broadcasted_iota(jnp.int32, (8, head_dim), 0)
        value = jnp.where(line == 0, mean, jnp.where(line == 1, scale, 0.0))
        st_norm[...] = value
        st_all[y] = value
        for c in sn_copies:
            c.start()
        for d in range(1, ny):
            arrived(st_all.at[y_at(d)], sn_r.at[y_at(d)])
        value = st_all[...].reshape(8 * ny, head_dim)
        value = jnp.concatenate([value, jnp.zeros((head_dim - 8 * ny, head_dim), F32)], axis=0)
        stats = jnp.transpose(value)
        for v in range(waves):
            for i in range(ny):
                mean = stats[v * rows : (v + 1) * rows, 8 * i : 8 * i + 1]
                scale = stats[v * rows : (v + 1) * rows, 8 * i + 1 : 8 * i + 2]
                for b in range(hz):

                    @pl.when(jnp.logical_not(is_own(i, b)))
                    def _():
                        arrived(xr.at[v, i, b], x_r.at[v, i, b])

                    at = pl.ds(pl.multiple_of((y * hz + b) * feat, feat), feat)
                    value = (xr[v, i, b].astype(F32) - mean) * scale
                    value = value * (1.0 + mod[1, :, at]) + mod[0, :, at]
                    xe[v, i, :, b * feat : (b + 1) * feat] = value.astype(BF16)
            if v == 0:
                for d in range(1, nx):
                    arrived(wbuf.at[:, y, x_at(d)], w_r.at[x_at(d)])
                pl.semaphore_signal(go.at[0], inc=1, device_id=other, device_id_type=MESH)
            tokens = xe[v].reshape(ny * rows, hz * feat)
            for i in range(3):
                weights = wbuf[i, y].reshape(nx * w_rows, feat)
                value = jnp.dot(tokens, weights, preferred_element_type=F32)
                psend[v, :, :, i * feat : (i + 1) * feat] = value.astype(BF16).reshape(
                    ny, rows, feat
                )
            for c in p_copies[v]:
                c.start()
        for v in range(waves):
            value = psend[v, y].astype(F32)
            for d in range(1, ny):
                arrived(precv.at[v, y_at(d)], p_r.at[v, y_at(d)])
                value += precv[v, y_at(d)].astype(F32)
            spread_keys(v, value[:, feat : 2 * feat], value[:, 2 * feat :])
            spread_queries(v, value[:, 0:feat])

    @pl.when(sec == 1)
    def _():
        for v in range(waves):
            for i in range(nz):
                arrived(xg.at[v, i], h_r.at[v, i])
            own[v] = xg[v, z]
            total = jnp.zeros((rows, feat), F32)
            for i in range(nz):
                total += xg[v, i].astype(F32)
            mean = jnp.sum(total, axis=-1, keepdims=True) * (1.0 / width)
            total = jnp.zeros((rows, feat), F32)
            for i in range(nz):
                diff = xg[v, i].astype(F32) - mean
                total += diff * diff
            scale = lax.rsqrt(jnp.sum(total, axis=-1, keepdims=True) * (1.0 / width) + 1e-06)
            for i in range(nz):
                at = slice(i * feat, (i + 1) * feat)
                value = (xg[v, i].astype(F32) - mean) * scale
                value = value * (1.0 + mod[1, :, at]) + mod[0, :, at]
                xn[v, :, at] = value.astype(BF16)
            parts = [None] * 3
            for i in (1, 2, 0):
                if v == 0:
                    for d in range(1, ny):
                        arrived(wbuf.at[i, y_at(d), :, upper], wc_r.at[i, y_at(d)])
                    for d in range(1, nx):
                        arrived(wbuf.at[i, :, x_at(d), lower], wd_r.at[i, x_at(d)])
                weights = wbuf[i].reshape(width, feat)
                parts[i] = jnp.dot(xn[v], weights, preferred_element_type=F32)
                if i == 2:
                    spread_keys(v, parts[1], parts[2])
            spread_queries(v, parts[0])

    for d in range(1, ny):
        arrived(kv.at[cached(y_at(d)), :], c_r.at[y_at(d)])
    lane_all = lax.broadcasted_iota(jnp.int32, (nx * rows, head_dim), 1)
    lane_tok = lax.broadcasted_iota(jnp.int32, (tok, head_dim), 1)
    exponent = math.log2(math.e) / math.sqrt(head_dim)
    for v in range(waves):
        for d in range(1, ny):
            arrived(kv.at[freshly(v, y_at(d)), :], kv_r.at[v, y_at(d)])
        for d in range(1, nx):
            arrived(qg.at[v, x_at(d)], q_r.at[v, x_at(d)])

        if v == 0:

            @pl.when(sec == 0)
            def _():
                pl.semaphore_signal(go.at[1], inc=1, device_id=other, device_id_type=MESH)

        keys_now = stale + (v + 1) * fresh
        tags = [
            jnp.where(lane_tok == s, 1.0, 0.0) for s in range(v * per_wave, (v + 1) * per_wave)
        ]
        tags = jnp.concatenate(tags * nx, axis=0).astype(BF16)
        sums = jnp.zeros((nx * rows, head_dim), F32)
        for h in range(heads):
            at = slice(h * head_dim, (h + 1) * head_dim)
            queries = jnp.concatenate([qg[v, :, :, at].reshape(nx * rows, head_dim), tags], axis=1)
            keys = jnp.concatenate([kv[0:keys_now, at], bias[0:keys_now, :]], axis=1)
            scores = lax.dot_general(
                queries, keys, (((1,), (1,)), ((), ())), preferred_element_type=F32
            )
            weight = jnp.exp2(scores * exponent)
            denom = jnp.sum(weight, axis=-1, keepdims=True)
            values = kv[0:keys_now, feat + h * head_dim : feat + (h + 1) * head_dim]
            numer = jnp.dot(weight.astype(BF16), values, preferred_element_type=F32)
            nsend[v, :, :, at] = numer.astype(BF16).reshape(nx, rows, head_dim)
            high = denom.astype(BF16).astype(F32)
            sums = jnp.where(lane_all == 2 * h, high, sums)
            sums = jnp.where(lane_all == 2 * h + 1, denom - high, sums)
        nsend[v, :, :, feat:] = sums.astype(BF16).reshape(nx, rows, head_dim)
        for c in num_copies[v]:
            c.start()

    for v in range(waves):
        total = nsend[v, x].astype(F32)
        for d in range(1, nx):
            arrived(nrecv.at[v, x_at(d)], n_r.at[v, x_at(d)])
            total += nrecv[v, x_at(d)].astype(F32)
        parts = []
        for h in range(heads):
            at = feat + 2 * h
            denom = total[:, at : at + 1] + total[:, at + 1 : at + 2]
            parts.append(total[:, h * head_dim : (h + 1) * head_dim] / denom)
        ag[v, z] = jnp.concatenate(parts, axis=1).astype(BF16)
        for c in a_copies[v]:
            c.start()

    @pl.when(sec == 0)
    def _():
        pl.semaphore_signal(go.at[2], inc=1, device_id=other, device_id_type=MESH)

    def source(c):
        pos = c * chunk
        first_row = -waves * fresh - pad
        for s in range(steps):
            row = (s // per_wave) * fresh + (s % per_wave) * tok
            row += (pos - begins[s]) // chunk * rows
            first_row = jnp.where(covers(s, pos), row, first_row)
        return first_row

    in_row = lax.broadcasted_iota(jnp.int32, (pad, waves * fresh), 0)
    in_col = lax.broadcasted_iota(jnp.int32, (pad, waves * fresh), 1)
    picks = []
    for c in range(nx):
        hit = (in_col - in_row == source(y * nx + c)) & (in_row < tok)
        picks.append(jnp.where(hit, 1.0, 0.0).astype(BF16))
    pick = jnp.concatenate(picks, axis=0)
    value = jnp.dot(pick, kv[stale:, :], preferred_element_type=F32)
    rsend[...] = value.astype(BF16).reshape(nx, pad, 2 * feat)
    for c in r_copies:
        c.start()

    def refresh():
        for d in range(1, nx):
            arrived(rrecv.at[x_at(d)], r_r.at[x_at(d)])
        rrecv[x] = rsend[x]
        out_row = lax.broadcasted_iota(jnp.int32, (chunk, nx * pad), 0)
        out_col = lax.broadcasted_iota(jnp.int32, (chunk, nx * pad), 1)
        block = out_col // pad
        within = out_col - block * pad
        hit = (out_row == block * tok + within) & (within < tok)
        place = jnp.where(hit, 1.0, 0.0).astype(BF16)
        written_to = source(seq) >= 0
        value = jnp.dot(place, rrecv[...].reshape(nx * pad, 2 * feat), preferred_element_type=F32)
        value = jnp.where(written_to, value, kv[cached(y), :].astype(F32)).astype(BF16)
        nk[...] = value[:, 0:feat]
        nv[...] = value[:, feat:]

    pl.when(sec == 1)(refresh)
    own_wo.wait()
    gate = mod[2, :, pl.ds(pl.multiple_of(z * feat, feat), feat)]
    results = []
    for v in range(waves):
        result = jnp.zeros((rows, feat), F32)
        for d in [0] + z_order[::-1]:
            if d:
                arrived(ag.at[v, z_at(d)], ag_r.at[v, z_at(d)])
            at = pl.ds(pl.multiple_of(z_at(d) * feat, feat), feat)
            result += jnp.dot(ag[v, z_at(d)], wo_v[at, :], preferred_element_type=F32)
        result = (own[v].astype(F32) + gate * result).astype(BF16)
        done[v] = result
        results.append(result.astype(F32))

        @pl.when(sec == 0)
        def _():
            for c in next_x[v]:
                c.start()

    result = jnp.concatenate(results, axis=0)
    parts = [result[s * tok : (s + 1) * tok] for s in range(steps)]
    value = []
    for p in range(steps):
        chosen = parts[0]
        for s in range(1, steps):
            chosen = jnp.where(places[s] == p, parts[s], chosen)
        value.append(chosen)
    bo[...] = jnp.concatenate(value, axis=0).astype(BF16)

    pl.when(sec == 0)(refresh)

    @pl.when(sec == 0)
    def _():
        for c in first_st + sn_copies + w_copies + sum(next_x + p_copies, []):
            c.wait_send()
        for v in range(waves):
            for c in first_x[v][1:]:
                c.wait_send()

            @pl.when(hy != y)
            def _():
                first_x[v][0].wait_send()

    @pl.when(sec == 1)
    def _():
        for c in wa_copies + wb_copies + sum(wc_copies + wd_copies, []):
            c.wait_send()

    for c in cache_copies + r_copies + sum(q_copies + kv_copies + num_copies + a_copies, []):
        c.wait_send()


def write_kernel(*refs):
    half = len(refs) // 2
    for src, dst in zip(refs[:half], refs[half:]):
        dst[...] = src[...]


def written(*arrays):
    vmem = pl.BlockSpec(memory_space=pltpu.VMEM)
    return pl.pallas_call(
        write_kernel,
        name="write",
        out_shape=tuple(jax.ShapeDtypeStruct(a.shape, a.dtype) for a in arrays),
        in_specs=[vmem] * len(arrays),
        out_specs=(vmem,) * len(arrays),
        compiler_params=pltpu.CompilerParams(vmem_limit_bytes=60 << 20),
    )(*arrays)


def per_device(
    patches, cache_k, cache_v, w_qkv, w_out, modulation, qk_gain, patch_order, patch_start
):
    nz = lax.axis_size("head")
    ny = nx = square_side(lax.axis_size("seq"))
    count, tok, feat = patches.shape
    chunk = cache_k.shape[1]
    head_dim = qk_gain.shape[-1]
    waves = 2
    per_wave = count // waves
    rows = per_wave * tok
    hz = nz // ny
    w_rows = w_qkv.shape[1]
    pad = -(-tok // 16) * 16
    keys = ny * (waves * rows + chunk)
    dma = pltpu.SemaphoreType.DMA
    vmem = pl.BlockSpec(memory_space=pltpu.VMEM)
    hbm = pl.BlockSpec(memory_space=pl.ANY)
    out, new_k, new_v = pl.pallas_call(
        functools.partial(block_kernel, nz, ny, nx, tok, waves, per_wave, head_dim),
        name="blocks",
        out_shape=(
            jax.ShapeDtypeStruct((count * tok, feat), BF16),
            jax.ShapeDtypeStruct((chunk, feat), BF16),
            jax.ShapeDtypeStruct((chunk, feat), BF16),
        ),
        in_specs=[hbm] * 9,
        out_specs=(vmem, vmem, vmem),
        scratch_shapes=[
            pltpu.SMEM((count,), jnp.int32),
            pltpu.SMEM((count,), jnp.int32),
            pltpu.VMEM((3, 1, nz * feat), F32),
            pltpu.VMEM((2, head_dim), F32),
            pltpu.VMEM((count * tok, feat), BF16),
            pltpu.VMEM((waves, rows, feat), BF16),
            pltpu.VMEM((waves, rows, feat), BF16),
            pltpu.VMEM((waves, ny, hz, rows, feat), BF16),
            pltpu.VMEM((waves, ny, rows, hz * feat), BF16),
            pltpu.VMEM((waves, nz, rows, feat), BF16),
            pltpu.VMEM((waves, rows, nz * feat), BF16),
            pltpu.VMEM((8, head_dim), F32),
            pltpu.VMEM((nz, 8, head_dim), F32),
            pltpu.VMEM((8, head_dim), F32),
            pltpu.VMEM((ny, 8, head_dim), F32),
            pltpu.VMEM((3, ny, nx, w_rows, feat), BF16),
            pltpu.VMEM((nz * feat, feat), BF16),
            pltpu.VMEM((waves, ny, rows, 3 * feat), BF16),
            pltpu.VMEM((waves, ny, rows, 3 * feat), BF16),
            pltpu.VMEM((waves, nx, rows, feat), BF16),
            pltpu.VMEM((keys, 2 * feat), BF16),
            pltpu.VMEM((keys, head_dim), BF16),
            pltpu.VMEM((waves, nx, rows, feat + head_dim), BF16),
            pltpu.VMEM((waves, nx, rows, feat + head_dim), BF16),
            pltpu.VMEM((waves, nz, rows, feat), BF16),
            pltpu.VMEM((nx, pad, 2 * feat), BF16),
            pltpu.VMEM((nx, pad, 2 * feat), BF16),
            dma((9,)),
            dma((waves, nz)),
            dma((waves, ny, hz)),
            dma((nz,)),
            dma((nz,)),
            dma((ny,)),
            dma((ny,)),
            dma((waves, nz)),
            dma((waves, nz)),
            dma((nx,)),
            dma((nx,)),
            dma((nx,)),
            dma((nx,)),
            dma((ny,)),
            dma((ny,)),
            dma((3, ny)),
            dma((3, ny)),
            dma((3, nx)),
            dma((3, nx)),
            dma((ny,)),
            dma((ny,)),
            dma((waves, ny)),
            dma((waves, ny)),
            dma((waves, nx)),
            dma((waves, nx)),
            dma((waves, ny)),
            dma((waves, ny)),
            dma((waves, nx)),
            dma((waves, nx)),
            dma((waves, nz)),
            dma((waves, nz)),
            dma((nx,)),
            dma((nx,)),
            pltpu.SemaphoreType.REGULAR((3,)),
        ],
        compiler_params=pltpu.CompilerParams(
            collective_id=0, has_side_effects=True, vmem_limit_bytes=60 << 20
        ),
    )(
        patch_order,
        patch_start,
        patches.reshape(count * tok, feat),
        cache_k[0],
        cache_v[0],
        jnp.transpose(w_qkv[0], (1, 0, 2)),
        w_out[0],
        jnp.transpose(modulation, (1, 0, 2)),
        qk_gain[0],
    )
    out, new_k, new_v = written(out, new_k, new_v)
    return (out.reshape(1, count, tok, feat), new_k[None], new_v[None])


def solution(mesh):
    return jax.shard_map(
        per_device,
        mesh=mesh,
        in_specs=(
            P(None, "seq", "head"),
            P("section", "seq", "head"),
            P("section", "seq", "head"),
            P("section", "seq", None, "head"),
            P("section", None, "head"),
            P("section", None, None),
            P("section", None, None),
            P(),
            P(),
        ),
        out_specs=(
            P("section", None, "seq", "head"),
            P("section", "seq", "head"),
            P("section", "seq", "head"),
        ),
        check_vma=False,
    )
```

```python
import functools
import math

import jax
import jax.numpy as jnp
from jax import lax
from jax.experimental import pallas as pl
from jax.experimental.pallas import tpu as pltpu
from jax.sharding import PartitionSpec as P

MESH = pl.DeviceIdType.MESH
F32 = jnp.float32
BF16 = jnp.bfloat16
FAR = -1e30


def square_side(count):
    side = math.isqrt(count)
    assert side * side == count
    return side


def block_kernel(
    nz,
    ny,
    nx,
    tok,
    waves,
    per_wave,
    head_dim,
    order_h,
    start_h,
    x_in,
    ck,
    cv,
    w,
    wo,
    mod_h,
    gain_h,
    bo,
    nk,
    nv,
    order,
    start,
    mod,
    gain,
    x_rows,
    own,
    done,
    xr,
    xe,
    xg,
    xn,
    st_send,
    st_recv,
    st_norm,
    st_all,
    wbuf,
    wo_v,
    psend,
    precv,
    qg,
    kv,
    bias,
    nsend,
    nrecv,
    ag,
    rsend,
    rrecv,
    loc,
    x_s,
    x_r,
    st_s,
    st_r,
    sn_s,
    sn_r,
    h_s,
    h_r,
    w_s,
    w_r,
    wa_s,
    wa_r,
    wb_s,
    wb_r,
    wc_s,
    wc_r,
    wd_s,
    wd_r,
    we_s,
    we_r,
    wf_s,
    wf_r,
    c_s,
    c_r,
    p_s,
    p_r,
    q_s,
    q_r,
    kv_s,
    kv_r,
    n_s,
    n_r,
    ag_s,
    ag_r,
    r_s,
    r_r,
    go,
):
    sec = lax.axis_index("section")
    z = lax.axis_index("head")
    seq = lax.axis_index("seq")
    y = seq // nx
    x = lax.rem(seq, nx)
    _, rows, feat = own.shape
    chunk = ck.shape[0]
    heads = feat // head_dim
    width = nz * feat
    w_rows = w.shape[1]
    hz = nz // ny
    hy = z // hz
    steps = waves * per_wave
    stale = ny * chunk
    fresh = ny * rows
    span = ny * chunk
    pad = rrecv.shape[1]

    def z_at(d):
        return lax.rem(z + d, nz)

    def y_at(d):
        return lax.rem(y + d, ny)

    def x_at(d):
        return lax.rem(x + d, nx)

    def on_z(d):
        return (sec, z_at(d), seq)

    def on_y(d):
        return (sec, z, y_at(d) * nx + x)

    def on_x(d):
        return (sec, z, y * nx + x_at(d))

    other = (1 - sec, z, seq)
    z_order = sorted(range(1, nz), key=lambda d: -min(d, nz - d))
    y_order = sorted(range(1, ny), key=lambda d: -min(d, ny - d))
    x_order = sorted(range(1, nx), key=lambda d: -min(d, nx - d))

    def copy(src, dst, ss, rs, dev):
        return pltpu.make_async_remote_copy(
            src_ref=src, dst_ref=dst, send_sem=ss, recv_sem=rs, device_id=dev, device_id_type=MESH
        )

    def arrived(dst, rs):
        copy(dst, dst, rs, rs, other).wait_recv()

    def cached(i):
        return pl.ds(pl.multiple_of(i * chunk, chunk), chunk)

    def freshly(v, i):
        return pl.ds(pl.multiple_of(stale + v * fresh + i * rows, rows), rows)

    w_slot = wbuf.at[:, y, x]
    own_x = pltpu.make_async_copy(x_in, x_rows, loc.at[0])
    own_w = pltpu.make_async_copy(w, w_slot, loc.at[1])
    own_cache = [
        pltpu.make_async_copy(ck, kv.at[cached(y), 0:feat], loc.at[2]),
        pltpu.make_async_copy(cv, kv.at[cached(y), feat : 2 * feat], loc.at[3]),
    ]
    own_places = [
        pltpu.make_async_copy(order_h, order, loc.at[4]),
        pltpu.make_async_copy(start_h, start, loc.at[5]),
    ]
    own_scales = [
        pltpu.make_async_copy(mod_h, mod, loc.at[6]),
        pltpu.make_async_copy(gain_h, gain, loc.at[7]),
    ]
    own_wo = pltpu.make_async_copy(wo, wo_v, loc.at[8])

    def by_wave(make):
        return [make(v) for v in range(waves)]

    first_x = by_wave(
        lambda v: [
            copy(
                own.at[v],
                xr.at[v, y, lax.rem(z, hz)],
                x_s.at[v, d],
                x_r.at[v, y, lax.rem(z, hz)],
                (0, z_at(d), hy * nx + x),
            )
            for d in [0] + z_order
        ]
    )
    first_st = [
        copy(st_send, st_recv.at[z], st_s.at[d], st_r.at[z], on_z(d)) for d in z_order
    ]
    next_x = by_wave(
        lambda v: [
            copy(done.at[v], xg.at[v, z], h_s.at[v, d], h_r.at[v, z], (1, z_at(d), seq))
            for d in [0] + z_order
        ]
    )
    sn_copies = [
        copy(st_norm, st_all.at[y], sn_s.at[d], sn_r.at[y], on_y(d)) for d in y_order
    ]
    w_copies = [copy(w_slot, w_slot, w_s.at[d], w_r.at[x], on_x(d)) for d in x_order]
    half = w_rows // 2
    upper, lower = pl.ds(0, half), pl.ds(half, half)

    def w_gather(view, ss, rs, at, to, count):
        return [copy(view, view, ss.at[d], rs.at[at], to(d)) for d in range(1, count)]

    wa_copies = w_gather(wbuf.at[:, y, x, upper], wa_s, wa_r, x, on_x, nx)
    wb_copies = w_gather(wbuf.at[:, y, x, lower], wb_s, wb_r, y, on_y, ny)
    def w_parts(view, ss, rs, fs, fr, at, to, count):
        near = sorted({1, count - 1})
        assert count in (2, 4)
        mine = [
            [copy(view(i, at(0)), view(i, at(0)), ss.at[i, d], rs.at[i, d], to(d)) for d in near]
            for i in range(3)
        ]

        def came(i):
            for d in near:
                arrived(view(i, at(count - d)), rs.at[i, d])

        onward = []
        for i in range(3):
            onward.append([])
            for d in near if count == 4 else ():
                part = view(i, at(count - d), d != 1)
                onward[i].append(copy(part, part, fs.at[i, d], fr.at[i, d], to(d)))

        def came_onward(i):
            for d in near if count == 4 else ():
                arrived(view(i, at(2), d != 1), fr.at[i, d])

        return mine, came, onward, came_onward

    def pick_shards(count, part):
        middle = count // 2
        return slice(None) if part is None else pl.ds(middle * part, middle)

    def upper_view(i, j, part=None):
        return wbuf.at[i, j, pick_shards(nx, part), upper]

    def lower_view(i, j, part=None):
        return wbuf.at[i, pick_shards(ny, part), j, lower]

    wc_copies, wc_came, wc_onward, wc_done = w_parts(
        upper_view, wc_s, wc_r, we_s, we_r, y_at, on_y, ny
    )
    wd_copies, wd_came, wd_onward, wd_done = w_parts(
        lower_view, wd_s, wd_r, wf_s, wf_r, x_at, on_x, nx
    )
    cache_slot = kv.at[cached(y), :]
    cache_copies = [copy(cache_slot, cache_slot, c_s.at[d], c_r.at[y], on_y(d)) for d in y_order]
    p_copies = by_wave(
        lambda v: [
            copy(psend.at[v, y_at(d)], precv.at[v, y], p_s.at[v, d], p_r.at[v, y], on_y(d))
            for d in y_order
        ]
    )
    q_copies = by_wave(
        lambda v: [
            copy(qg.at[v, x], qg.at[v, x], q_s.at[v, d], q_r.at[v, x], on_x(d))
            for d in x_order
        ]
    )
    kv_copies = by_wave(
        lambda v: [
            copy(
                kv.at[freshly(v, y), :],
                kv.at[freshly(v, y), :],
                kv_s.at[v, d],
                kv_r.at[v, y],
                on_y(d),
            )
            for d in y_order
        ]
    )
    num_copies = by_wave(
        lambda v: [
            copy(nsend.at[v, x_at(d)], nrecv.at[v, x], n_s.at[v, d], n_r.at[v, x], on_x(d))
            for d in x_order
        ]
    )
    a_copies = by_wave(
        lambda v: [
            copy(ag.at[v, z], ag.at[v, z], ag_s.at[v, d], ag_r.at[v, z], on_z(d))
            for d in z_order
        ]
    )
    r_copies = [
        copy(rsend.at[x_at(d)], rrecv.at[x], r_s.at[d], r_r.at[x], on_x(d)) for d in x_order
    ]

    @pl.when(sec == 0)
    def _():
        own_x.start()

    for c in own_places + [own_w] + own_cache + own_scales + [own_wo]:
        c.start()

    barrier = pltpu.get_barrier_semaphore()

    def greet(dev):
        pl.semaphore_signal(barrier, inc=1, device_id=dev, device_id_type=MESH)

    partners = (
        [on_z(d) for d in range(1, nz)]
        + [on_y(d) for d in range(1, ny)]
        + [on_x(d) for d in range(1, nx)]
    )
    for dev in partners:
        greet(dev)

    def is_own(i, b):
        return (y == i) & (z == y * hz + b)

    @pl.when(sec == 0)
    def _():
        for i in range(ny):
            for b in range(hz):

                @pl.when(jnp.logical_not(is_own(i, b)))
                def _():
                    greet((0, y * hz + b, i * nx + x))

    @pl.when(sec == 1)
    def _():
        for d in range(nz):
            greet((0, z_at(d), seq))

    for c in own_places:
        c.wait()
    places = [order[s] for s in range(steps)]
    begins = [sum(jnp.where(places[s] == p, start[p], 0) for p in range(steps)) for s in range(steps)]

    lane_rows = lax.broadcasted_iota(jnp.int32, (steps * tok, head_dim), 1)

    def shard_stats(value):
        middle = jnp.sum(value, axis=-1, keepdims=True) * (1.0 / feat)
        value = value - middle
        square = jnp.sum(value * value, axis=-1, keepdims=True)
        both = jnp.where(lane_rows == 0, middle, jnp.where(lane_rows == 1, square, 0.0))
        both = jnp.concatenate([both, jnp.zeros((head_dim - steps * tok, head_dim), F32)], axis=0)
        st_send[...] = jnp.transpose(both)[0:8, :]

    @pl.when(sec == 0)
    def _():
        own_x.wait()
        value = x_rows[...].astype(F32)
        parts = [value[p * tok : (p + 1) * tok] for p in range(steps)]
        value = []
        for s in range(steps):
            chosen = parts[0]
            for p in range(1, steps):
                chosen = jnp.where(places[s] == p, parts[p], chosen)
            value.append(chosen)
        value = jnp.concatenate(value, axis=0)
        own[...] = value.astype(BF16).reshape(waves, rows, feat)
        shard_stats(value)
        st_recv[z] = st_send[...]
        pl.semaphore_wait(barrier, len(partners) + 2 * nz - jnp.where(hy == y, 1, 0))
        own_w.wait()
        for c in w_copies + first_st:
            c.start()
        for v in range(waves):
            for c in first_x[v][1:]:
                c.start()

            @pl.when(hy == y)
            def _():
                xr[v, y, lax.rem(z, hz)] = own[v]

            @pl.when(hy != y)
            def _():
                first_x[v][0].start()

    @pl.when(sec == 1)
    def _():
        own_w.wait()

    for c in own_cache:
        c.wait()

    @pl.when(sec == 0)
    def _():
        for c in cache_copies:
            c.start()

    @pl.when(sec == 1)
    def _():
        pl.semaphore_wait(barrier, len(partners))
        for c in wb_copies:
            c.start()
        pl.semaphore_wait(go.at[0], 1)
        for c in wa_copies:
            c.start()
        for d in range(1, ny):
            arrived(wbuf.at[:, y_at(d), x, lower], wb_r.at[y_at(d)])
        for c in wd_copies[1]:
            c.start()
        for d in range(1, nx):
            arrived(wbuf.at[:, y, x_at(d), upper], wa_r.at[x_at(d)])
        wd_came(1)
        for c in wd_onward[1]:
            c.start()
        pl.semaphore_wait(go.at[1], 1)
        for c in wc_copies[1]:
            c.start()
        pl.semaphore_wait(go.at[2], 1)
        for c in wd_copies[2] + wc_copies[2] + wd_copies[0] + wc_copies[0]:
            c.start()
        wc_came(1)
        for c in wc_onward[1]:
            c.start()
        wd_came(2)
        for c in wd_onward[2]:
            c.start()
        wc_came(2)
        for c in wc_onward[2]:
            c.start()
        wd_came(0)
        for c in wd_onward[0]:
            c.start()
        wc_came(0)
        for c in wc_onward[0]:
            c.start()
        for c in cache_copies:
            c.start()

    def covers(s, pos):
        return (begins[s] <= pos) & (pos < begins[s] + span)

    def first_from(step, pos):
        found = steps
        for s in reversed(range(step, steps)):
            found = jnp.where(covers(s, pos), s, found)
        return found

    lane = lax.broadcasted_iota(jnp.int32, (tok, head_dim), 1)
    lane_chunk = lax.broadcasted_iota(jnp.int32, (chunk, head_dim), 1)
    for j in range(ny):
        upto = first_from(0, (j * nx + x) * chunk)
        value = jnp.where(lane_chunk < upto, 0.0, FAR)
        bias[j * chunk : (j + 1) * chunk, :] = value.astype(BF16)
        for v in range(waves):
            parts = []
            for s in range(v * per_wave, (v + 1) * per_wave):
                upto = first_from(s + 1, begins[s] + j * chunk)
                parts.append(jnp.where((lane >= s) & (lane < upto), 0.0, FAR))
            at = stale + v * fresh + j * rows
            bias[at : at + rows, :] = jnp.concatenate(parts, axis=0).astype(BF16)

    for c in own_scales:
        c.wait()

    def rms_heads(value, which):
        out = []
        for h in range(heads):
            part = value[:, h * head_dim : (h + 1) * head_dim]
            power = jnp.sum(part * part, axis=-1, keepdims=True) * (1.0 / head_dim)
            out.append(part * lax.rsqrt(power + 1e-06) * gain[which : which + 1, :])
        return jnp.concatenate(out, axis=-1).astype(BF16)

    def spread_keys(v, key, value):
        kv[freshly(v, y), 0:feat] = rms_heads(key, 1)
        kv[freshly(v, y), feat : 2 * feat] = value.astype(BF16)
        for c in kv_copies[v]:
            c.start()

    def spread_queries(v, query):
        qg[v, x] = rms_heads(query, 0)
        for c in q_copies[v]:
            c.start()

    @pl.when(sec == 0)
    def _():
        for d in range(1, nz):
            arrived(st_recv.at[z_at(d)], st_r.at[z_at(d)])
        middles = [st_recv[i, 0:1, :] for i in range(nz)]
        mean = sum(middles) * (1.0 / nz)
        square = sum(st_recv[i, 1:2, :] for i in range(nz))
        square += sum((m - mean) * (m - mean) for m in middles) * feat
        scale = lax.rsqrt(square * (1.0 / width) + 1e-06)
        line = lax.broadcasted_iota(jnp.int32, (8, head_dim), 0)
        value = jnp.where(line == 0, mean, jnp.where(line == 1, scale, 0.0))
        st_norm[...] = value
        st_all[y] = value
        for c in sn_copies:
            c.start()
        for d in range(1, ny):
            arrived(st_all.at[y_at(d)], sn_r.at[y_at(d)])
        value = st_all[...].reshape(8 * ny, head_dim)
        value = jnp.concatenate([value, jnp.zeros((head_dim - 8 * ny, head_dim), F32)], axis=0)
        stats = jnp.transpose(value)
        for v in range(waves):
            for i in range(ny):
                mean = stats[v * rows : (v + 1) * rows, 8 * i : 8 * i + 1]
                scale = stats[v * rows : (v + 1) * rows, 8 * i + 1 : 8 * i + 2]
                for b in range(hz):

                    @pl.when(jnp.logical_not(is_own(i, b)))
                    def _():
                        arrived(xr.at[v, i, b], x_r.at[v, i, b])

                    at = pl.ds(pl.multiple_of((y * hz + b) * feat, feat), feat)
                    value = (xr[v, i, b].astype(F32) - mean) * scale
                    value = value * (1.0 + mod[1, :, at]) + mod[0, :, at]
                    xe[v, i, :, b * feat : (b + 1) * feat] = value.astype(BF16)
            if v == 0:
                for d in range(1, nx):
                    arrived(wbuf.at[:, y, x_at(d)], w_r.at[x_at(d)])
                pl.semaphore_signal(go.at[0], inc=1, device_id=other, device_id_type=MESH)
            tokens = xe[v].reshape(ny * rows, hz * feat)
            for i in range(3):
                weights = wbuf[i, y].reshape(nx * w_rows, feat)
                value = jnp.dot(tokens, weights, preferred_element_type=F32)
                psend[v, :, :, i * feat : (i + 1) * feat] = value.astype(BF16).reshape(
                    ny, rows, feat
                )
            for c in p_copies[v]:
                c.start()
        for v in range(waves):
            value = psend[v, y].astype(F32)
            for d in range(1, ny):
                arrived(precv.at[v, y_at(d)], p_r.at[v, y_at(d)])
                value += precv[v, y_at(d)].astype(F32)
            spread_keys(v, value[:, feat : 2 * feat], value[:, 2 * feat :])
            spread_queries(v, value[:, 0:feat])

    @pl.when(sec == 1)
    def _():
        for v in range(waves):
            for i in range(nz):
                arrived(xg.at[v, i], h_r.at[v, i])
            own[v] = xg[v, z]
            total = jnp.zeros((rows, feat), F32)
            for i in range(nz):
                total += xg[v, i].astype(F32)
            mean = jnp.sum(total, axis=-1, keepdims=True) * (1.0 / width)
            total = jnp.zeros((rows, feat), F32)
            for i in range(nz):
                diff = xg[v, i].astype(F32) - mean
                total += diff * diff
            scale = lax.rsqrt(jnp.sum(total, axis=-1, keepdims=True) * (1.0 / width) + 1e-06)
            for i in range(nz):
                at = slice(i * feat, (i + 1) * feat)
                value = (xg[v, i].astype(F32) - mean) * scale
                value = value * (1.0 + mod[1, :, at]) + mod[0, :, at]
                xn[v, :, at] = value.astype(BF16)
            parts = [None] * 3
            for i in (1, 2, 0):
                if v == 0:
                    wc_done(i)
                    wd_done(i)
                weights = wbuf[i].reshape(width, feat)
                parts[i] = jnp.dot(xn[v], weights, preferred_element_type=F32)
                if i == 2:
                    spread_keys(v, parts[1], parts[2])
            spread_queries(v, parts[0])

    for d in range(1, ny):
        arrived(kv.at[cached(y_at(d)), :], c_r.at[y_at(d)])
    lane_all = lax.broadcasted_iota(jnp.int32, (nx * rows, head_dim), 1)
    lane_tok = lax.broadcasted_iota(jnp.int32, (tok, head_dim), 1)
    exponent = math.log2(math.e) / math.sqrt(head_dim)
    for v in range(waves):
        for d in range(1, ny):
            arrived(kv.at[freshly(v, y_at(d)), :], kv_r.at[v, y_at(d)])
        for d in range(1, nx):
            arrived(qg.at[v, x_at(d)], q_r.at[v, x_at(d)])

        if v == waves - 1:

            @pl.when(sec == 0)
            def _():
                pl.semaphore_signal(go.at[1], inc=1, device_id=other, device_id_type=MESH)

        keys_now = stale + (v + 1) * fresh
        tags = [
            jnp.where(lane_tok == s, 1.0, 0.0) for s in range(v * per_wave, (v + 1) * per_wave)
        ]
        tags = jnp.concatenate(tags * nx, axis=0).astype(BF16)
        sums = jnp.zeros((nx * rows, head_dim), F32)
        for h in range(heads):
            at = slice(h * head_dim, (h + 1) * head_dim)
            queries = jnp.concatenate([qg[v, :, :, at].reshape(nx * rows, head_dim), tags], axis=1)
            keys = jnp.concatenate([kv[0:keys_now, at], bias[0:keys_now, :]], axis=1)
            scores = lax.dot_general(
                queries, keys, (((1,), (1,)), ((), ())), preferred_element_type=F32
            )
            weight = jnp.exp2(scores * exponent)
            denom = jnp.sum(weight, axis=-1, keepdims=True)
            values = kv[0:keys_now, feat + h * head_dim : feat + (h + 1) * head_dim]
            numer = jnp.dot(weight.astype(BF16), values, preferred_element_type=F32)
            nsend[v, :, :, at] = numer.astype(BF16).reshape(nx, rows, head_dim)
            high = denom.astype(BF16).astype(F32)
            sums = jnp.where(lane_all == 2 * h, high, sums)
            sums = jnp.where(lane_all == 2 * h + 1, denom - high, sums)
        nsend[v, :, :, feat:] = sums.astype(BF16).reshape(nx, rows, head_dim)
        for c in num_copies[v]:
            c.start()

    @pl.when(sec == 0)
    def _():
        pl.semaphore_signal(go.at[2], inc=1, device_id=other, device_id_type=MESH)

    for v in range(waves):
        total = nsend[v, x].astype(F32)
        for d in range(1, nx):
            arrived(nrecv.at[v, x_at(d)], n_r.at[v, x_at(d)])
            total += nrecv[v, x_at(d)].astype(F32)
        parts = []
        for h in range(heads):
            at = feat + 2 * h
            denom = total[:, at : at + 1] + total[:, at + 1 : at + 2]
            parts.append(total[:, h * head_dim : (h + 1) * head_dim] / denom)
        ag[v, z] = jnp.concatenate(parts, axis=1).astype(BF16)
        for c in a_copies[v]:
            c.start()

    def source(c):
        pos = c * chunk
        first_row = -waves * fresh - pad
        for s in range(steps):
            row = (s // per_wave) * fresh + (s % per_wave) * tok
            row += (pos - begins[s]) // chunk * rows
            first_row = jnp.where(covers(s, pos), row, first_row)
        return first_row

    in_row = lax.broadcasted_iota(jnp.int32, (pad, waves * fresh), 0)
    in_col = lax.broadcasted_iota(jnp.int32, (pad, waves * fresh), 1)
    picks = []
    for c in range(nx):
        hit = (in_col - in_row == source(y * nx + c)) & (in_row < tok)
        picks.append(jnp.where(hit, 1.0, 0.0).astype(BF16))
    pick = jnp.concatenate(picks, axis=0)
    value = jnp.dot(pick, kv[stale:, :], preferred_element_type=F32)
    rsend[...] = value.astype(BF16).reshape(nx, pad, 2 * feat)
    for c in r_copies:
        c.start()

    def refresh():
        for d in range(1, nx):
            arrived(rrecv.at[x_at(d)], r_r.at[x_at(d)])
        rrecv[x] = rsend[x]
        out_row = lax.broadcasted_iota(jnp.int32, (chunk, nx * pad), 0)
        out_col = lax.broadcasted_iota(jnp.int32, (chunk, nx * pad), 1)
        block = out_col // pad
        within = out_col - block * pad
        hit = (out_row == block * tok + within) & (within < tok)
        place = jnp.where(hit, 1.0, 0.0).astype(BF16)
        written_to = source(seq) >= 0
        value = jnp.dot(place, rrecv[...].reshape(nx * pad, 2 * feat), preferred_element_type=F32)
        value = jnp.where(written_to, value, kv[cached(y), :].astype(F32)).astype(BF16)
        nk[...] = value[:, 0:feat]
        nv[...] = value[:, feat:]

    pl.when(sec == 1)(refresh)
    own_wo.wait()
    gate = mod[2, :, pl.ds(pl.multiple_of(z * feat, feat), feat)]
    results = []
    for v in range(waves):
        result = jnp.zeros((rows, feat), F32)
        for d in [0] + z_order[::-1]:
            if d:
                arrived(ag.at[v, z_at(d)], ag_r.at[v, z_at(d)])
            at = pl.ds(pl.multiple_of(z_at(d) * feat, feat), feat)
            result += jnp.dot(ag[v, z_at(d)], wo_v[at, :], preferred_element_type=F32)
        result = (own[v].astype(F32) + gate * result).astype(BF16)
        done[v] = result
        results.append(result.astype(F32))

        @pl.when(sec == 0)
        def _():
            for c in next_x[v]:
                c.start()

    result = jnp.concatenate(results, axis=0)
    parts = [result[s * tok : (s + 1) * tok] for s in range(steps)]
    value = []
    for p in range(steps):
        chosen = parts[0]
        for s in range(1, steps):
            chosen = jnp.where(places[s] == p, parts[s], chosen)
        value.append(chosen)
    bo[...] = jnp.concatenate(value, axis=0).astype(BF16)

    pl.when(sec == 0)(refresh)

    @pl.when(sec == 0)
    def _():
        for c in first_st + sn_copies + w_copies + sum(next_x + p_copies, []):
            c.wait_send()
        for v in range(waves):
            for c in first_x[v][1:]:
                c.wait_send()

            @pl.when(hy != y)
            def _():
                first_x[v][0].wait_send()

    @pl.when(sec == 1)
    def _():
        for c in wa_copies + wb_copies + sum(wc_copies + wd_copies + wc_onward + wd_onward, []):
            c.wait_send()

    for c in cache_copies + r_copies + sum(q_copies + kv_copies + num_copies + a_copies, []):
        c.wait_send()


def write_kernel(*refs):
    half = len(refs) // 2
    for src, dst in zip(refs[:half], refs[half:]):
        dst[...] = src[...]


def written(*arrays):
    vmem = pl.BlockSpec(memory_space=pltpu.VMEM)
    return pl.pallas_call(
        write_kernel,
        name="write",
        out_shape=tuple(jax.ShapeDtypeStruct(a.shape, a.dtype) for a in arrays),
        in_specs=[vmem] * len(arrays),
        out_specs=(vmem,) * len(arrays),
        compiler_params=pltpu.CompilerParams(vmem_limit_bytes=60 << 20),
    )(*arrays)


def per_device(
    patches, cache_k, cache_v, w_qkv, w_out, modulation, qk_gain, patch_order, patch_start
):
    nz = lax.axis_size("head")
    ny = nx = square_side(lax.axis_size("seq"))
    count, tok, feat = patches.shape
    chunk = cache_k.shape[1]
    head_dim = qk_gain.shape[-1]
    waves = 2
    per_wave = count // waves
    rows = per_wave * tok
    hz = nz // ny
    w_rows = w_qkv.shape[1]
    pad = -(-tok // 16) * 16
    keys = ny * (waves * rows + chunk)
    dma = pltpu.SemaphoreType.DMA
    vmem = pl.BlockSpec(memory_space=pltpu.VMEM)
    hbm = pl.BlockSpec(memory_space=pl.ANY)
    out, new_k, new_v = pl.pallas_call(
        functools.partial(block_kernel, nz, ny, nx, tok, waves, per_wave, head_dim),
        name="blocks",
        out_shape=(
            jax.ShapeDtypeStruct((count * tok, feat), BF16),
            jax.ShapeDtypeStruct((chunk, feat), BF16),
            jax.ShapeDtypeStruct((chunk, feat), BF16),
        ),
        in_specs=[hbm] * 9,
        out_specs=(vmem, vmem, vmem),
        scratch_shapes=[
            pltpu.SMEM((count,), jnp.int32),
            pltpu.SMEM((count,), jnp.int32),
            pltpu.VMEM((3, 1, nz * feat), F32),
            pltpu.VMEM((2, head_dim), F32),
            pltpu.VMEM((count * tok, feat), BF16),
            pltpu.VMEM((waves, rows, feat), BF16),
            pltpu.VMEM((waves, rows, feat), BF16),
            pltpu.VMEM((waves, ny, hz, rows, feat), BF16),
            pltpu.VMEM((waves, ny, rows, hz * feat), BF16),
            pltpu.VMEM((waves, nz, rows, feat), BF16),
            pltpu.VMEM((waves, rows, nz * feat), BF16),
            pltpu.VMEM((8, head_dim), F32),
            pltpu.VMEM((nz, 8, head_dim), F32),
            pltpu.VMEM((8, head_dim), F32),
            pltpu.VMEM((ny, 8, head_dim), F32),
            pltpu.VMEM((3, ny, nx, w_rows, feat), BF16),
            pltpu.VMEM((nz * feat, feat), BF16),
            pltpu.VMEM((waves, ny, rows, 3 * feat), BF16),
            pltpu.VMEM((waves, ny, rows, 3 * feat), BF16),
            pltpu.VMEM((waves, nx, rows, feat), BF16),
            pltpu.VMEM((keys, 2 * feat), BF16),
            pltpu.VMEM((keys, head_dim), BF16),
            pltpu.VMEM((waves, nx, rows, feat + head_dim), BF16),
            pltpu.VMEM((waves, nx, rows, feat + head_dim), BF16),
            pltpu.VMEM((waves, nz, rows, feat), BF16),
            pltpu.VMEM((nx, pad, 2 * feat), BF16),
            pltpu.VMEM((nx, pad, 2 * feat), BF16),
            dma((9,)),
            dma((waves, nz)),
            dma((waves, ny, hz)),
            dma((nz,)),
            dma((nz,)),
            dma((ny,)),
            dma((ny,)),
            dma((waves, nz)),
            dma((waves, nz)),
            dma((nx,)),
            dma((nx,)),
            dma((nx,)),
            dma((nx,)),
            dma((ny,)),
            dma((ny,)),
            dma((3, ny)),
            dma((3, ny)),
            dma((3, nx)),
            dma((3, nx)),
            dma((3, ny)),
            dma((3, ny)),
            dma((3, nx)),
            dma((3, nx)),
            dma((ny,)),
            dma((ny,)),
            dma((waves, ny)),
            dma((waves, ny)),
            dma((waves, nx)),
            dma((waves, nx)),
            dma((waves, ny)),
            dma((waves, ny)),
            dma((waves, nx)),
            dma((waves, nx)),
            dma((waves, nz)),
            dma((waves, nz)),
            dma((nx,)),
            dma((nx,)),
            pltpu.SemaphoreType.REGULAR((3,)),
        ],
        compiler_params=pltpu.CompilerParams(
            collective_id=0, has_side_effects=True, vmem_limit_bytes=60 << 20
        ),
    )(
        patch_order,
        patch_start,
        patches.reshape(count * tok, feat),
        cache_k[0],
        cache_v[0],
        jnp.transpose(w_qkv[0], (1, 0, 2)),
        w_out[0],
        jnp.transpose(modulation, (1, 0, 2)),
        qk_gain[0],
    )
    out, new_k, new_v = written(out, new_k, new_v)
    return (out.reshape(1, count, tok, feat), new_k[None], new_v[None])


def solution(mesh):
    return jax.shard_map(
        per_device,
        mesh=mesh,
        in_specs=(
            P(None, "seq", "head"),
            P("section", "seq", "head"),
            P("section", "seq", "head"),
            P("section", "seq", None, "head"),
            P("section", None, "head"),
            P("section", None, None),
            P("section", None, None),
            P(),
            P(),
        ),
        out_specs=(
            P("section", None, "seq", "head"),
            P("section", "seq", "head"),
            P("section", "seq", "head"),
        ),
        check_vma=False,
    )
```

```python
import functools
import math

import jax
import jax.numpy as jnp
from jax import lax
from jax.experimental import pallas as pl
from jax.experimental.pallas import tpu as pltpu
from jax.sharding import PartitionSpec as P

MESH = pl.DeviceIdType.MESH
F32 = jnp.float32
BF16 = jnp.bfloat16
FAR = -1e30


def square_side(count):
    side = math.isqrt(count)
    assert side * side == count
    return side


def block_kernel(
    nz,
    ny,
    nx,
    tok,
    waves,
    per_wave,
    head_dim,
    order_h,
    start_h,
    x_in,
    ck,
    cv,
    w,
    wo,
    mod_h,
    gain_h,
    bo,
    nk,
    nv,
    order,
    start,
    mod,
    gain,
    x_rows,
    own,
    done,
    xr,
    xe,
    xg,
    xn,
    st_send,
    st_recv,
    st_norm,
    st_all,
    wbuf,
    wo_v,
    psend,
    precv,
    qg,
    kv,
    bias,
    nsend,
    nrecv,
    ag,
    rsend,
    rrecv,
    loc,
    x_s,
    x_r,
    st_s,
    st_r,
    sn_s,
    sn_r,
    h_s,
    h_r,
    w_s,
    w_r,
    wa_s,
    wa_r,
    wb_s,
    wb_r,
    wc_s,
    wc_r,
    wd_s,
    wd_r,
    we_s,
    we_r,
    wf_s,
    wf_r,
    c_s,
    c_r,
    p_s,
    p_r,
    q_s,
    q_r,
    kv_s,
    kv_r,
    n_s,
    n_r,
    ag_s,
    ag_r,
    r_s,
    r_r,
    go,
):
    sec = lax.axis_index("section")
    z = lax.axis_index("head")
    seq = lax.axis_index("seq")
    y = seq // nx
    x = lax.rem(seq, nx)
    _, rows, feat = own.shape
    chunk = ck.shape[0]
    heads = feat // head_dim
    width = nz * feat
    w_rows = w.shape[1]
    hz = nz // ny
    hy = z // hz
    steps = waves * per_wave
    stale = ny * chunk
    fresh = ny * rows
    span = ny * chunk
    pad = rrecv.shape[1]

    def z_at(d):
        return lax.rem(z + d, nz)

    def y_at(d):
        return lax.rem(y + d, ny)

    def x_at(d):
        return lax.rem(x + d, nx)

    def on_z(d):
        return (sec, z_at(d), seq)

    def on_y(d):
        return (sec, z, y_at(d) * nx + x)

    def on_x(d):
        return (sec, z, y * nx + x_at(d))

    other = (1 - sec, z, seq)
    z_order = sorted(range(1, nz), key=lambda d: -min(d, nz - d))
    y_order = sorted(range(1, ny), key=lambda d: -min(d, ny - d))
    x_order = sorted(range(1, nx), key=lambda d: -min(d, nx - d))

    def copy(src, dst, ss, rs, dev):
        return pltpu.make_async_remote_copy(
            src_ref=src, dst_ref=dst, send_sem=ss, recv_sem=rs, device_id=dev, device_id_type=MESH
        )

    def arrived(dst, rs):
        copy(dst, dst, rs, rs, other).wait_recv()

    def cached(i):
        return pl.ds(pl.multiple_of(i * chunk, chunk), chunk)

    def freshly(v, i):
        return pl.ds(pl.multiple_of(stale + v * fresh + i * rows, rows), rows)

    w_slot = wbuf.at[:, y, x]
    own_x = pltpu.make_async_copy(x_in, x_rows, loc.at[0])
    own_w = pltpu.make_async_copy(w, w_slot, loc.at[1])
    own_cache = [
        pltpu.make_async_copy(ck, kv.at[cached(y), 0:feat], loc.at[2]),
        pltpu.make_async_copy(cv, kv.at[cached(y), feat : 2 * feat], loc.at[3]),
    ]
    own_places = [
        pltpu.make_async_copy(order_h, order, loc.at[4]),
        pltpu.make_async_copy(start_h, start, loc.at[5]),
    ]
    own_scales = [
        pltpu.make_async_copy(mod_h, mod, loc.at[6]),
        pltpu.make_async_copy(gain_h, gain, loc.at[7]),
    ]
    own_wo = pltpu.make_async_copy(wo, wo_v, loc.at[8])

    def by_wave(make):
        return [make(v) for v in range(waves)]

    first_x = by_wave(
        lambda v: [
            copy(
                own.at[v],
                xr.at[v, y, lax.rem(z, hz)],
                x_s.at[v, d],
                x_r.at[v, y, lax.rem(z, hz)],
                (0, z_at(d), hy * nx + x),
            )
            for d in [0] + z_order
        ]
    )
    first_st = [
        copy(st_send, st_recv.at[z], st_s.at[d], st_r.at[z], on_z(d)) for d in z_order
    ]
    next_x = by_wave(
        lambda v: [
            copy(done.at[v], xg.at[v, z], h_s.at[v, d], h_r.at[v, z], (1, z_at(d), seq))
            for d in [0] + z_order
        ]
    )
    sn_copies = [
        copy(st_norm, st_all.at[y], sn_s.at[d], sn_r.at[y], on_y(d)) for d in y_order
    ]
    w_copies = [copy(w_slot, w_slot, w_s.at[d], w_r.at[x], on_x(d)) for d in x_order]
    half = w_rows // 2
    upper, lower = pl.ds(0, half), pl.ds(half, half)

    def w_gather(view, ss, rs, at, to, count):
        return [copy(view, view, ss.at[d], rs.at[at], to(d)) for d in range(1, count)]

    wa_copies = w_gather(wbuf.at[:, y, x, upper], wa_s, wa_r, x, on_x, nx)
    wb_copies = w_gather(wbuf.at[:, y, x, lower], wb_s, wb_r, y, on_y, ny)
    def w_parts(view, ss, rs, fs, fr, at, to, count):
        near = sorted({1, count - 1})
        assert count in (2, 4)
        mine = [
            [copy(view(i, at(0)), view(i, at(0)), ss.at[i, d], rs.at[i, d], to(d)) for d in near]
            for i in range(3)
        ]

        def came(i):
            for d in near:
                arrived(view(i, at(count - d)), rs.at[i, d])

        onward = []
        for i in range(3):
            onward.append([])
            for d in near if count == 4 else ():
                part = view(i, at(count - d), d != 1)
                onward[i].append(copy(part, part, fs.at[i, d], fr.at[i, d], to(d)))

        def came_onward(i):
            for d in near if count == 4 else ():
                arrived(view(i, at(2), d != 1), fr.at[i, d])

        return mine, came, onward, came_onward

    def pick_shards(count, part):
        middle = count // 2
        return slice(None) if part is None else pl.ds(middle * part, middle)

    def upper_view(i, j, part=None):
        return wbuf.at[i, j, pick_shards(nx, part), upper]

    def lower_view(i, j, part=None):
        return wbuf.at[i, pick_shards(ny, part), j, lower]

    wc_copies, wc_came, wc_onward, wc_done = w_parts(
        upper_view, wc_s, wc_r, we_s, we_r, y_at, on_y, ny
    )
    wd_copies, wd_came, wd_onward, wd_done = w_parts(
        lower_view, wd_s, wd_r, wf_s, wf_r, x_at, on_x, nx
    )
    cache_slot = kv.at[cached(y), :]
    cache_copies = [copy(cache_slot, cache_slot, c_s.at[d], c_r.at[y], on_y(d)) for d in y_order]
    p_copies = by_wave(
        lambda v: [
            copy(psend.at[v, y_at(d)], precv.at[v, y], p_s.at[v, d], p_r.at[v, y], on_y(d))
            for d in y_order
        ]
    )
    q_copies = by_wave(
        lambda v: [
            copy(qg.at[v, x], qg.at[v, x], q_s.at[v, d], q_r.at[v, x], on_x(d))
            for d in x_order
        ]
    )
    kv_copies = by_wave(
        lambda v: [
            copy(
                kv.at[freshly(v, y), :],
                kv.at[freshly(v, y), :],
                kv_s.at[v, d],
                kv_r.at[v, y],
                on_y(d),
            )
            for d in y_order
        ]
    )
    num_copies = by_wave(
        lambda v: [
            copy(nsend.at[v, x_at(d)], nrecv.at[v, x], n_s.at[v, d], n_r.at[v, x], on_x(d))
            for d in x_order
        ]
    )
    a_copies = by_wave(
        lambda v: [
            copy(ag.at[v, z], ag.at[v, z], ag_s.at[v, d], ag_r.at[v, z], on_z(d))
            for d in z_order
        ]
    )
    r_copies = [
        copy(rsend.at[x_at(d)], rrecv.at[x], r_s.at[d], r_r.at[x], on_x(d)) for d in x_order
    ]

    @pl.when(sec == 0)
    def _():
        own_x.start()

    for c in own_places + [own_w] + own_cache + own_scales + [own_wo]:
        c.start()

    barrier = pltpu.get_barrier_semaphore()

    def greet(dev):
        pl.semaphore_signal(barrier, inc=1, device_id=dev, device_id_type=MESH)

    partners = (
        [on_z(d) for d in range(1, nz)]
        + [on_y(d) for d in range(1, ny)]
        + [on_x(d) for d in range(1, nx)]
    )
    for dev in partners:
        greet(dev)

    def is_own(i, b):
        return (y == i) & (z == y * hz + b)

    @pl.when(sec == 0)
    def _():
        for i in range(ny):
            for b in range(hz):

                @pl.when(jnp.logical_not(is_own(i, b)))
                def _():
                    greet((0, y * hz + b, i * nx + x))

    @pl.when(sec == 1)
    def _():
        for d in range(nz):
            greet((0, z_at(d), seq))

    for c in own_places:
        c.wait()
    places = [order[s] for s in range(steps)]
    begins = [sum(jnp.where(places[s] == p, start[p], 0) for p in range(steps)) for s in range(steps)]

    lane_rows = lax.broadcasted_iota(jnp.int32, (steps * tok, head_dim), 1)

    def shard_stats(value):
        middle = jnp.sum(value, axis=-1, keepdims=True) * (1.0 / feat)
        value = value - middle
        square = jnp.sum(value * value, axis=-1, keepdims=True)
        both = jnp.where(lane_rows == 0, middle, jnp.where(lane_rows == 1, square, 0.0))
        both = jnp.concatenate([both, jnp.zeros((head_dim - steps * tok, head_dim), F32)], axis=0)
        st_send[...] = jnp.transpose(both)[0:8, :]

    @pl.when(sec == 0)
    def _():
        own_x.wait()
        value = x_rows[...].astype(F32)
        parts = [value[p * tok : (p + 1) * tok] for p in range(steps)]
        value = []
        for s in range(steps):
            chosen = parts[0]
            for p in range(1, steps):
                chosen = jnp.where(places[s] == p, parts[p], chosen)
            value.append(chosen)
        value = jnp.concatenate(value, axis=0)
        own[...] = value.astype(BF16).reshape(waves, rows, feat)
        shard_stats(value)
        st_recv[z] = st_send[...]
        pl.semaphore_wait(barrier, len(partners) + 2 * nz - jnp.where(hy == y, 1, 0))
        own_w.wait()
        for c in w_copies + first_st:
            c.start()
        for v in range(waves):
            for c in first_x[v][1:]:
                c.start()

            @pl.when(hy == y)
            def _():
                xr[v, y, lax.rem(z, hz)] = own[v]

            @pl.when(hy != y)
            def _():
                first_x[v][0].start()

    @pl.when(sec == 1)
    def _():
        own_w.wait()

    for c in own_cache:
        c.wait()

    @pl.when(sec == 1)
    def _():
        pl.semaphore_wait(barrier, len(partners))
        for c in wb_copies:
            c.start()
        pl.semaphore_wait(go.at[0], 1)
        for c in wa_copies:
            c.start()
        for d in range(1, ny):
            arrived(wbuf.at[:, y_at(d), x, lower], wb_r.at[y_at(d)])
        for c in wd_copies[1]:
            c.start()
        for d in range(1, nx):
            arrived(wbuf.at[:, y, x_at(d), upper], wa_r.at[x_at(d)])
        wd_came(1)
        for c in wd_onward[1]:
            c.start()
        pl.semaphore_wait(go.at[1], 1)
        for c in wc_copies[1]:
            c.start()
        pl.semaphore_wait(go.at[2], 1)
        for c in wd_copies[2] + wc_copies[2] + wd_copies[0] + wc_copies[0]:
            c.start()
        wc_came(1)
        for c in wc_onward[1]:
            c.start()
        wd_came(2)
        for c in wd_onward[2]:
            c.start()
        wc_came(2)
        for c in wc_onward[2]:
            c.start()
        wd_came(0)
        for c in wd_onward[0]:
            c.start()
        wc_came(0)
        for c in wc_onward[0]:
            c.start()
        for c in cache_copies:
            c.start()

    def covers(s, pos):
        return (begins[s] <= pos) & (pos < begins[s] + span)

    def first_from(step, pos):
        found = steps
        for s in reversed(range(step, steps)):
            found = jnp.where(covers(s, pos), s, found)
        return found

    lane = lax.broadcasted_iota(jnp.int32, (tok, head_dim), 1)
    lane_chunk = lax.broadcasted_iota(jnp.int32, (chunk, head_dim), 1)
    for j in range(ny):
        upto = first_from(0, (j * nx + x) * chunk)
        value = jnp.where(lane_chunk < upto, 0.0, FAR)
        bias[j * chunk : (j + 1) * chunk, :] = value.astype(BF16)
        for v in range(waves):
            parts = []
            for s in range(v * per_wave, (v + 1) * per_wave):
                upto = first_from(s + 1, begins[s] + j * chunk)
                parts.append(jnp.where((lane >= s) & (lane < upto), 0.0, FAR))
            at = stale + v * fresh + j * rows
            bias[at : at + rows, :] = jnp.concatenate(parts, axis=0).astype(BF16)

    for c in own_scales:
        c.wait()

    def rms_heads(value, which):
        out = []
        for h in range(heads):
            part = value[:, h * head_dim : (h + 1) * head_dim]
            power = jnp.sum(part * part, axis=-1, keepdims=True) * (1.0 / head_dim)
            out.append(part * lax.rsqrt(power + 1e-06) * gain[which : which + 1, :])
        return jnp.concatenate(out, axis=-1).astype(BF16)

    def spread_keys(v, key, value):
        kv[freshly(v, y), 0:feat] = rms_heads(key, 1)
        kv[freshly(v, y), feat : 2 * feat] = value.astype(BF16)
        for c in kv_copies[v]:
            c.start()

    def spread_queries(v, query):
        qg[v, x] = rms_heads(query, 0)
        for c in q_copies[v]:
            c.start()

    @pl.when(sec == 0)
    def _():
        for d in range(1, nz):
            arrived(st_recv.at[z_at(d)], st_r.at[z_at(d)])
        middles = [st_recv[i, 0:1, :] for i in range(nz)]
        mean = sum(middles) * (1.0 / nz)
        square = sum(st_recv[i, 1:2, :] for i in range(nz))
        square += sum((m - mean) * (m - mean) for m in middles) * feat
        scale = lax.rsqrt(square * (1.0 / width) + 1e-06)
        line = lax.broadcasted_iota(jnp.int32, (8, head_dim), 0)
        value = jnp.where(line == 0, mean, jnp.where(line == 1, scale, 0.0))
        st_norm[...] = value
        st_all[y] = value
        for c in sn_copies:
            c.start()
        for d in range(1, ny):
            arrived(st_all.at[y_at(d)], sn_r.at[y_at(d)])
        for c in cache_copies:
            c.start()
        value = st_all[...].reshape(8 * ny, head_dim)
        value = jnp.concatenate([value, jnp.zeros((head_dim - 8 * ny, head_dim), F32)], axis=0)
        stats = jnp.transpose(value)
        for v in range(waves):
            for i in range(ny):
                mean = stats[v * rows : (v + 1) * rows, 8 * i : 8 * i + 1]
                scale = stats[v * rows : (v + 1) * rows, 8 * i + 1 : 8 * i + 2]
                for b in range(hz):

                    @pl.when(jnp.logical_not(is_own(i, b)))
                    def _():
                        arrived(xr.at[v, i, b], x_r.at[v, i, b])

                    at = pl.ds(pl.multiple_of((y * hz + b) * feat, feat), feat)
                    value = (xr[v, i, b].astype(F32) - mean) * scale
                    value = value * (1.0 + mod[1, :, at]) + mod[0, :, at]
                    xe[v, i, :, b * feat : (b + 1) * feat] = value.astype(BF16)
        for d in range(1, nx):
            arrived(wbuf.at[:, y, x_at(d)], w_r.at[x_at(d)])
        pl.semaphore_signal(go.at[0], inc=1, device_id=other, device_id_type=MESH)
        for v in range(waves):
            tokens = xe[v].reshape(ny * rows, hz * feat)
            for i in range(3):
                weights = wbuf[i, y].reshape(nx * w_rows, feat)
                value = jnp.dot(tokens, weights, preferred_element_type=F32)
                psend[v, :, :, i * feat : (i + 1) * feat] = value.astype(BF16).reshape(
                    ny, rows, feat
                )
            for c in p_copies[v]:
                c.start()
        for v in range(waves):
            value = psend[v, y].astype(F32)
            for d in range(1, ny):
                arrived(precv.at[v, y_at(d)], p_r.at[v, y_at(d)])
                value += precv[v, y_at(d)].astype(F32)
            spread_keys(v, value[:, feat : 2 * feat], value[:, 2 * feat :])
            spread_queries(v, value[:, 0:feat])

    @pl.when(sec == 1)
    def _():
        for v in range(waves):
            for i in range(nz):
                arrived(xg.at[v, i], h_r.at[v, i])
            own[v] = xg[v, z]
            total = jnp.zeros((rows, feat), F32)
            for i in range(nz):
                total += xg[v, i].astype(F32)
            mean = jnp.sum(total, axis=-1, keepdims=True) * (1.0 / width)
            total = jnp.zeros((rows, feat), F32)
            for i in range(nz):
                diff = xg[v, i].astype(F32) - mean
                total += diff * diff
            scale = lax.rsqrt(jnp.sum(total, axis=-1, keepdims=True) * (1.0 / width) + 1e-06)
            for i in range(nz):
                at = slice(i * feat, (i + 1) * feat)
                value = (xg[v, i].astype(F32) - mean) * scale
                value = value * (1.0 + mod[1, :, at]) + mod[0, :, at]
                xn[v, :, at] = value.astype(BF16)
            parts = [None] * 3
            for i in (1, 2, 0):
                if v == 0:
                    wc_done(i)
                    wd_done(i)
                weights = wbuf[i].reshape(width, feat)
                parts[i] = jnp.dot(xn[v], weights, preferred_element_type=F32)
                if i == 2:
                    spread_keys(v, parts[1], parts[2])
            spread_queries(v, parts[0])

    for d in range(1, ny):
        arrived(kv.at[cached(y_at(d)), :], c_r.at[y_at(d)])
    lane_all = lax.broadcasted_iota(jnp.int32, (nx * rows, head_dim), 1)
    lane_tok = lax.broadcasted_iota(jnp.int32, (tok, head_dim), 1)
    exponent = math.log2(math.e) / math.sqrt(head_dim)
    for v in range(waves):
        for d in range(1, ny):
            arrived(kv.at[freshly(v, y_at(d)), :], kv_r.at[v, y_at(d)])
        for d in range(1, nx):
            arrived(qg.at[v, x_at(d)], q_r.at[v, x_at(d)])

        if v == waves - 1:

            @pl.when(sec == 0)
            def _():
                pl.semaphore_signal(go.at[1], inc=1, device_id=other, device_id_type=MESH)

        keys_now = stale + (v + 1) * fresh
        tags = [
            jnp.where(lane_tok == s, 1.0, 0.0) for s in range(v * per_wave, (v + 1) * per_wave)
        ]
        tags = jnp.concatenate(tags * nx, axis=0).astype(BF16)
        sums = jnp.zeros((nx * rows, head_dim), F32)
        for h in range(heads):
            at = slice(h * head_dim, (h + 1) * head_dim)
            queries = jnp.concatenate([qg[v, :, :, at].reshape(nx * rows, head_dim), tags], axis=1)
            keys = jnp.concatenate([kv[0:keys_now, at], bias[0:keys_now, :]], axis=1)
            scores = lax.dot_general(
                queries, keys, (((1,), (1,)), ((), ())), preferred_element_type=F32
            )
            weight = jnp.exp2(scores * exponent)
            denom = jnp.sum(weight, axis=-1, keepdims=True)
            values = kv[0:keys_now, feat + h * head_dim : feat + (h + 1) * head_dim]
            numer = jnp.dot(weight.astype(BF16), values, preferred_element_type=F32)
            nsend[v, :, :, at] = numer.astype(BF16).reshape(nx, rows, head_dim)
            high = denom.astype(BF16).astype(F32)
            sums = jnp.where(lane_all == 2 * h, high, sums)
            sums = jnp.where(lane_all == 2 * h + 1, denom - high, sums)
        nsend[v, :, :, feat:] = sums.astype(BF16).reshape(nx, rows, head_dim)
        for c in num_copies[v]:
            c.start()

    @pl.when(sec == 0)
    def _():
        pl.semaphore_signal(go.at[2], inc=1, device_id=other, device_id_type=MESH)

    for v in range(waves):
        total = nsend[v, x].astype(F32)
        for d in range(1, nx):
            arrived(nrecv.at[v, x_at(d)], n_r.at[v, x_at(d)])
            total += nrecv[v, x_at(d)].astype(F32)
        parts = []
        for h in range(heads):
            at = feat + 2 * h
            denom = total[:, at : at + 1] + total[:, at + 1 : at + 2]
            parts.append(total[:, h * head_dim : (h + 1) * head_dim] / denom)
        ag[v, z] = jnp.concatenate(parts, axis=1).astype(BF16)
        for c in a_copies[v]:
            c.start()

    def source(c):
        pos = c * chunk
        first_row = -waves * fresh - pad
        for s in range(steps):
            row = (s // per_wave) * fresh + (s % per_wave) * tok
            row += (pos - begins[s]) // chunk * rows
            first_row = jnp.where(covers(s, pos), row, first_row)
        return first_row

    in_row = lax.broadcasted_iota(jnp.int32, (pad, waves * fresh), 0)
    in_col = lax.broadcasted_iota(jnp.int32, (pad, waves * fresh), 1)
    picks = []
    for c in range(nx):
        hit = (in_col - in_row == source(y * nx + c)) & (in_row < tok)
        picks.append(jnp.where(hit, 1.0, 0.0).astype(BF16))
    pick = jnp.concatenate(picks, axis=0)
    value = jnp.dot(pick, kv[stale:, :], preferred_element_type=F32)
    rsend[...] = value.astype(BF16).reshape(nx, pad, 2 * feat)
    for c in r_copies:
        c.start()

    def refresh():
        for d in range(1, nx):
            arrived(rrecv.at[x_at(d)], r_r.at[x_at(d)])
        rrecv[x] = rsend[x]
        out_row = lax.broadcasted_iota(jnp.int32, (chunk, nx * pad), 0)
        out_col = lax.broadcasted_iota(jnp.int32, (chunk, nx * pad), 1)
        block = out_col // pad
        within = out_col - block * pad
        hit = (out_row == block * tok + within) & (within < tok)
        place = jnp.where(hit, 1.0, 0.0).astype(BF16)
        written_to = source(seq) >= 0
        value = jnp.dot(place, rrecv[...].reshape(nx * pad, 2 * feat), preferred_element_type=F32)
        value = jnp.where(written_to, value, kv[cached(y), :].astype(F32)).astype(BF16)
        nk[...] = value[:, 0:feat]
        nv[...] = value[:, feat:]

    pl.when(sec == 1)(refresh)
    own_wo.wait()
    gate = mod[2, :, pl.ds(pl.multiple_of(z * feat, feat), feat)]
    results = []
    for v in range(waves):
        result = jnp.zeros((rows, feat), F32)
        for d in [0] + z_order[::-1]:
            if d:
                arrived(ag.at[v, z_at(d)], ag_r.at[v, z_at(d)])
            at = pl.ds(pl.multiple_of(z_at(d) * feat, feat), feat)
            result += jnp.dot(ag[v, z_at(d)], wo_v[at, :], preferred_element_type=F32)
        result = (own[v].astype(F32) + gate * result).astype(BF16)
        done[v] = result
        results.append(result.astype(F32))

        @pl.when(sec == 0)
        def _():
            for c in next_x[v]:
                c.start()

    result = jnp.concatenate(results, axis=0)
    parts = [result[s * tok : (s + 1) * tok] for s in range(steps)]
    value = []
    for p in range(steps):
        chosen = parts[0]
        for s in range(1, steps):
            chosen = jnp.where(places[s] == p, parts[s], chosen)
        value.append(chosen)
    bo[...] = jnp.concatenate(value, axis=0).astype(BF16)

    pl.when(sec == 0)(refresh)

    @pl.when(sec == 0)
    def _():
        for c in first_st + sn_copies + w_copies + sum(next_x + p_copies, []):
            c.wait_send()
        for v in range(waves):
            for c in first_x[v][1:]:
                c.wait_send()

            @pl.when(hy != y)
            def _():
                first_x[v][0].wait_send()

    @pl.when(sec == 1)
    def _():
        for c in wa_copies + wb_copies + sum(wc_copies + wd_copies + wc_onward + wd_onward, []):
            c.wait_send()

    for c in cache_copies + r_copies + sum(q_copies + kv_copies + num_copies + a_copies, []):
        c.wait_send()


def write_kernel(*refs):
    half = len(refs) // 2
    for src, dst in zip(refs[:half], refs[half:]):
        dst[...] = src[...]


def written(*arrays):
    vmem = pl.BlockSpec(memory_space=pltpu.VMEM)
    return pl.pallas_call(
        write_kernel,
        name="write",
        out_shape=tuple(jax.ShapeDtypeStruct(a.shape, a.dtype) for a in arrays),
        in_specs=[vmem] * len(arrays),
        out_specs=(vmem,) * len(arrays),
        compiler_params=pltpu.CompilerParams(vmem_limit_bytes=60 << 20),
    )(*arrays)


def per_device(
    patches, cache_k, cache_v, w_qkv, w_out, modulation, qk_gain, patch_order, patch_start
):
    nz = lax.axis_size("head")
    ny = nx = square_side(lax.axis_size("seq"))
    count, tok, feat = patches.shape
    chunk = cache_k.shape[1]
    head_dim = qk_gain.shape[-1]
    waves = 2
    per_wave = count // waves
    rows = per_wave * tok
    hz = nz // ny
    w_rows = w_qkv.shape[1]
    pad = -(-tok // 16) * 16
    keys = ny * (waves * rows + chunk)
    dma = pltpu.SemaphoreType.DMA
    vmem = pl.BlockSpec(memory_space=pltpu.VMEM)
    hbm = pl.BlockSpec(memory_space=pl.ANY)
    out, new_k, new_v = pl.pallas_call(
        functools.partial(block_kernel, nz, ny, nx, tok, waves, per_wave, head_dim),
        name="blocks",
        out_shape=(
            jax.ShapeDtypeStruct((count * tok, feat), BF16),
            jax.ShapeDtypeStruct((chunk, feat), BF16),
            jax.ShapeDtypeStruct((chunk, feat), BF16),
        ),
        in_specs=[hbm] * 9,
        out_specs=(vmem, vmem, vmem),
        scratch_shapes=[
            pltpu.SMEM((count,), jnp.int32),
            pltpu.SMEM((count,), jnp.int32),
            pltpu.VMEM((3, 1, nz * feat), F32),
            pltpu.VMEM((2, head_dim), F32),
            pltpu.VMEM((count * tok, feat), BF16),
            pltpu.VMEM((waves, rows, feat), BF16),
            pltpu.VMEM((waves, rows, feat), BF16),
            pltpu.VMEM((waves, ny, hz, rows, feat), BF16),
            pltpu.VMEM((waves, ny, rows, hz * feat), BF16),
            pltpu.VMEM((waves, nz, rows, feat), BF16),
            pltpu.VMEM((waves, rows, nz * feat), BF16),
            pltpu.VMEM((8, head_dim), F32),
            pltpu.VMEM((nz, 8, head_dim), F32),
            pltpu.VMEM((8, head_dim), F32),
            pltpu.VMEM((ny, 8, head_dim), F32),
            pltpu.VMEM((3, ny, nx, w_rows, feat), BF16),
            pltpu.VMEM((nz * feat, feat), BF16),
            pltpu.VMEM((waves, ny, rows, 3 * feat), BF16),
            pltpu.VMEM((waves, ny, rows, 3 * feat), BF16),
            pltpu.VMEM((waves, nx, rows, feat), BF16),
            pltpu.VMEM((keys, 2 * feat), BF16),
            pltpu.VMEM((keys, head_dim), BF16),
            pltpu.VMEM((waves, nx, rows, feat + head_dim), BF16),
            pltpu.VMEM((waves, nx, rows, feat + head_dim), BF16),
            pltpu.VMEM((waves, nz, rows, feat), BF16),
            pltpu.VMEM((nx, pad, 2 * feat), BF16),
            pltpu.VMEM((nx, pad, 2 * feat), BF16),
            dma((9,)),
            dma((waves, nz)),
            dma((waves, ny, hz)),
            dma((nz,)),
            dma((nz,)),
            dma((ny,)),
            dma((ny,)),
            dma((waves, nz)),
            dma((waves, nz)),
            dma((nx,)),
            dma((nx,)),
            dma((nx,)),
            dma((nx,)),
            dma((ny,)),
            dma((ny,)),
            dma((3, ny)),
            dma((3, ny)),
            dma((3, nx)),
            dma((3, nx)),
            dma((3, ny)),
            dma((3, ny)),
            dma((3, nx)),
            dma((3, nx)),
            dma((ny,)),
            dma((ny,)),
            dma((waves, ny)),
            dma((waves, ny)),
            dma((waves, nx)),
            dma((waves, nx)),
            dma((waves, ny)),
            dma((waves, ny)),
            dma((waves, nx)),
            dma((waves, nx)),
            dma((waves, nz)),
            dma((waves, nz)),
            dma((nx,)),
            dma((nx,)),
            pltpu.SemaphoreType.REGULAR((3,)),
        ],
        compiler_params=pltpu.CompilerParams(
            collective_id=0, has_side_effects=True, vmem_limit_bytes=60 << 20
        ),
    )(
        patch_order,
        patch_start,
        patches.reshape(count * tok, feat),
        cache_k[0],
        cache_v[0],
        jnp.transpose(w_qkv[0], (1, 0, 2)),
        w_out[0],
        jnp.transpose(modulation, (1, 0, 2)),
        qk_gain[0],
    )
    out, new_k, new_v = written(out, new_k, new_v)
    return (out.reshape(1, count, tok, feat), new_k[None], new_v[None])


def solution(mesh):
    return jax.shard_map(
        per_device,
        mesh=mesh,
        in_specs=(
            P(None, "seq", "head"),
            P("section", "seq", "head"),
            P("section", "seq", "head"),
            P("section", "seq", None, "head"),
            P("section", None, "head"),
            P("section", None, None),
            P("section", None, None),
            P(),
            P(),
        ),
        out_specs=(
            P("section", None, "seq", "head"),
            P("section", "seq", "head"),
            P("section", "seq", "head"),
        ),
        check_vma=False,
    )
```

```python
import functools
import math

import jax
import jax.numpy as jnp
from jax import lax
from jax.experimental import pallas as pl
from jax.experimental.pallas import tpu as pltpu
from jax.sharding import PartitionSpec as P

MESH = pl.DeviceIdType.MESH
F32 = jnp.float32
BF16 = jnp.bfloat16
FAR = -1e30


def square_side(count):
    side = math.isqrt(count)
    assert side * side == count
    return side


def block_kernel(
    nz,
    ny,
    nx,
    tok,
    waves,
    per_wave,
    head_dim,
    order_h,
    start_h,
    x_in,
    ck,
    cv,
    w,
    wo,
    mod_h,
    gain_h,
    bo_h,
    nk_h,
    nv_h,
    bo,
    nk,
    nv,
    order,
    start,
    mod,
    gain,
    x_rows,
    own,
    done,
    xr,
    xe,
    xg,
    xn,
    st_send,
    st_recv,
    st_norm,
    st_all,
    wbuf,
    wo_v,
    psend,
    precv,
    qg,
    kv,
    bias,
    nsend,
    nrecv,
    ag,
    rsend,
    rrecv,
    loc,
    x_s,
    x_r,
    st_s,
    st_r,
    sn_s,
    sn_r,
    h_s,
    h_r,
    w_s,
    w_r,
    wa_s,
    wa_r,
    wb_s,
    wb_r,
    wc_s,
    wc_r,
    wd_s,
    wd_r,
    we_s,
    we_r,
    wf_s,
    wf_r,
    c_s,
    c_r,
    p_s,
    p_r,
    q_s,
    q_r,
    kv_s,
    kv_r,
    n_s,
    n_r,
    ag_s,
    ag_r,
    r_s,
    r_r,
    go,
):
    sec = lax.axis_index("section")
    z = lax.axis_index("head")
    seq = lax.axis_index("seq")
    y = seq // nx
    x = lax.rem(seq, nx)
    _, rows, feat = own.shape
    chunk = ck.shape[0]
    heads = feat // head_dim
    width = nz * feat
    w_rows = w.shape[1]
    hz = nz // ny
    hy = z // hz
    steps = waves * per_wave
    stale = ny * chunk
    fresh = ny * rows
    span = ny * chunk
    pad = rrecv.shape[1]

    def z_at(d):
        return lax.rem(z + d, nz)

    def y_at(d):
        return lax.rem(y + d, ny)

    def x_at(d):
        return lax.rem(x + d, nx)

    def on_z(d):
        return (sec, z_at(d), seq)

    def on_y(d):
        return (sec, z, y_at(d) * nx + x)

    def on_x(d):
        return (sec, z, y * nx + x_at(d))

    other = (1 - sec, z, seq)
    z_order = sorted(range(1, nz), key=lambda d: -min(d, nz - d))
    y_order = sorted(range(1, ny), key=lambda d: -min(d, ny - d))
    x_order = sorted(range(1, nx), key=lambda d: -min(d, nx - d))

    def copy(src, dst, ss, rs, dev):
        return pltpu.make_async_remote_copy(
            src_ref=src, dst_ref=dst, send_sem=ss, recv_sem=rs, device_id=dev, device_id_type=MESH
        )

    def arrived(dst, rs):
        copy(dst, dst, rs, rs, other).wait_recv()

    def cached(i):
        return pl.ds(pl.multiple_of(i * chunk, chunk), chunk)

    def freshly(v, i):
        return pl.ds(pl.multiple_of(stale + v * fresh + i * rows, rows), rows)

    w_slot = wbuf.at[:, y, x]
    own_x = pltpu.make_async_copy(x_in, x_rows, loc.at[0])
    own_w = pltpu.make_async_copy(w, w_slot, loc.at[1])
    own_cache = [
        pltpu.make_async_copy(ck, kv.at[cached(y), 0:feat], loc.at[2]),
        pltpu.make_async_copy(cv, kv.at[cached(y), feat : 2 * feat], loc.at[3]),
    ]
    own_places = [
        pltpu.make_async_copy(order_h, order, loc.at[4]),
        pltpu.make_async_copy(start_h, start, loc.at[5]),
    ]
    own_scales = [
        pltpu.make_async_copy(mod_h, mod, loc.at[6]),
        pltpu.make_async_copy(gain_h, gain, loc.at[7]),
    ]
    own_wo = pltpu.make_async_copy(wo, wo_v, loc.at[8])
    out_cache = [
        pltpu.make_async_copy(nk, nk_h, loc.at[9]),
        pltpu.make_async_copy(nv, nv_h, loc.at[10]),
    ]
    out_block = pltpu.make_async_copy(bo, bo_h, loc.at[11])

    def by_wave(make):
        return [make(v) for v in range(waves)]

    first_x = by_wave(
        lambda v: [
            copy(
                own.at[v],
                xr.at[v, y, lax.rem(z, hz)],
                x_s.at[v, d],
                x_r.at[v, y, lax.rem(z, hz)],
                (0, z_at(d), hy * nx + x),
            )
            for d in [0] + z_order
        ]
    )
    first_st = [
        copy(st_send, st_recv.at[z], st_s.at[d], st_r.at[z], on_z(d)) for d in z_order
    ]
    next_x = by_wave(
        lambda v: [
            copy(done.at[v], xg.at[v, z], h_s.at[v, d], h_r.at[v, z], (1, z_at(d), seq))
            for d in [0] + z_order
        ]
    )
    sn_copies = [
        copy(st_norm, st_all.at[y], sn_s.at[d], sn_r.at[y], on_y(d)) for d in y_order
    ]
    w_copies = [copy(w_slot, w_slot, w_s.at[d], w_r.at[x], on_x(d)) for d in x_order]
    half = w_rows // 2
    upper, lower = pl.ds(0, half), pl.ds(half, half)

    def w_gather(view, ss, rs, at, to, count):
        return [copy(view, view, ss.at[d], rs.at[at], to(d)) for d in range(1, count)]

    wa_copies = w_gather(wbuf.at[:, y, x, upper], wa_s, wa_r, x, on_x, nx)
    wb_copies = w_gather(wbuf.at[:, y, x, lower], wb_s, wb_r, y, on_y, ny)
    def w_parts(view, ss, rs, fs, fr, at, to, count):
        near = sorted({1, count - 1})
        assert count in (2, 4)
        mine = [
            [copy(view(i, at(0)), view(i, at(0)), ss.at[i, d], rs.at[i, d], to(d)) for d in near]
            for i in range(3)
        ]

        def came(i):
            for d in near:
                arrived(view(i, at(count - d)), rs.at[i, d])

        onward = []
        for i in range(3):
            onward.append([])
            for d in near if count == 4 else ():
                part = view(i, at(count - d), d != 1)
                onward[i].append(copy(part, part, fs.at[i, d], fr.at[i, d], to(d)))

        def came_onward(i):
            for d in near if count == 4 else ():
                arrived(view(i, at(2), d != 1), fr.at[i, d])

        return mine, came, onward, came_onward

    def pick_shards(count, part):
        middle = count // 2
        return slice(None) if part is None else pl.ds(middle * part, middle)

    def upper_view(i, j, part=None):
        return wbuf.at[i, j, pick_shards(nx, part), upper]

    def lower_view(i, j, part=None):
        return wbuf.at[i, pick_shards(ny, part), j, lower]

    wc_copies, wc_came, wc_onward, wc_done = w_parts(
        upper_view, wc_s, wc_r, we_s, we_r, y_at, on_y, ny
    )
    wd_copies, wd_came, wd_onward, wd_done = w_parts(
        lower_view, wd_s, wd_r, wf_s, wf_r, x_at, on_x, nx
    )
    cache_slot = kv.at[cached(y), :]
    cache_copies = [copy(cache_slot, cache_slot, c_s.at[d], c_r.at[y], on_y(d)) for d in y_order]
    p_copies = by_wave(
        lambda v: [
            copy(psend.at[v, y_at(d)], precv.at[v, y], p_s.at[v, d], p_r.at[v, y], on_y(d))
            for d in y_order
        ]
    )
    q_copies = by_wave(
        lambda v: [
            copy(qg.at[v, x], qg.at[v, x], q_s.at[v, d], q_r.at[v, x], on_x(d))
            for d in x_order
        ]
    )
    kv_copies = by_wave(
        lambda v: [
            copy(
                kv.at[freshly(v, y), :],
                kv.at[freshly(v, y), :],
                kv_s.at[v, d],
                kv_r.at[v, y],
                on_y(d),
            )
            for d in y_order
        ]
    )
    num_copies = by_wave(
        lambda v: [
            copy(nsend.at[v, x_at(d)], nrecv.at[v, x], n_s.at[v, d], n_r.at[v, x], on_x(d))
            for d in x_order
        ]
    )
    a_copies = by_wave(
        lambda v: [
            copy(ag.at[v, z], ag.at[v, z], ag_s.at[v, d], ag_r.at[v, z], on_z(d))
            for d in z_order
        ]
    )
    r_copies = [
        copy(rsend.at[x_at(d)], rrecv.at[x], r_s.at[d], r_r.at[x], on_x(d)) for d in x_order
    ]

    @pl.when(sec == 0)
    def _():
        own_x.start()

    for c in own_places + [own_w] + own_cache + own_scales + [own_wo]:
        c.start()

    barrier = pltpu.get_barrier_semaphore()

    def greet(dev):
        pl.semaphore_signal(barrier, inc=1, device_id=dev, device_id_type=MESH)

    partners = (
        [on_z(d) for d in range(1, nz)]
        + [on_y(d) for d in range(1, ny)]
        + [on_x(d) for d in range(1, nx)]
    )
    for dev in partners:
        greet(dev)

    def is_own(i, b):
        return (y == i) & (z == y * hz + b)

    @pl.when(sec == 0)
    def _():
        for i in range(ny):
            for b in range(hz):

                @pl.when(jnp.logical_not(is_own(i, b)))
                def _():
                    greet((0, y * hz + b, i * nx + x))

    @pl.when(sec == 1)
    def _():
        for d in range(nz):
            greet((0, z_at(d), seq))

    for c in own_places:
        c.wait()
    places = [order[s] for s in range(steps)]
    begins = [sum(jnp.where(places[s] == p, start[p], 0) for p in range(steps)) for s in range(steps)]

    lane_rows = lax.broadcasted_iota(jnp.int32, (steps * tok, head_dim), 1)

    def shard_stats(value):
        middle = jnp.sum(value, axis=-1, keepdims=True) * (1.0 / feat)
        value = value - middle
        square = jnp.sum(value * value, axis=-1, keepdims=True)
        both = jnp.where(lane_rows == 0, middle, jnp.where(lane_rows == 1, square, 0.0))
        both = jnp.concatenate([both, jnp.zeros((head_dim - steps * tok, head_dim), F32)], axis=0)
        st_send[...] = jnp.transpose(both)[0:8, :]

    @pl.when(sec == 0)
    def _():
        own_x.wait()
        value = x_rows[...].astype(F32)
        parts = [value[p * tok : (p + 1) * tok] for p in range(steps)]
        value = []
        for s in range(steps):
            chosen = parts[0]
            for p in range(1, steps):
                chosen = jnp.where(places[s] == p, parts[p], chosen)
            value.append(chosen)
        value = jnp.concatenate(value, axis=0)
        own[...] = value.astype(BF16).reshape(waves, rows, feat)
        shard_stats(value)
        st_recv[z] = st_send[...]
        pl.semaphore_wait(barrier, len(partners) + 2 * nz - jnp.where(hy == y, 1, 0))
        own_w.wait()
        for c in w_copies + first_st:
            c.start()
        for v in range(waves):
            for c in first_x[v][1:]:
                c.start()

            @pl.when(hy == y)
            def _():
                xr[v, y, lax.rem(z, hz)] = own[v]

            @pl.when(hy != y)
            def _():
                first_x[v][0].start()

    @pl.when(sec == 1)
    def _():
        own_w.wait()

    for c in own_cache:
        c.wait()

    @pl.when(sec == 1)
    def _():
        pl.semaphore_wait(barrier, len(partners))
        for c in wb_copies:
            c.start()
        pl.semaphore_wait(go.at[0], 1)
        for c in wa_copies:
            c.start()
        for d in range(1, ny):
            arrived(wbuf.at[:, y_at(d), x, lower], wb_r.at[y_at(d)])
        for c in wd_copies[1]:
            c.start()
        for d in range(1, nx):
            arrived(wbuf.at[:, y, x_at(d), upper], wa_r.at[x_at(d)])
        wd_came(1)
        for c in wd_onward[1]:
            c.start()
        pl.semaphore_wait(go.at[1], 1)
        for c in wc_copies[1]:
            c.start()
        pl.semaphore_wait(go.at[2], 1)
        for c in wd_copies[2] + wc_copies[2] + wd_copies[0] + wc_copies[0]:
            c.start()
        wc_came(1)
        for c in wc_onward[1]:
            c.start()
        wd_came(2)
        for c in wd_onward[2]:
            c.start()
        wc_came(2)
        for c in wc_onward[2]:
            c.start()
        wd_came(0)
        for c in wd_onward[0]:
            c.start()
        wc_came(0)
        for c in wc_onward[0]:
            c.start()
        for c in cache_copies:
            c.start()

    def covers(s, pos):
        return (begins[s] <= pos) & (pos < begins[s] + span)

    def first_from(step, pos):
        found = steps
        for s in reversed(range(step, steps)):
            found = jnp.where(covers(s, pos), s, found)
        return found

    lane = lax.broadcasted_iota(jnp.int32, (tok, head_dim), 1)
    lane_chunk = lax.broadcasted_iota(jnp.int32, (chunk, head_dim), 1)
    for j in range(ny):
        upto = first_from(0, (j * nx + x) * chunk)
        value = jnp.where(lane_chunk < upto, 0.0, FAR)
        bias[j * chunk : (j + 1) * chunk, :] = value.astype(BF16)
        for v in range(waves):
            parts = []
            for s in range(v * per_wave, (v + 1) * per_wave):
                upto = first_from(s + 1, begins[s] + j * chunk)
                parts.append(jnp.where((lane >= s) & (lane < upto), 0.0, FAR))
            at = stale + v * fresh + j * rows
            bias[at : at + rows, :] = jnp.concatenate(parts, axis=0).astype(BF16)

    for c in own_scales:
        c.wait()

    def rms_heads(value, which):
        out = []
        for h in range(heads):
            part = value[:, h * head_dim : (h + 1) * head_dim]
            power = jnp.sum(part * part, axis=-1, keepdims=True) * (1.0 / head_dim)
            out.append(part * lax.rsqrt(power + 1e-06) * gain[which : which + 1, :])
        return jnp.concatenate(out, axis=-1).astype(BF16)

    def spread_keys(v, key, value):
        kv[freshly(v, y), 0:feat] = rms_heads(key, 1)
        kv[freshly(v, y), feat : 2 * feat] = value.astype(BF16)
        for c in kv_copies[v]:
            c.start()

    def spread_queries(v, query):
        qg[v, x] = rms_heads(query, 0)
        for c in q_copies[v]:
            c.start()

    @pl.when(sec == 0)
    def _():
        for d in range(1, nz):
            arrived(st_recv.at[z_at(d)], st_r.at[z_at(d)])
        middles = [st_recv[i, 0:1, :] for i in range(nz)]
        mean = sum(middles) * (1.0 / nz)
        square = sum(st_recv[i, 1:2, :] for i in range(nz))
        square += sum((m - mean) * (m - mean) for m in middles) * feat
        scale = lax.rsqrt(square * (1.0 / width) + 1e-06)
        line = lax.broadcasted_iota(jnp.int32, (8, head_dim), 0)
        value = jnp.where(line == 0, mean, jnp.where(line == 1, scale, 0.0))
        st_norm[...] = value
        st_all[y] = value
        for c in sn_copies:
            c.start()
        for d in range(1, ny):
            arrived(st_all.at[y_at(d)], sn_r.at[y_at(d)])
        for c in cache_copies:
            c.start()
        value = st_all[...].reshape(8 * ny, head_dim)
        value = jnp.concatenate([value, jnp.zeros((head_dim - 8 * ny, head_dim), F32)], axis=0)
        stats = jnp.transpose(value)
        for v in range(waves):
            for i in range(ny):
                mean = stats[v * rows : (v + 1) * rows, 8 * i : 8 * i + 1]
                scale = stats[v * rows : (v + 1) * rows, 8 * i + 1 : 8 * i + 2]
                for b in range(hz):

                    @pl.when(jnp.logical_not(is_own(i, b)))
                    def _():
                        arrived(xr.at[v, i, b], x_r.at[v, i, b])

                    at = pl.ds(pl.multiple_of((y * hz + b) * feat, feat), feat)
                    value = (xr[v, i, b].astype(F32) - mean) * scale
                    value = value * (1.0 + mod[1, :, at]) + mod[0, :, at]
                    xe[v, i, :, b * feat : (b + 1) * feat] = value.astype(BF16)
        for d in range(1, nx):
            arrived(wbuf.at[:, y, x_at(d)], w_r.at[x_at(d)])
        pl.semaphore_signal(go.at[0], inc=1, device_id=other, device_id_type=MESH)
        for v in range(waves):
            tokens = xe[v].reshape(ny * rows, hz * feat)
            for i in range(3):
                weights = wbuf[i, y].reshape(nx * w_rows, feat)
                value = jnp.dot(tokens, weights, preferred_element_type=F32)
                psend[v, :, :, i * feat : (i + 1) * feat] = value.astype(BF16).reshape(
                    ny, rows, feat
                )
            for c in p_copies[v]:
                c.start()
        for v in range(waves):
            value = psend[v, y].astype(F32)
            for d in range(1, ny):
                arrived(precv.at[v, y_at(d)], p_r.at[v, y_at(d)])
                value += precv[v, y_at(d)].astype(F32)
            spread_keys(v, value[:, feat : 2 * feat], value[:, 2 * feat :])
            spread_queries(v, value[:, 0:feat])

    @pl.when(sec == 1)
    def _():
        for v in range(waves):
            for i in range(nz):
                arrived(xg.at[v, i], h_r.at[v, i])
            own[v] = xg[v, z]
            total = jnp.zeros((rows, feat), F32)
            for i in range(nz):
                total += xg[v, i].astype(F32)
            mean = jnp.sum(total, axis=-1, keepdims=True) * (1.0 / width)
            total = jnp.zeros((rows, feat), F32)
            for i in range(nz):
                diff = xg[v, i].astype(F32) - mean
                total += diff * diff
            scale = lax.rsqrt(jnp.sum(total, axis=-1, keepdims=True) * (1.0 / width) + 1e-06)
            for i in range(nz):
                at = slice(i * feat, (i + 1) * feat)
                value = (xg[v, i].astype(F32) - mean) * scale
                value = value * (1.0 + mod[1, :, at]) + mod[0, :, at]
                xn[v, :, at] = value.astype(BF16)
            parts = [None] * 3
            for i in (1, 2, 0):
                if v == 0:
                    wc_done(i)
                    wd_done(i)
                weights = wbuf[i].reshape(width, feat)
                parts[i] = jnp.dot(xn[v], weights, preferred_element_type=F32)
                if i == 2:
                    spread_keys(v, parts[1], parts[2])
            spread_queries(v, parts[0])

    for d in range(1, ny):
        arrived(kv.at[cached(y_at(d)), :], c_r.at[y_at(d)])
    lane_all = lax.broadcasted_iota(jnp.int32, (nx * rows, head_dim), 1)
    lane_tok = lax.broadcasted_iota(jnp.int32, (tok, head_dim), 1)
    exponent = math.log2(math.e) / math.sqrt(head_dim)
    for v in range(waves):
        for d in range(1, ny):
            arrived(kv.at[freshly(v, y_at(d)), :], kv_r.at[v, y_at(d)])
        for d in range(1, nx):
            arrived(qg.at[v, x_at(d)], q_r.at[v, x_at(d)])

        if v == waves - 1:

            @pl.when(sec == 0)
            def _():
                pl.semaphore_signal(go.at[1], inc=1, device_id=other, device_id_type=MESH)

        keys_now = stale + (v + 1) * fresh
        tags = [
            jnp.where(lane_tok == s, 1.0, 0.0) for s in range(v * per_wave, (v + 1) * per_wave)
        ]
        tags = jnp.concatenate(tags * nx, axis=0).astype(BF16)
        sums = jnp.zeros((nx * rows, head_dim), F32)
        for h in range(heads):
            at = slice(h * head_dim, (h + 1) * head_dim)
            queries = jnp.concatenate([qg[v, :, :, at].reshape(nx * rows, head_dim), tags], axis=1)
            keys = jnp.concatenate([kv[0:keys_now, at], bias[0:keys_now, :]], axis=1)
            scores = lax.dot_general(
                queries, keys, (((1,), (1,)), ((), ())), preferred_element_type=F32
            )
            weight = jnp.exp2(scores * exponent)
            denom = jnp.sum(weight, axis=-1, keepdims=True)
            values = kv[0:keys_now, feat + h * head_dim : feat + (h + 1) * head_dim]
            numer = jnp.dot(weight.astype(BF16), values, preferred_element_type=F32)
            nsend[v, :, :, at] = numer.astype(BF16).reshape(nx, rows, head_dim)
            high = denom.astype(BF16).astype(F32)
            sums = jnp.where(lane_all == 2 * h, high, sums)
            sums = jnp.where(lane_all == 2 * h + 1, denom - high, sums)
        nsend[v, :, :, feat:] = sums.astype(BF16).reshape(nx, rows, head_dim)
        for c in num_copies[v]:
            c.start()

    @pl.when(sec == 0)
    def _():
        pl.semaphore_signal(go.at[2], inc=1, device_id=other, device_id_type=MESH)

    for v in range(waves):
        total = nsend[v, x].astype(F32)
        for d in range(1, nx):
            arrived(nrecv.at[v, x_at(d)], n_r.at[v, x_at(d)])
            total += nrecv[v, x_at(d)].astype(F32)
        parts = []
        for h in range(heads):
            at = feat + 2 * h
            denom = total[:, at : at + 1] + total[:, at + 1 : at + 2]
            parts.append(total[:, h * head_dim : (h + 1) * head_dim] / denom)
        ag[v, z] = jnp.concatenate(parts, axis=1).astype(BF16)
        for c in a_copies[v]:
            c.start()

    def source(c):
        pos = c * chunk
        first_row = -waves * fresh - pad
        for s in range(steps):
            row = (s // per_wave) * fresh + (s % per_wave) * tok
            row += (pos - begins[s]) // chunk * rows
            first_row = jnp.where(covers(s, pos), row, first_row)
        return first_row

    in_row = lax.broadcasted_iota(jnp.int32, (pad, waves * fresh), 0)
    in_col = lax.broadcasted_iota(jnp.int32, (pad, waves * fresh), 1)
    picks = []
    for c in range(nx):
        hit = (in_col - in_row == source(y * nx + c)) & (in_row < tok)
        picks.append(jnp.where(hit, 1.0, 0.0).astype(BF16))
    pick = jnp.concatenate(picks, axis=0)
    value = jnp.dot(pick, kv[stale:, :], preferred_element_type=F32)
    rsend[...] = value.astype(BF16).reshape(nx, pad, 2 * feat)
    for c in r_copies:
        c.start()

    def refresh():
        for d in range(1, nx):
            arrived(rrecv.at[x_at(d)], r_r.at[x_at(d)])
        rrecv[x] = rsend[x]
        out_row = lax.broadcasted_iota(jnp.int32, (chunk, nx * pad), 0)
        out_col = lax.broadcasted_iota(jnp.int32, (chunk, nx * pad), 1)
        block = out_col // pad
        within = out_col - block * pad
        hit = (out_row == block * tok + within) & (within < tok)
        place = jnp.where(hit, 1.0, 0.0).astype(BF16)
        written_to = source(seq) >= 0
        value = jnp.dot(place, rrecv[...].reshape(nx * pad, 2 * feat), preferred_element_type=F32)
        value = jnp.where(written_to, value, kv[cached(y), :].astype(F32)).astype(BF16)
        nk[...] = value[:, 0:feat]
        nv[...] = value[:, feat:]
        for c in out_cache:
            c.start()

    pl.when(sec == 1)(refresh)
    own_wo.wait()
    gate = mod[2, :, pl.ds(pl.multiple_of(z * feat, feat), feat)]
    results = []
    for v in range(waves):
        result = jnp.zeros((rows, feat), F32)
        for d in [0] + z_order[::-1]:
            if d:
                arrived(ag.at[v, z_at(d)], ag_r.at[v, z_at(d)])
            at = pl.ds(pl.multiple_of(z_at(d) * feat, feat), feat)
            result += jnp.dot(ag[v, z_at(d)], wo_v[at, :], preferred_element_type=F32)
        result = (own[v].astype(F32) + gate * result).astype(BF16)
        done[v] = result
        results.append(result.astype(F32))

        @pl.when(sec == 0)
        def _():
            for c in next_x[v]:
                c.start()

    result = jnp.concatenate(results, axis=0)
    parts = [result[s * tok : (s + 1) * tok] for s in range(steps)]
    value = []
    for p in range(steps):
        chosen = parts[0]
        for s in range(1, steps):
            chosen = jnp.where(places[s] == p, parts[s], chosen)
        value.append(chosen)
    bo[...] = jnp.concatenate(value, axis=0).astype(BF16)
    out_block.start()

    pl.when(sec == 0)(refresh)

    @pl.when(sec == 0)
    def _():
        for c in first_st + sn_copies + w_copies + sum(next_x + p_copies, []):
            c.wait_send()
        for v in range(waves):
            for c in first_x[v][1:]:
                c.wait_send()

            @pl.when(hy != y)
            def _():
                first_x[v][0].wait_send()

    @pl.when(sec == 1)
    def _():
        for c in wa_copies + wb_copies + sum(wc_copies + wd_copies + wc_onward + wd_onward, []):
            c.wait_send()

    for c in cache_copies + r_copies + sum(q_copies + kv_copies + num_copies + a_copies, []):
        c.wait_send()
    for c in out_cache + [out_block]:
        c.wait()


def write_kernel(*refs):
    half = len(refs) // 2
    for src, dst in zip(refs[:half], refs[half:]):
        dst[...] = src[...]


def written(*arrays):
    vmem = pl.BlockSpec(memory_space=pltpu.VMEM)
    return pl.pallas_call(
        write_kernel,
        name="write",
        out_shape=tuple(jax.ShapeDtypeStruct(a.shape, a.dtype) for a in arrays),
        in_specs=[vmem] * len(arrays),
        out_specs=(vmem,) * len(arrays),
        compiler_params=pltpu.CompilerParams(vmem_limit_bytes=60 << 20),
    )(*arrays)


def per_device(
    patches, cache_k, cache_v, w_qkv, w_out, modulation, qk_gain, patch_order, patch_start
):
    nz = lax.axis_size("head")
    ny = nx = square_side(lax.axis_size("seq"))
    count, tok, feat = patches.shape
    chunk = cache_k.shape[1]
    head_dim = qk_gain.shape[-1]
    waves = 2
    per_wave = count // waves
    rows = per_wave * tok
    hz = nz // ny
    w_rows = w_qkv.shape[1]
    pad = -(-tok // 16) * 16
    keys = ny * (waves * rows + chunk)
    dma = pltpu.SemaphoreType.DMA
    hbm = pl.BlockSpec(memory_space=pl.ANY)
    out, new_k, new_v = pl.pallas_call(
        functools.partial(block_kernel, nz, ny, nx, tok, waves, per_wave, head_dim),
        name="blocks",
        out_shape=(
            jax.ShapeDtypeStruct((count * tok, feat), BF16),
            jax.ShapeDtypeStruct((chunk, feat), BF16),
            jax.ShapeDtypeStruct((chunk, feat), BF16),
        ),
        in_specs=[hbm] * 9,
        out_specs=(hbm, hbm, hbm),
        scratch_shapes=[
            pltpu.VMEM((count * tok, feat), BF16),
            pltpu.VMEM((chunk, feat), BF16),
            pltpu.VMEM((chunk, feat), BF16),
            pltpu.SMEM((count,), jnp.int32),
            pltpu.SMEM((count,), jnp.int32),
            pltpu.VMEM((3, 1, nz * feat), F32),
            pltpu.VMEM((2, head_dim), F32),
            pltpu.VMEM((count * tok, feat), BF16),
            pltpu.VMEM((waves, rows, feat), BF16),
            pltpu.VMEM((waves, rows, feat), BF16),
            pltpu.VMEM((waves, ny, hz, rows, feat), BF16),
            pltpu.VMEM((waves, ny, rows, hz * feat), BF16),
            pltpu.VMEM((waves, nz, rows, feat), BF16),
            pltpu.VMEM((waves, rows, nz * feat), BF16),
            pltpu.VMEM((8, head_dim), F32),
            pltpu.VMEM((nz, 8, head_dim), F32),
            pltpu.VMEM((8, head_dim), F32),
            pltpu.VMEM((ny, 8, head_dim), F32),
            pltpu.VMEM((3, ny, nx, w_rows, feat), BF16),
            pltpu.VMEM((nz * feat, feat), BF16),
            pltpu.VMEM((waves, ny, rows, 3 * feat), BF16),
            pltpu.VMEM((waves, ny, rows, 3 * feat), BF16),
            pltpu.VMEM((waves, nx, rows, feat), BF16),
            pltpu.VMEM((keys, 2 * feat), BF16),
            pltpu.VMEM((keys, head_dim), BF16),
            pltpu.VMEM((waves, nx, rows, feat + head_dim), BF16),
            pltpu.VMEM((waves, nx, rows, feat + head_dim), BF16),
            pltpu.VMEM((waves, nz, rows, feat), BF16),
            pltpu.VMEM((nx, pad, 2 * feat), BF16),
            pltpu.VMEM((nx, pad, 2 * feat), BF16),
            dma((12,)),
            dma((waves, nz)),
            dma((waves, ny, hz)),
            dma((nz,)),
            dma((nz,)),
            dma((ny,)),
            dma((ny,)),
            dma((waves, nz)),
            dma((waves, nz)),
            dma((nx,)),
            dma((nx,)),
            dma((nx,)),
            dma((nx,)),
            dma((ny,)),
            dma((ny,)),
            dma((3, ny)),
            dma((3, ny)),
            dma((3, nx)),
            dma((3, nx)),
            dma((3, ny)),
            dma((3, ny)),
            dma((3, nx)),
            dma((3, nx)),
            dma((ny,)),
            dma((ny,)),
            dma((waves, ny)),
            dma((waves, ny)),
            dma((waves, nx)),
            dma((waves, nx)),
            dma((waves, ny)),
            dma((waves, ny)),
            dma((waves, nx)),
            dma((waves, nx)),
            dma((waves, nz)),
            dma((waves, nz)),
            dma((nx,)),
            dma((nx,)),
            pltpu.SemaphoreType.REGULAR((3,)),
        ],
        compiler_params=pltpu.CompilerParams(
            collective_id=0, has_side_effects=True, vmem_limit_bytes=60 << 20
        ),
    )(
        patch_order,
        patch_start,
        patches.reshape(count * tok, feat),
        cache_k[0],
        cache_v[0],
        jnp.transpose(w_qkv[0], (1, 0, 2)),
        w_out[0],
        jnp.transpose(modulation, (1, 0, 2)),
        qk_gain[0],
    )
    out, new_k, new_v = written(out, new_k, new_v)
    return (out.reshape(1, count, tok, feat), new_k[None], new_v[None])


def solution(mesh):
    return jax.shard_map(
        per_device,
        mesh=mesh,
        in_specs=(
            P(None, "seq", "head"),
            P("section", "seq", "head"),
            P("section", "seq", "head"),
            P("section", "seq", None, "head"),
            P("section", None, "head"),
            P("section", None, None),
            P("section", None, None),
            P(),
            P(),
        ),
        out_specs=(
            P("section", None, "seq", "head"),
            P("section", "seq", "head"),
            P("section", "seq", "head"),
        ),
        check_vma=False,
    )
```
